256 devices in a mesh: pair: 2 (over y_lo), seq: 16 (over y_hi, z), dp: 8 (over x, core).
Axes of the slice: x: 4, y: 4 (y_hi: 2, y_lo: 2; y = y_hi * 2 + y_lo), z: 8, core: 2. Of those that a mesh axis runs over, the one named last changes fastest.
Arguments:
- latents: bfloat16 [8, 2, 1536, 64], P('dp', 'pair', 'seq'), may hold values from -6 to 6
- noise: bfloat16 [8, 1536, 64], P('dp', 'seq'), may hold values from -6 to 6
- pair_timestep_index: int32 [8], P('dp'), may hold values from 0 to 999
- preferred_image_slot: int32 [8], P('dp'), may hold values from 0 to 1
- prompt_token_states: bfloat16 [8, 512, 3072], P('dp', 'seq'), may hold values from -6 to 6
- image_embed_weight: bfloat16 [64, 3072], replicated, may hold values from -0.75 to 0.75
- timestep_modulation_weight: bfloat16 [256, 18432], P(None, 'seq'), may hold values from -0.375 to 0.375
- image_query_key_value: bfloat16 [3072, 16, 384], P(None, 'seq'), may hold values from -0.109375 to 0.109375
- text_key_value: bfloat16 [3072, 16, 256], P(None, 'seq'), may hold values from -0.109375 to 0.109375
- query_norm_gain: float32 [128], replicated, may hold values from 0.1 to 1.9
- key_norm_gain: float32 [128], replicated, may hold values from 0.1 to 1.9
- adapter_down_weight: bfloat16 [3072, 64], replicated, may hold values from -0.109375 to 0.109375
- adapter_up_weight: bfloat16 [64, 2048], replicated, may hold values from -0.75 to 0.75
- image_output_weight: bfloat16 [2048, 3072], P('seq'), may hold values from -1.25 to 1.25
- latent_out_weight: bfloat16 [3072, 64], replicated, may hold values from -0.109375 to 0.109375
Outputs:
- grad_down: float32 [3072, 64], replicated
- grad_up: float32 [64, 2048], replicated
- pair_loss: float32 [8], P('dp')
The draws below stay inside these ranges and needn't reach their ends.
All inputs are finite; a program needn't handle non-finite values.
Results may differ from the reference program's by a relative error of at most 0.025.
Values may be sent and summed in bfloat16 or wider, within the bound.
A program may use at most 128 MiB of HBM per device.

```python
import math
import jax
import jax.numpy as jnp
from jax import lax

MODEL_WIDTH_SIZE = 3072
ATTENTION_HEADS = 16
HEAD_SIZE = 128
CH = 64
FREQ = 256
ADAPTER_RANK = 64
PAIRS = 8
IMAGE_TOKENS = 1536
TXT = 512


def set_ends(array, key, low, largest):
    longest = array.shape.index(max(array.shape))
    spots = []
    for shift in (0, 1):
        where = [jax.random.randint(jax.random.fold_in(key, axis), (), 0, length) for axis, length in enumerate(array.shape)]
        where[longest] = (where[longest] + shift) % array.shape[longest]
        spots.append(tuple(where))
    return array.at[spots[0]].set(low).at[spots[1]].set(largest)


def levels(key, shape, cuts, least, top_value):
    level = 1.0
    for axis_at, parts in cuts:
        draws = jax.random.uniform(jax.random.fold_in(jax.random.fold_in(key, 6), axis_at), (parts,), jnp.float32, least / len(cuts), top_value / len(cuts))
        level = level * jnp.repeat(jnp.exp(draws), shape[axis_at] // parts).reshape((-1,) + (1,) * (len(shape) - 1 - axis_at))
    return level


def gaussian(stream_key, shape, scale, bound, split=(), kind=jnp.bfloat16):
    entries = scale * jax.random.normal(stream_key, shape, jnp.float32)
    if split:
        entries = entries * levels(stream_key, shape, split, -0.22, 0.18)
    return jnp.clip(entries, -bound, bound).astype(kind)


def setup_inputs(seed: int = 0) -> dict:
    arg_keys = jax.random.split(jax.random.key(seed), 16)
    return {
        "latents": gaussian(arg_keys[0], (PAIRS, 2, IMAGE_TOKENS, CH), 1.0, 6.0, ((0, 8), (1, 2), (2, 16))),
        "noise": gaussian(arg_keys[1], (PAIRS, IMAGE_TOKENS, CH), 1.0, 6.0, ((0, 8), (1, 16))),
        "pair_timestep_index": set_ends(jax.random.randint(arg_keys[2], (PAIRS,), 0, 1000), jax.random.fold_in(arg_keys[2], 1), 0, 999).astype(jnp.int32),
        "preferred_image_slot": set_ends(jax.random.randint(arg_keys[3], (PAIRS,), 0, 2), jax.random.fold_in(arg_keys[3], 1), 0, 1).astype(jnp.int32),
        "prompt_token_states": gaussian(arg_keys[4], (PAIRS, TXT, MODEL_WIDTH_SIZE), 1.0, 6.0, ((0, 8), (1, 16))),
        "image_embed_weight": gaussian(arg_keys[5], (CH, MODEL_WIDTH_SIZE), CH ** -0.5, 0.75),
        "timestep_modulation_weight": gaussian(arg_keys[6], (FREQ, 6 * MODEL_WIDTH_SIZE), FREQ ** -0.5, 0.375, ((1, 16),)),
        "image_query_key_value": gaussian(arg_keys[7], (MODEL_WIDTH_SIZE, ATTENTION_HEADS, 3 * HEAD_SIZE), MODEL_WIDTH_SIZE ** -0.5, 0.109375, ((1, 16),)),
        "text_key_value": gaussian(arg_keys[8], (MODEL_WIDTH_SIZE, ATTENTION_HEADS, 2 * HEAD_SIZE), MODEL_WIDTH_SIZE ** -0.5, 0.109375, ((1, 16),)),
        "query_norm_gain": jnp.clip(1.0 + 0.18 * jax.random.normal(arg_keys[9], (HEAD_SIZE,), jnp.float32), 0.1, 1.9),
        "key_norm_gain": jnp.clip(1.0 + 0.18 * jax.random.normal(arg_keys[10], (HEAD_SIZE,), jnp.float32), 0.1, 1.9),
        "adapter_down_weight": gaussian(arg_keys[11], (MODEL_WIDTH_SIZE, ADAPTER_RANK), MODEL_WIDTH_SIZE ** -0.5, 0.109375),
        "adapter_up_weight": gaussian(arg_keys[12], (ADAPTER_RANK, ATTENTION_HEADS * HEAD_SIZE), ADAPTER_RANK ** -0.5, 0.75),
        "image_output_weight": gaussian(arg_keys[13], (ATTENTION_HEADS * HEAD_SIZE, MODEL_WIDTH_SIZE), (4.0 * (ATTENTION_HEADS * HEAD_SIZE) ** -0.5), 1.25, ((0, 16),)),
        "latent_out_weight": gaussian(arg_keys[14], (MODEL_WIDTH_SIZE, CH), MODEL_WIDTH_SIZE ** -0.5, 0.109375),
    }


epsilon = 1e-06
half_beta = 20.0
horizon = 1000.0

def sinusoid(step_value, width):
    half_width = width // 2
    freqs = jnp.exp(-math.log(10000.0) * jnp.arange(half_width, dtype=jnp.float32) / half_width)
    angle = step_value * freqs
    return jnp.concatenate([jnp.cos(angle), jnp.sin(angle)])

def normalize(states):
    average = lax.optimization_barrier(jnp.mean(states, -1, keepdims=True))
    centred = states - average
    inv_spread = lax.rsqrt(lax.optimization_barrier(jnp.mean(centred * centred, -1, keepdims=True)) + epsilon)
    return (centred * inv_spread, inv_spread)

def modulated(states, scale_vec, shift_vec):
    return normalize(states)[0] * (1.0 + scale_vec) + shift_vec

def rms_gain(rows, gain):
    return rows * lax.rsqrt(lax.optimization_barrier(jnp.mean(rows * rows, -1, keepdims=True)) + epsilon) * gain

def rms_back(rows, gain, grads):
    inv_root = lax.rsqrt(lax.optimization_barrier(jnp.mean(rows * rows, -1, keepdims=True)) + epsilon)
    weighted = grads * gain
    return inv_root * weighted - rows * inv_root * inv_root * inv_root * lax.optimization_barrier(jnp.mean(rows * weighted, -1, keepdims=True))

def norm_back(unit_rows, inv_spread, grads):
    return (grads - lax.optimization_barrier(jnp.mean(grads, -1, keepdims=True)) - unit_rows * lax.optimization_barrier(jnp.mean(grads * unit_rows, -1, keepdims=True))) * inv_spread

def head_attend(operands):
    query, key_rows, value_rows = operands
    scores = jnp.dot(query, key_rows.T, preferred_element_type=jnp.float32) * (1.0 / math.sqrt(HEAD_SIZE))
    probs = jax.nn.softmax(scores, axis=-1)
    return jnp.dot(probs.astype(jnp.bfloat16), value_rows, preferred_element_type=jnp.float32).astype(jnp.bfloat16)

def head_back(operands):
    query, key_rows, value_rows, grad_out = operands
    inv_root = 1.0 / math.sqrt(HEAD_SIZE)
    scores = jnp.dot(query, key_rows.T, preferred_element_type=jnp.float32) * inv_root
    probs = jax.nn.softmax(scores, axis=-1)
    g_probs = jnp.dot(grad_out, value_rows.T, preferred_element_type=jnp.float32)
    g_scores = (probs * (g_probs - lax.optimization_barrier(jnp.sum(probs * g_probs, -1, keepdims=True))) * inv_root).astype(jnp.bfloat16)
    return jnp.dot(g_scores, key_rows, preferred_element_type=jnp.float32)

def reference(latents, noise, pair_timestep_index, preferred_image_slot, prompt_token_states, image_embed_weight, timestep_modulation_weight, image_query_key_value, text_key_value, query_norm_gain, key_norm_gain, adapter_down_weight, adapter_up_weight, image_output_weight, latent_out_weight):

    def one_pair(totals, pair_index):
        step_value = pair_timestep_index[pair_index].astype(jnp.float32)
        noise_level = (step_value + 1.0) / horizon
        modulation = jnp.dot(sinusoid(step_value, FREQ).astype(jnp.bfloat16)[None], timestep_modulation_weight, preferred_element_type=jnp.float32)[0]
        pieces = [modulation[part_index * MODEL_WIDTH_SIZE:(part_index + 1) * MODEL_WIDTH_SIZE] for part_index in range(6)]
        shift_img, scale_img, shift_txt, scale_txt, shift_out, scale_out = pieces
        txt_normed = modulated(prompt_token_states[pair_index].astype(jnp.float32), scale_txt, shift_txt).astype(jnp.bfloat16)
        kv_text = jnp.dot(txt_normed, text_key_value.reshape(MODEL_WIDTH_SIZE, -1), preferred_element_type=jnp.float32).reshape(TXT, ATTENTION_HEADS, 2 * HEAD_SIZE)
        noise_now = noise[pair_index].astype(jnp.float32)
        saved = []
        for slot_index in range(2):
            latent = latents[pair_index, slot_index].astype(jnp.float32)
            noisy = ((1.0 - noise_level) * latent + noise_level * noise_now).astype(jnp.bfloat16)
            target = noise_now - latent
            states = jnp.dot(noisy, image_embed_weight, preferred_element_type=jnp.float32)
            image_rows_normed = modulated(states, scale_img, shift_img).astype(jnp.bfloat16)
            qkv = jnp.dot(image_rows_normed, image_query_key_value.reshape(MODEL_WIDTH_SIZE, -1), preferred_element_type=jnp.float32).reshape(IMAGE_TOKENS, ATTENTION_HEADS, 3 * HEAD_SIZE)
            key_rows = jnp.concatenate([rms_gain(kv_text[..., :HEAD_SIZE], key_norm_gain), rms_gain(qkv[..., HEAD_SIZE:2 * HEAD_SIZE], key_norm_gain)], 0).astype(jnp.bfloat16)
            value_rows = jnp.concatenate([kv_text[..., HEAD_SIZE:], qkv[..., 2 * HEAD_SIZE:]], 0).astype(jnp.bfloat16)
            rank_projected = jnp.dot(image_rows_normed, adapter_down_weight, preferred_element_type=jnp.float32).astype(jnp.bfloat16)
            query_adapter_change = jnp.dot(rank_projected, adapter_up_weight, preferred_element_type=jnp.float32).astype(jnp.bfloat16).reshape(IMAGE_TOKENS, ATTENTION_HEADS, HEAD_SIZE)
            q_lin = qkv[..., :HEAD_SIZE]
            pol_lin = q_lin + query_adapter_change.astype(jnp.float32)
            q_ref = rms_gain(q_lin, query_norm_gain).astype(jnp.bfloat16)
            q_pol = rms_gain(pol_lin, query_norm_gain).astype(jnp.bfloat16)
            head_keys = key_rows.transpose(1, 0, 2)
            head_values = value_rows.transpose(1, 0, 2)
            out_ref = lax.map(head_attend, (q_ref.transpose(1, 0, 2), head_keys, head_values)).transpose(1, 0, 2)
            out_pol = lax.map(head_attend, (q_pol.transpose(1, 0, 2), head_keys, head_values)).transpose(1, 0, 2)
            results = []
            for heads_out in (out_ref, out_pol):
                mixed = states + jnp.dot(heads_out.reshape(IMAGE_TOKENS, -1), image_output_weight, preferred_element_type=jnp.float32)
                unit_rows, inv_spread = normalize(mixed)
                normed_out = (unit_rows * (1.0 + scale_out) + shift_out).astype(jnp.bfloat16)
                pred = jnp.dot(normed_out, latent_out_weight, preferred_element_type=jnp.float32)
                diff = target - pred
                error = jnp.sum(diff * diff) / (IMAGE_TOKENS * CH)
                results.append((error, diff, unit_rows, inv_spread))
            saved.append((results, image_rows_normed, rank_projected, pol_lin, q_pol, head_keys, head_values))
        gaps = [saved[slot_index][0][1][0] - saved[slot_index][0][0][0] for slot_index in range(2)]
        winner = preferred_image_slot[pair_index]
        margin = jnp.where(winner == 0, gaps[0] - gaps[1], gaps[1] - gaps[0])
        pair_value = jax.nn.softplus(half_beta * margin)
        weight_now = jax.nn.sigmoid(half_beta * margin) * half_beta / PAIRS
        grad_down_sum, grad_up_sum = totals
        for slot_index in range(2):
            results, image_rows_normed, rank_projected, pol_lin, q_pol, head_keys, head_values = saved[slot_index]
            error, diff, unit_rows, inv_spread = results[1]
            signed = jnp.where(winner == slot_index, weight_now, -weight_now)
            factor = signed * (-2.0 / (IMAGE_TOKENS * CH))
            g_pred = (factor * diff).astype(jnp.bfloat16)
            g_ln = jnp.dot(g_pred, latent_out_weight.T, preferred_element_type=jnp.float32) * (1.0 + scale_out)
            g_mixed = norm_back(unit_rows, inv_spread, g_ln).astype(jnp.bfloat16)
            g_heads = jnp.dot(g_mixed, image_output_weight.T, preferred_element_type=jnp.float32).astype(jnp.bfloat16).reshape(IMAGE_TOKENS, ATTENTION_HEADS, HEAD_SIZE)
            g_query = lax.map(head_back, (q_pol.transpose(1, 0, 2), head_keys, head_values, g_heads.transpose(1, 0, 2))).transpose(1, 0, 2)
            grad_query_change = rms_back(pol_lin, query_norm_gain, g_query).astype(jnp.bfloat16).reshape(IMAGE_TOKENS, ATTENTION_HEADS * HEAD_SIZE)
            grad_up_sum = grad_up_sum + jnp.dot(rank_projected.T, grad_query_change, preferred_element_type=jnp.float32)
            grad_low_rank = jnp.dot(grad_query_change, adapter_up_weight.T, preferred_element_type=jnp.float32).astype(jnp.bfloat16)
            grad_down_sum = grad_down_sum + jnp.dot(image_rows_normed.T, grad_low_rank, preferred_element_type=jnp.float32)
        return ((grad_down_sum, grad_up_sum), pair_value)
    start = (jnp.zeros((MODEL_WIDTH_SIZE, ADAPTER_RANK), jnp.float32), jnp.zeros((ADAPTER_RANK, ATTENTION_HEADS * HEAD_SIZE), jnp.float32))
    totals, losses = lax.scan(one_pair, start, jnp.arange(PAIRS, dtype=jnp.int32))
    return (totals[0], totals[1], losses)
```

```python
import functools
import math

import jax
import jax.numpy as jnp
from jax import lax
from jax.experimental import pallas as pl
from jax.experimental.pallas import tpu as pltpu
from jax.sharding import PartitionSpec as P

epsilon = 1e-06
half_beta = 20.0
horizon = 1000.0
F32 = jnp.float32
BF16 = jnp.bfloat16
VMEM_BYTES = 58 * 1024 * 1024


def sinusoid(step_value, width):
    half_width = width // 2
    freqs = jnp.exp(-math.log(10000.0) * jnp.arange(half_width, dtype=jnp.float32) / half_width)
    angle = step_value * freqs
    return jnp.concatenate([jnp.cos(angle), jnp.sin(angle)])


def mm(a, b):
    return lax.dot_general(a, b, (((1,), (0,)), ((), ())), preferred_element_type=F32)


def mm_nt(a, b):
    return lax.dot_general(a, b, (((1,), (1,)), ((), ())), preferred_element_type=F32)


def mm_tn(a, b):
    return lax.dot_general(a, b, (((0,), (0,)), ((), ())), preferred_element_type=F32)


def halves(a):
    top = a.astype(BF16)
    return top, (a - top.astype(F32)).astype(BF16)


def stacked(a):
    top, rest = halves(a)
    return jnp.concatenate([top, rest], 0)


def row_mean(a):
    return jnp.mean(a, -1, keepdims=True)


def rms_rows(rows):
    return lax.rsqrt(row_mean(rows * rows) + epsilon)


def remote(src, dst, send, recv, device):
    return pltpu.make_async_remote_copy(
        src_ref=src,
        dst_ref=dst,
        send_sem=send,
        recv_sem=recv,
        device_id=device,
        device_id_type=pl.DeviceIdType.MESH,
    )


def each(count, body):
    @pl.loop(0, count)
    def _(i):
        body(i)


def others(me, count, body):
    @pl.loop(1, count)
    def _(step):
        body(lax.rem(me + step, count))


def greet(axes):
    barrier = pltpu.get_barrier_semaphore()
    total = 0
    for axis, me, count in axes:
        others(
            me,
            count,
            lambda peer: pl.semaphore_signal(
                barrier,
                inc=1,
                device_id={axis: peer},
                device_id_type=pl.DeviceIdType.MESH,
            ),
        )
        total += count - 1
    return barrier, total


def at_rows(start, size):
    return pl.ds(pl.multiple_of(start, 16), size)


def at_lanes(start, size):
    return pl.ds(pl.multiple_of(start, 128), size)


def with_shift(scaled, shift):
    width = shift.shape[1]
    top, rest = halves(shift)
    which = lax.broadcasted_iota(jnp.int32, (16, width), 0)
    extra = jnp.where(
        which == 0,
        top.astype(F32),
        jnp.where(which == 1, rest.astype(F32), 0.0),
    )
    return jnp.concatenate([scaled, extra], 0).astype(BF16)


def front_kernel(
    seqs, dps, level, emb, lat, noi, txt, embed, wmod, wimg, wtxt, qg, kg, adown, aup, wo, lw,
    x, nz, mod, moddp, qp, kk, vext, pol, lhs, outf, rl, nn, ne, shl,
    noisy, text, oacc, q2, outb, modrow,
    mod_s, mod_r, noi_s, noi_r, txt_s, txt_r, nz_s, nz_r, dp_s, dp_r, kv_s, kv_r, x_s, x_r,
):
    me = lax.axis_index("seq")
    slot = lax.axis_index("pair")
    mine = lax.axis_index("dp")
    rows = lat.shape[0]
    images = rows * seqs
    width = embed.shape[1]
    half = txt.shape[0] // 2
    texts = half * seqs
    block = 4 * rows
    blocks = images // block
    part = wmod.shape[1]
    barrier, total = greet([("seq", me, seqs), ("dp", mine, dps), ("pair", slot, 2)])

    mod_part = mm(emb[...], wmod[...])[0:1]
    modrow[...] = mod_part
    lev = level[0, 0]
    noisy_mine = (
        (1.0 - lev) * lat[...].astype(F32) + lev * noi[...].astype(F32)
    ).astype(BF16)
    noisy[at_rows(me * rows, rows), :] = jnp.concatenate([noisy_mine, noisy_mine], 1)
    t = txt[at_rows(slot * half, half), :].astype(F32)
    t = t - row_mean(t)
    text[at_rows(me * half, half), :] = (t * lax.rsqrt(row_mean(t * t) + epsilon)).astype(BF16)
    pl.semaphore_wait(barrier, total)

    def mod_copy(owner, peer):
        return remote(
            modrow,
            mod.at[:, at_lanes(owner * part, part)],
            mod_s.at[peer],
            mod_r.at[owner],
            {"seq": peer},
        )

    def noisy_copy(owner, peer):
        where = noisy.at[at_rows(owner * rows, rows)]
        return remote(where, where, noi_s.at[peer], noi_r.at[owner], {"seq": peer})

    def text_copy(owner, peer):
        where = text.at[at_rows(owner * half, half)]
        return remote(where, where, txt_s.at[peer], txt_r.at[owner], {"seq": peer})

    def nz_copy(owner, peer):
        where = nz.at[at_rows(owner * 128, 128)]
        return remote(where, where, nz_s.at[peer], nz_r.at[owner], {"seq": peer})

    def dp_copy(owner, peer):
        return remote(
            mod.at[:, pl.ds(0, 2 * width)],
            moddp.at[owner],
            dp_s.at[peer],
            dp_r.at[owner],
            {"dp": peer},
        )

    def send_small(peer):
        mod_copy(me, peer).start()
        noisy_copy(me, peer).start()

    others(me, seqs, send_small)
    others(me, seqs, lambda peer: text_copy(me, peer).start())
    mod[:, at_lanes(me * part, part)] = mod_part

    emb_c = embed[...].astype(F32)
    emb_c = emb_c - row_mean(emb_c)
    e_top, e_rest = halves(emb_c)
    gram = stacked(mm_nt(e_top, e_top) + mm_nt(e_top, e_rest) + mm_nt(e_rest, e_top))
    wo_c = wo[...].astype(F32)
    wo_c = wo_c - row_mean(wo_c)
    zt = mm_nt(wo_c.astype(BF16), e_top)

    others(me, seqs, lambda peer: mod_copy(peer, peer).wait_recv())
    shift_img, scale_img, shift_txt, scale_txt, shift_out, scale_out = [
        mod[:, i * width : (i + 1) * width] for i in range(6)
    ]
    moddp[mine] = mod[:, 0 : 2 * width]
    others(mine, dps, lambda peer: dp_copy(mine, peer).start())
    ch = embed.shape[0]
    n_mine = mm((wo_c * (1.0 + scale_out)).astype(BF16), lw[...])
    nz[at_rows(me * 128, 128), :] = jnp.concatenate([n_mine, zt], 1).astype(BF16)
    others(me, seqs, lambda peer: nz_copy(me, peer).start())

    img_lhs = with_shift(emb_c * (1.0 + scale_img), shift_img)
    img_m = mm(img_lhs, wimg[...])
    img_m2 = stacked(img_m[0:ch])
    img_shift = img_m[ch : ch + 1] + img_m[ch + 1 : ch + 2]
    low_m = mm(img_lhs, adown[...])
    low_m2 = stacked(low_m[0:ch])
    low_shift = low_m[ch : ch + 1] + low_m[ch + 1 : ch + 2]
    out_m = mm(with_shift(emb_c * (1.0 + scale_out), shift_out), lw[...])
    out_m2 = stacked(out_m[0:ch])
    shl[...] = jnp.broadcast_to(out_m[ch : ch + 1] + out_m[ch + 1 : ch + 2], shl.shape)
    up = aup[:, at_lanes(me * 128, 128)]
    gain_q = qg[...]
    gain_k = kg[...]
    score_scale = math.log2(math.e) / math.sqrt(128.0)

    own = noisy[at_rows(me * rows, rows), :]
    ne[...] = mm(own, out_m2)
    own_nn = jnp.sum(mm(own, gram) * own[:, 0:ch].astype(F32), -1, keepdims=True)
    nn[...] = jnp.broadcast_to(own_nn, nn.shape)
    vext[:, 128:256] = jnp.ones((vext.shape[0], 128), BF16)

    others(me, seqs, lambda peer: noisy_copy(peer, peer).wait_recv())

    def project(i):
        here = at_rows(i * block, block)
        nb = noisy[here, :]
        nf = nb[:, 0:ch].astype(F32)
        var = jnp.sum(mm(nb, gram) * nf, -1, keepdims=True) * (1.0 / width)
        inv = lax.rsqrt(var + epsilon)
        qkv = mm(nb, img_m2) * inv + img_shift
        low = (mm(nb, low_m2) * inv + low_shift).astype(BF16)
        delta = mm(low, up).astype(BF16).astype(F32)
        q = qkv[:, 0:128]
        k = qkv[:, 128:256]
        q_pol = q + delta
        q2[here, :] = (q * rms_rows(q) * (gain_q * score_scale)).astype(BF16)
        qpol = (q_pol * rms_rows(q_pol) * (gain_q * score_scale)).astype(BF16)
        q2[at_rows(images + i * block, block), :] = qpol
        qp[here, :] = qpol
        pol[here, :] = q_pol
        kk[here, :] = (k * rms_rows(k) * gain_k).astype(BF16)
        vext[here, 0:128] = qkv[:, 256:384].astype(BF16)
        lhs[here, :] = jnp.concatenate([low, (nf * inv).astype(BF16)], 1)

    each(blocks, project)

    def attend(here, keys):
        s = mm_nt(q2[here, :], kk[keys, :])
        return mm(jnp.exp2(s).astype(BF16), vext[keys, :])

    def image_keys(i):
        here = at_rows(i * block, block)
        oacc[here, :] = attend(here, pl.ds(0, images))

    each(2 * blocks, image_keys)

    others(me, seqs, lambda peer: text_copy(peer, peer).wait_recv())
    text_n = (text[...].astype(F32) * (1.0 + scale_txt) + shift_txt).astype(BF16)
    kv = mm(text_n, wtxt[...])
    k = kv[:, 0:128]
    my_keys = at_rows(images + slot * texts, texts)
    kk[my_keys, :] = (k * rms_rows(k) * gain_k).astype(BF16)
    vext[my_keys, 0:128] = kv[:, 128:256].astype(BF16)
    other = 1 - slot

    def kv_copies(owner):
        keys = at_rows(images + owner * texts, texts)
        v = vext.at[keys, pl.ds(0, 128)]
        return (
            remote(kk.at[keys], kk.at[keys], kv_s.at[0], kv_r.at[0], {"pair": other}),
            remote(v, v, kv_s.at[1], kv_r.at[1], {"pair": other}),
        )

    for copy in kv_copies(slot):
        copy.start()
    for copy in kv_copies(other):
        copy.wait_recv()

    def out_copy(kind, owner, peer):
        return remote(
            outb.at[at_rows(kind * images + peer * rows, rows)],
            x.at[at_rows(kind * rows, rows), at_lanes(owner * 128, 128)],
            x_s.at[kind, peer],
            x_r.at[kind, owner],
            {"seq": peer},
        )

    def text_keys(i):
        kind = lax.div(i, blocks)
        b = lax.rem(i + lax.div(me, 4), blocks)
        here = at_rows(kind * images + b * block, block)
        o = oacc[here, :] + attend(here, pl.ds(images, 2 * texts))
        inv = 1.0 / o[:, 128:256]
        out = o[:, 0:128] * inv
        outb[here, :] = out.astype(BF16)

        @pl.when(kind == 1)
        def _():
            outf[at_rows(b * block, block), :] = out
            rl[at_rows(b * block, block), :] = inv

        for j in range(4):
            peer = b * 4 + j

            @pl.when(peer != me)
            def _():
                out_copy(kind, me, peer).start()

            @pl.when(peer == me)
            def _():
                x[at_rows(kind * rows, rows), at_lanes(me * 128, 128)] = outb[
                    at_rows(kind * images + me * rows, rows), :
                ]

    each(2 * blocks, text_keys)

    def finish(peer):
        mod_copy(me, peer).wait_send()
        noisy_copy(me, peer).wait_send()
        text_copy(me, peer).wait_send()
        nz_copy(me, peer).wait_send()
        nz_copy(peer, peer).wait_recv()
        for kind in range(2):
            out_copy(kind, me, peer).wait_send()
            out_copy(kind, peer, peer).wait_recv()

    others(me, seqs, finish)

    def finish_dp(peer):
        dp_copy(mine, peer).wait_send()
        dp_copy(peer, peer).wait_recv()

    others(mine, dps, finish_dp)
    for copy in kv_copies(slot):
        copy.wait_send()


def middle_kernel(
    seqs, dps, model, sign, x, nz, kb, lat, noi, nown, nn, ne, shl, qp, kk, vext, pol, lhs, outf, rl, qg, aup,
    ua, value,
    km, ghs, gh, gapbuf, acc, csum,
    k_sem, g_s, g_r, e_s, e_r,
):
    me = lax.axis_index("seq")
    slot = lax.axis_index("pair")
    rows = lat.shape[0]
    ch = lat.shape[1]
    images = rows * seqs
    width = 128 * seqs
    model_width = float(model)
    count = kb.shape[0]
    barrier, total = greet([("seq", me, seqs), ("pair", slot, 2)])
    other = 1 - slot

    others(
        me,
        seqs,
        lambda peer: pl.semaphore_signal(
            barrier,
            inc=1,
            device_id={"seq": peer, "pair": other},
            device_id_type=pl.DeviceIdType.MESH,
        ),
    )

    def k_copy(i):
        h = lax.rem(i, seqs)
        j = lax.rem(h + lax.div(i, seqs), seqs)
        return pltpu.make_async_copy(
            kb.at[i], km.at[at_rows(h * 128, 128), at_lanes(j * 128, 128)], k_sem.at[0]
        )

    each(count, lambda i: k_copy(i).start())
    each(count, lambda i: k_copy(i).wait())
    xv = x[...]
    y = mm(xv, km[...])
    xn = mm(xv, nz[...])
    own = nown[:, 0:ch].astype(F32)
    noise2 = jnp.concatenate([own, own], 0)
    nn2 = jnp.concatenate([nn[:, 0:1], nn[:, 0:1]], 0)
    ne2 = jnp.concatenate([ne[...], ne[...]], 0)
    quad = (
        nn2
        + 2.0 * jnp.sum(noise2 * xn[:, ch : 2 * ch], -1, keepdims=True)
        + jnp.sum(xv.astype(F32) * y, -1, keepdims=True)
    )
    inv = lax.rsqrt(quad * (1.0 / model_width) + epsilon)
    proj = inv * (xn[:, 0:ch] + ne2)
    target = noi[...].astype(F32) - lat[...].astype(F32)
    diff = jnp.concatenate([target, target], 0) - (proj + shl[0:1, :])
    squares = diff * diff
    gap = (jnp.sum(squares[rows:]) - jnp.sum(squares[:rows])) * (1.0 / (images * ch))
    gapbuf[slot * seqs + me] = jnp.full((8, 128), gap, F32)

    d = diff[rows:]
    inv_p = inv[rows:]
    m = jnp.sum(d * proj[rows:], -1, keepdims=True) * (1.0 / model_width) * inv_p
    left = jnp.concatenate([d, -m * own], 1).astype(BF16)
    ghs[...] = (inv_p * (mm_nt(left, nz[...]) - m * y[rows:])).astype(BF16)

    pl.semaphore_wait(barrier, total + seqs - 1)

    def g_copy(owner, peer):
        return remote(
            ghs.at[:, at_lanes(peer * 128, 128)],
            gh.at[at_rows(owner * rows, rows)],
            g_s.at[peer],
            g_r.at[owner],
            {"seq": peer},
        )

    def gap_copy(to_slot, from_slot, owner, peer):
        return remote(
            gapbuf.at[slot * seqs + me],
            gapbuf.at[from_slot * seqs + owner],
            e_s.at[to_slot * seqs + peer],
            e_r.at[from_slot * seqs + owner],
            {"seq": peer, "pair": to_slot},
        )

    others(me, seqs, lambda peer: g_copy(me, peer).start())

    def send_gap(peer):
        gap_copy(slot, slot, me, peer).start()
        gap_copy(other, slot, me, peer).start()

    others(me, seqs, send_gap)
    gap_copy(other, slot, me, me).start()
    gh[at_rows(me * rows, rows), :] = ghs[:, at_lanes(me * 128, 128)]
    acc[...] = jnp.zeros_like(acc)
    csum[...] = jnp.zeros_like(csum)
    others(me, seqs, lambda peer: g_copy(peer, peer).wait_recv())
    block = 4 * rows
    gain = qg[...]
    keys = kk[...]
    vals = vext[:, 0:128]

    def back(i):
        here = at_rows(i * block, block)
        g = gh[here, :]
        p = jnp.exp2(mm_nt(qp[here, :], keys))
        gp = mm_nt(g, vals)
        dsum = jnp.sum(g.astype(F32) * outf[here, :], -1, keepdims=True)
        gs = (p * (gp - dsum)).astype(BF16)
        gq = mm(gs, keys) * (rl[here, :] * (1.0 / math.sqrt(128.0)))
        u = pol[here, :]
        r = rms_rows(u)
        w = gq * gain
        gd = (r * w - u * (r * r * r) * row_mean(u * w)).astype(BF16)
        acc[...] += mm_tn(lhs[here, :], gd)
        csum[...] += jnp.broadcast_to(
            jnp.sum(gd.astype(F32), 0, keepdims=True), csum.shape
        )

    each(images // block, back)

    def wait_gap(peer):
        gap_copy(slot, slot, peer, peer).wait_recv()
        gap_copy(slot, other, peer, peer).wait_recv()
        gap_copy(slot, slot, me, peer).wait_send()
        gap_copy(other, slot, me, peer).wait_send()
        g_copy(me, peer).wait_send()

    others(me, seqs, wait_gap)
    gap_copy(slot, other, me, me).wait_recv()
    gap_copy(other, slot, me, me).wait_send()
    own_gap = jnp.sum(gapbuf[pl.ds(slot * seqs, seqs)], 0)
    other_gap = jnp.sum(gapbuf[pl.ds(other * seqs, seqs)], 0)
    sgn = sign[0, 0]
    z = half_beta * sgn * (own_gap - other_gap)
    value[...] = jnp.maximum(z, 0.0) + jnp.log1p(jnp.exp(-jnp.abs(z)))
    weight = half_beta / dps / (1.0 + jnp.exp(-z))
    factor = (sgn * weight * (-2.0 / (images * ch)))[0:1, :]
    up = aup[:, at_lanes(me * 128, 128)]
    rank = up.shape[0]
    ua[0:rank, :] = acc[0:rank, :] * factor
    a_top, a_rest = halves(jnp.concatenate([acc[rank : rank + ch, :], csum[...]], 0))
    tail = mm_nt(a_top, up) + mm_nt(a_rest, up)
    ua[rank:, :] = jnp.concatenate([tail, tail], 1) * factor


def last_kernel(
    seqs, dps, ua, embed, moddp,
    down, upg,
    ubuf, abuf, a2, usum, asum, left, right,
    u_s, u_r, a_s, a_r, v_s, v_r, b_s, b_r,
):
    me = lax.axis_index("seq")
    slot = lax.axis_index("pair")
    mine = lax.axis_index("dp")
    width = embed.shape[1]
    ch = embed.shape[0]
    rank = upg.shape[0]
    tail = ua.shape[0] - rank
    reps = 2 * dps
    rep = slot * dps + mine
    barrier, total = greet([("seq", me, seqs)])

    def to(r):
        return {"pair": lax.div(r, dps), "dp": lax.rem(r, dps)}

    others(
        rep,
        reps,
        lambda peer: pl.semaphore_signal(
            barrier, inc=1, device_id=to(peer), device_id_type=pl.DeviceIdType.MESH
        ),
    )
    pl.semaphore_wait(barrier, total + reps - 1)

    def u_copy(owner, peer):
        return remote(
            ua.at[pl.ds(0, rank)], ubuf.at[owner], u_s.at[peer], u_r.at[owner], to(peer)
        )

    def a_copy(owner, peer):
        return remote(
            ua.at[pl.ds(rank, tail)], abuf.at[owner], a_s.at[peer], a_r.at[owner], {"seq": peer}
        )

    def v_copy(owner, peer):
        return remote(
            usum,
            upg.at[:, at_lanes(owner * 128, 128)],
            v_s.at[peer],
            v_r.at[owner],
            {"seq": peer},
        )

    def b_copy(owner, peer):
        return remote(asum, a2.at[owner], b_s.at[peer], b_r.at[owner], to(peer))

    others(rep, reps, lambda peer: u_copy(rep, peer).start())
    others(me, seqs, lambda peer: a_copy(me, peer).start())
    ubuf[rep] = ua[0:rank, :]
    abuf[me] = ua[rank:, :]
    emb_c = embed[...].astype(F32)
    emb_c = emb_c - row_mean(emb_c)
    first = lax.broadcasted_iota(jnp.int32, (8, width), 0) == 0
    for p in range(dps):
        shift = moddp[p, :, 0:width]
        scale = moddp[p, :, width:]
        scaled = emb_c * (1.0 + scale)
        extra = jnp.where(first, shift, 0.0)
        left[p * tail : (p + 1) * tail, :] = jnp.concatenate([scaled, extra], 0)
    others(rep, reps, lambda peer: u_copy(peer, peer).wait_recv())
    sums = jnp.sum(ubuf[...], 0)
    usum[...] = sums
    upg[:, at_lanes(me * 128, 128)] = sums
    others(me, seqs, lambda peer: v_copy(me, peer).start())
    others(me, seqs, lambda peer: a_copy(peer, peer).wait_recv())
    sums = jnp.sum(abuf[...], 0)
    asum[...] = sums
    a2[rep] = sums
    others(rep, reps, lambda peer: b_copy(rep, peer).start())
    others(rep, reps, lambda peer: b_copy(peer, peer).wait_recv())
    for p in range(dps):
        right[p * tail : (p + 1) * tail, :] = a2[p] + a2[dps + p]
    got = mm_tn(right[...].astype(BF16), left[...].astype(BF16))
    down[...] = got[0:ch, :].T

    def finish(peer):
        a_copy(me, peer).wait_send()
        v_copy(me, peer).wait_send()
        v_copy(peer, peer).wait_recv()

    others(me, seqs, finish)

    def finish_reps(peer):
        u_copy(rep, peer).wait_send()
        b_copy(rep, peer).wait_send()

    others(rep, reps, finish_reps)


def shape(dims, kind):
    return jax.ShapeDtypeStruct(dims, kind)


def call(kernel, ident, specs, outs, scratch, cost, *operands):
    return pl.pallas_call(
        kernel,
        out_shape=outs,
        in_specs=[pl.BlockSpec(memory_space=s) for s in specs],
        out_specs=[pl.BlockSpec(memory_space=pltpu.VMEM)] * len(outs),
        scratch_shapes=scratch,
        compiler_params=pltpu.CompilerParams(
            collective_id=ident, has_side_effects=True, vmem_limit_bytes=VMEM_BYTES
        ),
        cost_estimate=pl.CostEstimate(flops=cost, bytes_accessed=16 << 20, transcendentals=0),
    )(*operands)


def on_device(
    latents,
    noise,
    pair_timestep_index,
    preferred_image_slot,
    prompt_token_states,
    image_embed_weight,
    timestep_modulation_weight,
    image_query_key_value,
    text_key_value,
    query_norm_gain,
    key_norm_gain,
    adapter_down_weight,
    adapter_up_weight,
    image_output_weight,
    latent_out_weight,
):
    seqs = lax.axis_size("seq")
    dps = lax.axis_size("dp")
    slot = lax.axis_index("pair")
    rows, ch = latents.shape[2:]
    images = rows * seqs
    width = image_embed_weight.shape[1]
    texts = prompt_token_states.shape[1] * seqs
    keys = images + texts
    rank = adapter_down_weight.shape[1]
    step_value = pair_timestep_index[0].astype(jnp.float32)
    level = ((step_value + 1.0) / horizon).reshape(1, 1)
    emb = jnp.broadcast_to(
        sinusoid(step_value, timestep_modulation_weight.shape[0]).astype(BF16)[None],
        (16, timestep_modulation_weight.shape[0]),
    )
    lat = latents[0, 0]
    noi = noise[0]

    everyone = ("pair", "seq", "dp")
    moves = []
    for s in range(2):
        for h in range(seqs):
            for p in range(dps):
                source = (h + s * dps + p) % seqs
                moves.append(((s * seqs + source) * dps + p, (s * seqs + h) * dps + p))
    wo_c = image_output_weight.astype(F32)
    wo_c = (wo_c - jnp.mean(wo_c, -1, keepdims=True)).astype(BF16)
    wo_other = lax.ppermute(wo_c, everyone, moves)
    kb = lax.all_gather(mm_nt(wo_c, wo_other).astype(BF16), "seq")
    kb = lax.all_gather(kb, ("pair", "dp")).reshape(2, dps, seqs, 128, 128)
    kb = kb.reshape(-1, 128, 128)

    V, S, A = pltpu.VMEM, pltpu.SMEM, pl.ANY
    DMA = pltpu.SemaphoreType.DMA
    outs = [
        shape((2 * rows, 128 * seqs), BF16),
        shape((128 * seqs, 128), BF16),
        shape((1, 6 * width), F32),
        shape((dps, 1, 2 * width), F32),
        shape((images, 128), BF16),
        shape((keys, 128), BF16),
        shape((keys, 256), BF16),
        shape((images, 128), F32),
        shape((images, 128), BF16),
        shape((images, 128), F32),
        shape((images, 128), F32),
        shape((rows, 128), F32),
        shape((rows, ch), F32),
        shape((8, ch), F32),
    ]
    scratch = [
        V((images, 128), BF16),
        V((texts // 2, width), BF16),
        V((2 * images, 256), F32),
        V((2 * images, 128), BF16),
        V((2 * images, 128), BF16),
        V((1, timestep_modulation_weight.shape[1]), F32),
    ]
    scratch += [DMA((seqs,))] * 8 + [DMA((dps,))] * 2 + [DMA((2,))] * 2 + [DMA((2, seqs))] * 2
    front = call(
        functools.partial(front_kernel, seqs, dps),
        0,
        [S] + [V] * 14,
        outs,
        scratch,
        20 * 10**9,
        level,
        emb,
        lat,
        noi,
        prompt_token_states[0],
        image_embed_weight,
        timestep_modulation_weight,
        image_query_key_value.reshape(width, -1),
        text_key_value.reshape(width, -1),
        query_norm_gain.reshape(1, -1),
        key_norm_gain.reshape(1, -1),
        adapter_down_weight,
        adapter_up_weight,
        image_output_weight,
        latent_out_weight,
    )
    x, nz, mod, moddp, qp, kk, vext, pol, lhs, outf, rl, nn, ne, shl = front
    del mod
    nown = ((1.0 - level) * lat.astype(F32) + level * noi.astype(F32)).astype(BF16)
    sign = jnp.where(preferred_image_slot[0] == slot, 1.0, -1.0).astype(F32).reshape(1, 1)
    tail = ch + 8
    scratch = [
        V((128 * seqs, 128 * seqs), BF16),
        V((rows, 128 * seqs), BF16),
        V((images, 128), BF16),
        V((2 * seqs, 8, 128), F32),
        V((rank + ch, 128), F32),
        V((8, 128), F32),
        DMA((1,)),
        DMA((seqs,)),
        DMA((seqs,)),
        DMA((2 * seqs,)),
        DMA((2 * seqs,)),
    ]
    ua, value = call(
        functools.partial(middle_kernel, seqs, dps, width),
        1,
        [S, V, V, A] + [V] * 15,
        [shape((rank + tail, 128), F32), shape((8, 128), F32)],
        scratch,
        10 * 10**9,
        sign,
        x,
        nz,
        kb,
        lat,
        noi,
        nown,
        nn,
        ne,
        shl,
        qp,
        kk,
        vext,
        pol,
        lhs,
        outf,
        rl,
        query_norm_gain.reshape(1, -1),
        adapter_up_weight,
    )
    reps = 2 * dps
    scratch = [
        V((reps, rank, 128), F32),
        V((seqs, tail, 128), F32),
        V((reps, tail, 128), F32),
        V((rank, 128), F32),
        V((tail, 128), F32),
        V((dps * tail, width), F32),
        V((dps * tail, 128), F32),
    ]
    scratch += [DMA((reps,))] * 2 + [DMA((seqs,))] * 4 + [DMA((reps,))] * 2
    down, upg = call(
        functools.partial(last_kernel, seqs, dps),
        2,
        [V] * 3,
        [shape((width, rank), F32), shape((rank, 128 * seqs), F32)],
        scratch,
        10**9,
        ua,
        image_embed_weight,
        moddp,
    )
    return (down, upg, value[0, 0:1])


def solution(mesh):
    return jax.shard_map(
        on_device,
        mesh=mesh,
        in_specs=(
            P("dp", "pair", "seq", None),
            P("dp", "seq", None),
            P("dp"),
            P("dp"),
            P("dp", "seq", None),
            P(),
            P(None, "seq"),
            P(None, "seq", None),
            P(None, "seq", None),
            P(),
            P(),
            P(),
            P(),
            P("seq", None),
            P(),
        ),
        out_specs=(P(), P(), P("dp")),
        check_vma=False,
    )
```

```python
import functools
import math

import jax
import jax.numpy as jnp
from jax import lax
from jax.experimental import pallas as pl
from jax.experimental.pallas import tpu as pltpu
from jax.sharding import PartitionSpec as P

epsilon = 1e-06
half_beta = 20.0
horizon = 1000.0
F32 = jnp.float32
BF16 = jnp.bfloat16
VMEM_BYTES = 58 * 1024 * 1024


def sinusoid(step_value, width):
    half_width = width // 2
    freqs = jnp.exp(-math.log(10000.0) * jnp.arange(half_width, dtype=jnp.float32) / half_width)
    angle = step_value * freqs
    return jnp.concatenate([jnp.cos(angle), jnp.sin(angle)])


def mm(a, b):
    return lax.dot_general(a, b, (((1,), (0,)), ((), ())), preferred_element_type=F32)


def mm_nt(a, b):
    return lax.dot_general(a, b, (((1,), (1,)), ((), ())), preferred_element_type=F32)


def mm_tn(a, b):
    return lax.dot_general(a, b, (((0,), (0,)), ((), ())), preferred_element_type=F32)


def halves(a):
    top = a.astype(BF16)
    return top, (a - top.astype(F32)).astype(BF16)


def stacked(a):
    top, rest = halves(a)
    return jnp.concatenate([top, rest], 0)


def row_mean(a):
    return jnp.mean(a, -1, keepdims=True)


def rms_rows(rows):
    return lax.rsqrt(row_mean(rows * rows) + epsilon)


def remote(src, dst, send, recv, device):
    return pltpu.make_async_remote_copy(
        src_ref=src,
        dst_ref=dst,
        send_sem=send,
        recv_sem=recv,
        device_id=device,
        device_id_type=pl.DeviceIdType.MESH,
    )


def each(count, body):
    @pl.loop(0, count)
    def _(i):
        body(i)


def others(me, count, body):
    @pl.loop(1, count)
    def _(step):
        body(lax.rem(me + step, count))


def greet(axes):
    barrier = pltpu.get_barrier_semaphore()
    total = 0
    for axis, me, count in axes:
        others(
            me,
            count,
            lambda peer: pl.semaphore_signal(
                barrier,
                inc=1,
                device_id={axis: peer},
                device_id_type=pl.DeviceIdType.MESH,
            ),
        )
        total += count - 1
    return barrier, total


def at_rows(start, size):
    return pl.ds(pl.multiple_of(start, 16), size)


def at_lanes(start, size):
    return pl.ds(pl.multiple_of(start, 128), size)


def with_shift(scaled, shift):
    width = shift.shape[1]
    top, rest = halves(shift)
    which = lax.broadcasted_iota(jnp.int32, (16, width), 0)
    extra = jnp.where(
        which == 0,
        top.astype(F32),
        jnp.where(which == 1, rest.astype(F32), 0.0),
    )
    return jnp.concatenate([scaled, extra], 0).astype(BF16)


def main_kernel(
    seqs, dps, level, sign, emb, lat, noi, txt, embed, wmod, wimg, wtxt, qg, kg, adown_t, aup, wo, lw_t,
    ua, value, moddp,
    mod, noisy, text, oacc, q2, outb, modrow, x, wall, kk, vext, pol, lhs, outf, rl,
    mixed, gmix, gh, ghs, gapbuf, acc, csum,
    mod_s, mod_r, noi_s, noi_r, txt_s, txt_r, dp_s, dp_r, kv_s, kv_r, x_s, x_r,
    g_s, g_r, e_s, e_r, wz_s, wz_r, wx_s, wx_r, wy_s, wy_r, wc_s, wc_r,
):
    me = lax.axis_index("seq")
    slot = lax.axis_index("pair")
    mine = lax.axis_index("dp")
    other = 1 - slot
    rows, ch = lat.shape
    images = rows * seqs
    width = embed.shape[1]
    span = width // 2
    strip = 128 // dps
    ring = dps // 2
    half = txt.shape[0] // 2
    texts = half * seqs
    block = 4 * rows
    blocks = images // block
    part = wmod.shape[1]
    barrier, total = greet([("seq", me, seqs), ("dp", mine, dps)])
    total += seqs

    def greet_other(peer):
        pl.semaphore_signal(
            barrier,
            inc=1,
            device_id={"seq": peer, "pair": other},
            device_id_type=pl.DeviceIdType.MESH,
        )

    each(seqs, greet_other)

    mod_part = mm(emb[...], wmod[...])[0:1]
    modrow[...] = mod_part
    lev = level[0, 0]
    noisy_mine = (
        (1.0 - lev) * lat[...].astype(F32) + lev * noi[...].astype(F32)
    ).astype(BF16)
    noisy[at_rows(me * rows, rows), :] = jnp.concatenate([noisy_mine, noisy_mine], 1)
    mine_rows, mine_cols = at_rows(mine * strip, strip), at_lanes(slot * span, span)
    wall[me, mine_rows, mine_cols] = wo[mine_rows, mine_cols]
    t = txt[at_rows(slot * half, half), :].astype(F32)
    t = t - row_mean(t)
    text[at_rows(me * half, half), :] = (t * lax.rsqrt(row_mean(t * t) + epsilon)).astype(BF16)
    pl.semaphore_wait(barrier, total)

    def mod_copy(owner, peer):
        return remote(
            modrow,
            mod.at[:, at_lanes(owner * part, part)],
            mod_s.at[peer],
            mod_r.at[owner],
            {"seq": peer},
        )

    def noisy_copy(owner, peer):
        where = noisy.at[at_rows(owner * rows, rows)]
        return remote(where, where, noi_s.at[peer], noi_r.at[owner], {"seq": peer})

    def text_copy(owner, peer):
        where = text.at[at_rows(owner * half, half)]
        return remote(where, where, txt_s.at[peer], txt_r.at[owner], {"seq": peer})

    def dp_copy(owner, peer):
        return remote(
            mod.at[:, pl.ds(0, 2 * width)],
            moddp.at[owner],
            dp_s.at[peer],
            dp_r.at[owner],
            {"dp": peer},
        )

    def region(first, count, p, s):
        return wall.at[pl.ds(first, count), at_rows(p * strip, strip), at_lanes(s * span, span)]

    def z_copy(owner, peer):
        where = region(owner, 1, mine, slot)
        return remote(where, where, wz_s.at[peer], wz_r.at[owner], {"seq": peer})

    def along(step):
        return lax.rem(mine + 2 * step + dps, dps)

    def x_near(step, origin, to):
        where = region(0, seqs, origin, slot)
        return remote(where, where, wx_s.at[step], wx_r.at[step], {"dp": to})

    def x_far(step, origin, to):
        where = region(step * (seqs // 2), seqs // 2, origin, slot)
        return remote(where, where, wx_s.at[2 + step], wx_r.at[2 + step], {"dp": to})

    def y_copy(which, side, origin, s):
        where = region(side * (seqs // 2), seqs // 2, origin, s)
        to = me if side == 0 else lax.rem(me + seqs // 2, seqs)
        return remote(
            where,
            where,
            wy_s.at[which * 2 + side],
            wy_r.at[which * 2 + side],
            {"pair": other, "seq": to},
        )

    sibling = mine + 1 - 2 * lax.rem(mine, 2)

    def c_copy(which, origin, s):
        where = region(0, seqs, origin, s)
        return remote(where, where, wc_s.at[which], wc_r.at[which], {"dp": sibling})

    def spread(which, origin):
        y_copy(which, 0, origin, slot).start()
        y_copy(which, 1, origin, slot).start()
        c_copy(which, origin, slot).start()

    def send_small(peer):
        mod_copy(me, peer).start()
        noisy_copy(me, peer).start()

    others(me, seqs, send_small)
    others(me, seqs, lambda peer: z_copy(me, peer).start())
    others(me, seqs, lambda peer: text_copy(me, peer).start())
    mod[:, at_lanes(me * part, part)] = mod_part

    emb_c = embed[...].astype(F32)
    emb_c = emb_c - row_mean(emb_c)
    e_top, e_rest = halves(emb_c)
    gram = stacked(mm_nt(e_top, e_top) + mm_nt(e_top, e_rest) + mm_nt(e_rest, e_top))

    others(me, seqs, lambda peer: mod_copy(peer, peer).wait_recv())
    shift_img, scale_img, shift_txt, scale_txt, shift_out, scale_out = [
        mod[:, i * width : (i + 1) * width] for i in range(6)
    ]
    moddp[mine] = mod[:, 0 : 2 * width]
    others(mine, dps, lambda peer: dp_copy(mine, peer).start())

    img_lhs = with_shift(emb_c * (1.0 + scale_img), shift_img)
    img_m = mm(img_lhs, wimg[...])
    img_m2 = stacked(img_m[0:ch])
    img_shift = img_m[ch : ch + 1] + img_m[ch + 1 : ch + 2]
    low_m = mm_nt(img_lhs, adown_t[...])
    low_m2 = stacked(low_m[0:ch])
    low_shift = low_m[ch : ch + 1] + low_m[ch + 1 : ch + 2]
    up = aup[:, at_lanes(me * 128, 128)]
    gain_q = qg[...]
    gain_k = kg[...]
    score_scale = math.log2(math.e) / math.sqrt(128.0)
    vext[:, 128:256] = jnp.ones((vext.shape[0], 128), BF16)

    others(me, seqs, lambda peer: noisy_copy(peer, peer).wait_recv())

    def project(i):
        here = at_rows(i * block, block)
        nb = noisy[here, :]
        nf = nb[:, 0:ch].astype(F32)
        var = jnp.sum(mm(nb, gram) * nf, -1, keepdims=True) * (1.0 / width)
        inv = lax.rsqrt(var + epsilon)
        qkv = mm(nb, img_m2) * inv + img_shift
        low = (mm(nb, low_m2) * inv + low_shift).astype(BF16)
        delta = mm(low, up).astype(BF16).astype(F32)
        q = qkv[:, 0:128]
        k = qkv[:, 128:256]
        q_pol = q + delta
        q2[here, :] = (q * rms_rows(q) * (gain_q * score_scale)).astype(BF16)
        q2[at_rows(images + i * block, block), :] = (
            q_pol * rms_rows(q_pol) * (gain_q * score_scale)
        ).astype(BF16)
        pol[here, :] = q_pol
        kk[here, :] = (k * rms_rows(k) * gain_k).astype(BF16)
        vext[here, 0:128] = qkv[:, 256:384].astype(BF16)
        lhs[here, :] = jnp.concatenate([low, (nf * inv).astype(BF16)], 1)

    each(blocks, project)

    others(me, seqs, lambda peer: z_copy(peer, peer).wait_recv())
    if ring > 1:
        x_near(0, mine, along(1)).start()
        x_near(1, mine, along(-1)).start()
    spread(0, mine)

    def attend(here, keys):
        s = mm_nt(q2[here, :], kk[keys, :])
        return mm(jnp.exp2(s).astype(BF16), vext[keys, :])

    def image_keys(i):
        here = at_rows(i * block, block)
        oacc[here, :] = attend(here, pl.ds(0, images))

    each(2 * blocks, image_keys)

    if ring > 1:
        x_near(0, along(-1), along(1)).wait_recv()
        x_far(0, along(-1), along(1)).start()
        spread(1, along(-1))
        x_near(1, along(1), along(-1)).wait_recv()
        x_far(1, along(1), along(-1)).start()
        spread(2, along(1))

    others(me, seqs, lambda peer: text_copy(peer, peer).wait_recv())
    text_n = (text[...].astype(F32) * (1.0 + scale_txt) + shift_txt).astype(BF16)
    kv = mm(text_n, wtxt[...])
    k = kv[:, 0:128]
    my_keys = at_rows(images + slot * texts, texts)
    kk[my_keys, :] = (k * rms_rows(k) * gain_k).astype(BF16)
    vext[my_keys, 0:128] = kv[:, 128:256].astype(BF16)

    def kv_copies(owner):
        keys = at_rows(images + owner * texts, texts)
        v = vext.at[keys, pl.ds(0, 128)]
        return (
            remote(kk.at[keys], kk.at[keys], kv_s.at[0], kv_r.at[0], {"pair": other}),
            remote(v, v, kv_s.at[1], kv_r.at[1], {"pair": other}),
        )

    for copy in kv_copies(slot):
        copy.start()
    for copy in kv_copies(other):
        copy.wait_recv()

    def out_copy(kind, owner, peer):
        return remote(
            outb.at[at_rows(kind * images + peer * rows, rows)],
            x.at[at_rows(kind * rows, rows), at_lanes(owner * 128, 128)],
            x_s.at[kind, peer],
            x_r.at[kind, owner],
            {"seq": peer},
        )

    def text_keys(i):
        kind = lax.div(i, blocks)
        b = lax.rem(i + lax.div(me, 4), blocks)
        here = at_rows(kind * images + b * block, block)
        o = oacc[here, :] + attend(here, pl.ds(images, 2 * texts))
        inv = 1.0 / o[:, 128:256]
        out = o[:, 0:128] * inv
        outb[here, :] = out.astype(BF16)

        @pl.when(kind == 1)
        def _():
            outf[at_rows(b * block, block), :] = out
            rl[at_rows(b * block, block), :] = inv

        for j in range(4):
            peer = b * 4 + j

            @pl.when(peer != me)
            def _():
                out_copy(kind, me, peer).start()

            @pl.when(peer == me)
            def _():
                x[at_rows(kind * rows, rows), at_lanes(me * 128, 128)] = outb[
                    at_rows(kind * images + me * rows, rows), :
                ]

    each(2 * blocks, text_keys)

    if ring > 1:
        x_far(0, along(2), along(1)).wait_recv()
        x_far(1, along(2), along(-1)).wait_recv()
        spread(3, along(2))
    for which in range(ring):
        origin = [mine, along(-1), along(1), along(2)][which]
        y_copy(which, 0, origin, other).wait_recv()
        y_copy(which, 1, origin, other).wait_recv()
        c_copy(4 + which, origin, other).start()
    for which in range(ring):
        origin = [sibling, lax.rem(sibling - 2 + dps, dps), lax.rem(sibling + 2, dps), lax.rem(sibling + 4, dps)][which]
        c_copy(which, origin, slot).wait_recv()
        c_copy(4 + which, origin, other).wait_recv()

    def finish_out(peer):
        for kind in range(2):
            out_copy(kind, peer, peer).wait_recv()

    others(me, seqs, finish_out)

    own = noisy[at_rows(me * rows, rows), :][:, 0:ch]
    tile = 256
    xv = x[...]

    def mix(i):
        here = at_lanes(i * tile, tile)
        states = mm(own, embed[:, here])
        w = wall[:, :, here].reshape(128 * seqs, tile)
        mixed[:, here] = mm(xv, w) + jnp.concatenate([states, states], 0)

    each(width // tile, mix)
    full = mixed[...]
    full = full - row_mean(full)
    inv = lax.rsqrt(row_mean(full * full) + epsilon)
    unit = full * inv
    mixed[...] = unit
    pred = mm_nt((unit * (1.0 + scale_out) + shift_out).astype(BF16), lw_t[...])
    target = noi[...].astype(F32) - lat[...].astype(F32)
    diff = jnp.concatenate([target, target], 0) - pred
    squares = diff * diff
    gap = (jnp.sum(squares[rows:]) - jnp.sum(squares[:rows])) * (1.0 / (images * ch))
    gapbuf[slot * seqs + me] = jnp.full((8, 128), gap, F32)

    def gap_copy(to_slot, from_slot, owner, peer):
        return remote(
            gapbuf.at[slot * seqs + me],
            gapbuf.at[from_slot * seqs + owner],
            e_s.at[to_slot * seqs + peer],
            e_r.at[from_slot * seqs + owner],
            {"seq": peer, "pair": to_slot},
        )

    g_ln = mm(diff[rows:].astype(BF16), lw_t[...]) * (1.0 + scale_out)
    unit_p = mixed[rows:, :]
    gmix[...] = (
        (g_ln - row_mean(g_ln) - unit_p * row_mean(g_ln * unit_p)) * inv[rows:]
    ).astype(BF16)

    def g_copy(owner, peer):
        return remote(
            ghs.at[peer],
            gh.at[at_rows(owner * rows, rows)],
            g_s.at[peer],
            g_r.at[owner],
            {"seq": peer},
        )

    def heads_back(i):
        pair = lax.rem(i + lax.div(me, 2), seqs // 2)
        w = wall[pl.ds(2 * pair, 2)].reshape(256, width)
        g = mm_nt(gmix[...], w).astype(BF16)
        for j in range(2):
            peer = 2 * pair + j
            ghs[peer] = g[:, j * 128 : (j + 1) * 128]

            @pl.when(peer != me)
            def _():
                g_copy(me, peer).start()

            @pl.when(peer == me)
            def _():
                gh[at_rows(me * rows, rows), :] = ghs[me]

    each(seqs // 2, heads_back)

    def send_gap(peer):
        gap_copy(slot, slot, me, peer).start()
        gap_copy(other, slot, me, peer).start()

    others(me, seqs, send_gap)
    gap_copy(other, slot, me, me).start()
    acc[...] = jnp.zeros_like(acc)
    csum[...] = jnp.zeros_like(csum)
    others(me, seqs, lambda peer: g_copy(peer, peer).wait_recv())
    keys = kk[...]
    vals = vext[:, 0:128]

    def back(i):
        here = at_rows(i * block, block)
        g = gh[here, :]
        p = jnp.exp2(mm_nt(q2[at_rows(images + i * block, block), :], keys))
        gp = mm_nt(g, vals)
        dsum = jnp.sum(g.astype(F32) * outf[here, :], -1, keepdims=True)
        gs = (p * (gp - dsum)).astype(BF16)
        gq = mm(gs, keys) * (rl[here, :] * (1.0 / math.sqrt(128.0)))
        u = pol[here, :]
        r = rms_rows(u)
        w = gq * gain_q
        gd = (r * w - u * (r * r * r) * row_mean(u * w)).astype(BF16)
        acc[...] += mm_tn(lhs[here, :], gd)
        csum[...] += jnp.broadcast_to(
            jnp.sum(gd.astype(F32), 0, keepdims=True), csum.shape
        )

    each(blocks, back)

    def finish(peer):
        mod_copy(me, peer).wait_send()
        noisy_copy(me, peer).wait_send()
        text_copy(me, peer).wait_send()
        z_copy(me, peer).wait_send()
        for kind in range(2):
            out_copy(kind, me, peer).wait_send()
        gap_copy(slot, slot, peer, peer).wait_recv()
        gap_copy(slot, other, peer, peer).wait_recv()
        gap_copy(slot, slot, me, peer).wait_send()
        gap_copy(other, slot, me, peer).wait_send()
        g_copy(me, peer).wait_send()

    others(me, seqs, finish)
    gap_copy(slot, other, me, me).wait_recv()
    gap_copy(other, slot, me, me).wait_send()

    def finish_dp(peer):
        dp_copy(mine, peer).wait_send()
        dp_copy(peer, peer).wait_recv()

    others(mine, dps, finish_dp)
    for copy in kv_copies(slot):
        copy.wait_send()
    if ring > 1:
        for step in range(2):
            x_near(step, mine, along(1)).wait_send()
            x_far(step, mine, along(1)).wait_send()
    for which in range(ring):
        for side in range(2):
            y_copy(which, side, mine, slot).wait_send()
        c_copy(which, mine, slot).wait_send()
        c_copy(4 + which, mine, slot).wait_send()

    own_gap = jnp.sum(gapbuf[pl.ds(slot * seqs, seqs)], 0)
    other_gap = jnp.sum(gapbuf[pl.ds(other * seqs, seqs)], 0)
    sgn = sign[0, 0]
    z = half_beta * sgn * (own_gap - other_gap)
    value[...] = jnp.maximum(z, 0.0) + jnp.log1p(jnp.exp(-jnp.abs(z)))
    weight = half_beta / dps / (1.0 + jnp.exp(-z))
    factor = (sgn * weight * (-2.0 / (images * ch)))[0:1, :]
    rank = up.shape[0]
    ua[0:rank, :] = (acc[0:rank, :] * factor).astype(BF16)
    a_top, a_rest = halves(jnp.concatenate([acc[rank : rank + ch, :], csum[...]], 0))
    tail = mm_nt(a_top, up) + mm_nt(a_rest, up)
    lower = jnp.concatenate([tail[0 : ch // 2], tail[ch // 2 : ch]], 1)
    lowest = jnp.concatenate([tail[ch:], tail[ch:]], 1)
    packed = jnp.concatenate([lower, lowest, lowest], 0) * factor
    ua[rank:, :] = packed.astype(BF16)


def last_kernel(
    seqs, dps, ua, embed, moddp,
    down_t, upg,
    ubuf, abuf, a2, usum, asum, left, right, upb,
    u_s, u_r, a_s, a_r, v_s, v_r, b_s, b_r,
):
    me = lax.axis_index("seq")
    slot = lax.axis_index("pair")
    mine = lax.axis_index("dp")
    width = embed.shape[1]
    ch = embed.shape[0]
    rank = upg.shape[0]
    tail = ua.shape[0] - rank
    reps = 2 * dps
    rep = slot * dps + mine
    barrier, total = greet([("seq", me, seqs)])

    def to(r):
        return {"pair": lax.div(r, dps), "dp": lax.rem(r, dps)}

    others(
        rep,
        reps,
        lambda peer: pl.semaphore_signal(
            barrier, inc=1, device_id=to(peer), device_id_type=pl.DeviceIdType.MESH
        ),
    )
    pl.semaphore_wait(barrier, total + reps - 1)

    def u_copy(owner, peer):
        return remote(
            ua.at[pl.ds(0, rank)], ubuf.at[owner], u_s.at[peer], u_r.at[owner], to(peer)
        )

    def a_copy(owner, peer):
        return remote(
            ua.at[pl.ds(rank, tail)], abuf.at[owner], a_s.at[peer], a_r.at[owner], {"seq": peer}
        )

    def v_copy(owner, peer):
        return remote(
            usum,
            upb.at[:, at_lanes(owner * 128, 128)],
            v_s.at[peer],
            v_r.at[owner],
            {"seq": peer},
        )

    def b_copy(owner, peer):
        return remote(asum, a2.at[owner], b_s.at[peer], b_r.at[owner], to(peer))

    others(rep, reps, lambda peer: u_copy(rep, peer).start())
    others(me, seqs, lambda peer: a_copy(me, peer).start())
    ubuf[rep] = ua[0:rank, :]
    abuf[me] = ua[rank:, :]
    emb_c = embed[...].astype(F32)
    emb_c = emb_c - row_mean(emb_c)
    first = lax.broadcasted_iota(jnp.int32, (16, width), 0) == 0
    deep = ch + 16
    for p in range(dps):
        shift = moddp[p, :, 0:width]
        scale = moddp[p, :, width:]
        scaled = emb_c * (1.0 + scale)
        extra = jnp.where(first, shift, 0.0)
        left[p * deep : (p + 1) * deep, :] = jnp.concatenate([scaled, extra], 0).astype(BF16)
    others(rep, reps, lambda peer: u_copy(peer, peer).wait_recv())
    sums = jnp.sum(ubuf[...].astype(F32), 0).astype(BF16)
    usum[...] = sums
    upb[:, at_lanes(me * 128, 128)] = sums
    others(me, seqs, lambda peer: v_copy(me, peer).start())
    others(me, seqs, lambda peer: a_copy(peer, peer).wait_recv())
    sums = jnp.sum(abuf[...].astype(F32), 0).astype(BF16)
    asum[...] = sums
    a2[rep] = sums
    others(rep, reps, lambda peer: b_copy(rep, peer).start())
    others(rep, reps, lambda peer: b_copy(peer, peer).wait_recv())
    for p in range(dps):
        a = a2[p].astype(F32) + a2[dps + p].astype(F32)
        top = a[0 : ch // 2]
        right[p * deep : (p + 1) * deep, :] = jnp.concatenate(
            [top[:, 0:ch], top[:, ch:], a[ch // 2 :, 0:ch]], 0
        ).astype(BF16)
    down_t[...] = mm_tn(right[...], left[...])

    def finish(peer):
        a_copy(me, peer).wait_send()
        v_copy(me, peer).wait_send()
        v_copy(peer, peer).wait_recv()

    others(me, seqs, finish)
    upg[...] = upb[...].astype(F32)

    def finish_reps(peer):
        u_copy(rep, peer).wait_send()
        b_copy(rep, peer).wait_send()

    others(rep, reps, finish_reps)


def shape(dims, kind):
    return jax.ShapeDtypeStruct(dims, kind)


def call(kernel, ident, specs, outs, scratch, cost, *operands):
    return pl.pallas_call(
        kernel,
        out_shape=outs,
        in_specs=[pl.BlockSpec(memory_space=s) for s in specs],
        out_specs=[pl.BlockSpec(memory_space=pltpu.VMEM)] * len(outs),
        scratch_shapes=scratch,
        compiler_params=pltpu.CompilerParams(
            collective_id=ident, has_side_effects=True, vmem_limit_bytes=VMEM_BYTES
        ),
        cost_estimate=pl.CostEstimate(flops=cost, bytes_accessed=16 << 20, transcendentals=0),
    )(*operands)


def on_device(
    latents,
    noise,
    pair_timestep_index,
    preferred_image_slot,
    prompt_token_states,
    image_embed_weight,
    timestep_modulation_weight,
    image_query_key_value,
    text_key_value,
    query_norm_gain,
    key_norm_gain,
    adapter_down_weight,
    adapter_up_weight,
    image_output_weight,
    latent_out_weight,
):
    seqs = lax.axis_size("seq")
    dps = lax.axis_size("dp")
    slot = lax.axis_index("pair")
    rows, ch = latents.shape[2:]
    images = rows * seqs
    width = image_embed_weight.shape[1]
    texts = prompt_token_states.shape[1] * seqs
    keys = images + texts
    rank = adapter_down_weight.shape[1]
    step_value = pair_timestep_index[0].astype(jnp.float32)
    level = ((step_value + 1.0) / horizon).reshape(1, 1)
    emb = jnp.broadcast_to(
        sinusoid(step_value, timestep_modulation_weight.shape[0]).astype(BF16)[None],
        (16, timestep_modulation_weight.shape[0]),
    )
    lat = latents[0, 0]
    noi = noise[0]

    sign = jnp.where(preferred_image_slot[0] == slot, 1.0, -1.0).astype(F32).reshape(1, 1)
    V, S = pltpu.VMEM, pltpu.SMEM
    DMA = pltpu.SemaphoreType.DMA
    tail = ch // 2 + 16
    heads = 128 * seqs
    scratch = [
        V((1, 6 * width), F32),
        V((images, 128), BF16),
        V((texts // 2, width), BF16),
        V((2 * images, 256), F32),
        V((2 * images, 128), BF16),
        V((2 * images, 128), BF16),
        V((1, timestep_modulation_weight.shape[1]), F32),
        V((2 * rows, heads), BF16),
        V((seqs, 128, width), BF16),
        V((keys, 128), BF16),
        V((keys, 256), BF16),
        V((images, 128), F32),
        V((images, 128), BF16),
        V((images, 128), F32),
        V((images, 128), F32),
        V((2 * rows, width), F32),
        V((rows, width), BF16),
        V((images, 128), BF16),
        V((seqs, rows, 128), BF16),
        V((2 * seqs, 8, 128), F32),
        V((rank + ch, 128), F32),
        V((8, 128), F32),
    ]
    scratch += [DMA((seqs,))] * 6 + [DMA((dps,))] * 2 + [DMA((2,))] * 2 + [DMA((2, seqs))] * 2
    scratch += [DMA((seqs,))] * 2 + [DMA((2 * seqs,))] * 2 + [DMA((seqs,))] * 2
    scratch += [DMA((4,))] * 2 + [DMA((8,))] * 4
    ua, value, moddp = call(
        functools.partial(main_kernel, seqs, dps),
        0,
        [S, S] + [V] * 14,
        [
            shape((rank + tail, 128), BF16),
            shape((8, 128), F32),
            shape((dps, 1, 2 * width), F32),
        ],
        scratch,
        30 * 10**9,
        level,
        sign,
        emb,
        lat,
        noi,
        prompt_token_states[0],
        image_embed_weight,
        timestep_modulation_weight,
        image_query_key_value.reshape(width, -1),
        text_key_value.reshape(width, -1),
        query_norm_gain.reshape(1, -1),
        key_norm_gain.reshape(1, -1),
        adapter_down_weight.T,
        adapter_up_weight,
        image_output_weight,
        latent_out_weight.T,
    )
    reps = 2 * dps
    deep = ch + 16
    scratch = [
        V((reps, rank, 128), BF16),
        V((seqs, tail, 128), BF16),
        V((reps, tail, 128), BF16),
        V((rank, 128), BF16),
        V((tail, 128), BF16),
        V((dps * deep, width), BF16),
        V((dps * deep, ch), BF16),
        V((rank, heads), BF16),
    ]
    scratch += [DMA((reps,))] * 2 + [DMA((seqs,))] * 4 + [DMA((reps,))] * 2
    down_t, upg = call(
        functools.partial(last_kernel, seqs, dps),
        1,
        [V] * 3,
        [shape((ch, width), F32), shape((rank, heads), F32)],
        scratch,
        10**9,
        ua,
        image_embed_weight,
        moddp,
    )
    return (down_t.T, upg, value[0, 0:1])


def solution(mesh):
    return jax.shard_map(
        on_device,
        mesh=mesh,
        in_specs=(
            P("dp", "pair", "seq", None),
            P("dp", "seq", None),
            P("dp"),
            P("dp"),
            P("dp", "seq", None),
            P(),
            P(None, "seq"),
            P(None, "seq", None),
            P(None, "seq", None),
            P(),
            P(),
            P(),
            P(),
            P("seq", None),
            P(),
        ),
        out_specs=(P(), P(), P("dp")),
        check_vma=False,
    )
```

```python
import functools
import math

import jax
import jax.numpy as jnp
from jax import lax
from jax.experimental import pallas as pl
from jax.experimental.pallas import tpu as pltpu
from jax.sharding import PartitionSpec as P

epsilon = 1e-06
half_beta = 20.0
horizon = 1000.0
F32 = jnp.float32
BF16 = jnp.bfloat16
VMEM_BYTES = 58 * 1024 * 1024


def sinusoid(step_value, width):
    half_width = width // 2
    freqs = jnp.exp(-math.log(10000.0) * jnp.arange(half_width, dtype=jnp.float32) / half_width)
    angle = step_value * freqs
    return jnp.concatenate([jnp.cos(angle), jnp.sin(angle)])


def mm(a, b):
    return lax.dot_general(a, b, (((1,), (0,)), ((), ())), preferred_element_type=F32)


def mm_nt(a, b):
    return lax.dot_general(a, b, (((1,), (1,)), ((), ())), preferred_element_type=F32)


def mm_tn(a, b):
    return lax.dot_general(a, b, (((0,), (0,)), ((), ())), preferred_element_type=F32)


def halves(a):
    top = a.astype(BF16)
    return top, (a - top.astype(F32)).astype(BF16)


def stacked(a):
    top, rest = halves(a)
    return jnp.concatenate([top, rest], 0)


def row_mean(a):
    return jnp.mean(a, -1, keepdims=True)


def rms_rows(rows):
    return lax.rsqrt(row_mean(rows * rows) + epsilon)


def remote(src, dst, send, recv, device):
    return pltpu.make_async_remote_copy(
        src_ref=src,
        dst_ref=dst,
        send_sem=send,
        recv_sem=recv,
        device_id=device,
        device_id_type=pl.DeviceIdType.MESH,
    )


def each(count, body):
    @pl.loop(0, count)
    def _(i):
        body(i)


def others(me, count, body):
    @pl.loop(1, count)
    def _(step):
        body(lax.rem(me + step, count))


def greet(axes):
    barrier = pltpu.get_barrier_semaphore()
    total = 0
    for axis, me, count in axes:
        others(
            me,
            count,
            lambda peer: pl.semaphore_signal(
                barrier,
                inc=1,
                device_id={axis: peer},
                device_id_type=pl.DeviceIdType.MESH,
            ),
        )
        total += count - 1
    return barrier, total


def at_rows(start, size):
    return pl.ds(pl.multiple_of(start, 16), size)


def at_lanes(start, size):
    return pl.ds(pl.multiple_of(start, 128), size)


def with_shift(scaled, shift):
    width = shift.shape[1]
    top, rest = halves(shift)
    which = lax.broadcasted_iota(jnp.int32, (16, width), 0)
    extra = jnp.where(
        which == 0,
        top.astype(F32),
        jnp.where(which == 1, rest.astype(F32), 0.0),
    )
    return jnp.concatenate([scaled, extra], 0).astype(BF16)


def main_kernel(
    seqs, dps, step, pref, emb, lat_t, noi_t, txt, embed, wmod, wimg, wtxt, qg, kg, adown_t, aup, wo, lw_t,
    down, upb, value,
    wimg_v, wtxt_v, mod, moddp, noisy, text, oacc, q2, outb, modrow, x, wall, kk, vext, pol, lhs, outf, rl,
    mixed, gmix, gh, ghs, gapbuf, acc, csum, ua, ubuf, abuf, a2, usum, asum, left, right,
    in_s, mod_s, mod_r, noi_s, noi_r, txt_s, txt_r, dp_s, dp_r, kv_s, kv_r, x_s, x_r,
    g_s, g_r, e_s, e_r, wz_s, wz_r, wx_s, wx_r, wy_s, wy_r, wc_s, wc_r,
    u_s, u_r, a_s, a_r, v_s, v_r, b_s, b_r,
):
    me = lax.axis_index("seq")
    slot = lax.axis_index("pair")
    mine = lax.axis_index("dp")
    other = 1 - slot
    ch, rows = lat_t.shape
    images = rows * seqs
    width = embed.shape[1]
    span = width // 2
    strip = 128 // dps
    origins = dps // 2
    half = txt.shape[0] // 2
    texts = half * seqs
    block = 4 * rows
    blocks = images // block
    part = wmod.shape[1]
    zs = seqs // 2
    z_at, hi = lax.rem(me, zs), lax.div(me, zs)
    flip = lax.rem(me + zs, seqs)
    reps = 2 * dps
    rep = slot * dps + mine

    loads = [
        pltpu.make_async_copy(
            wo.at[at_rows(mine * strip, strip), at_lanes(slot * span, span)],
            wall.at[me, at_rows(mine * strip, strip), at_lanes(slot * span, span)],
            in_s.at[0],
        ),
        pltpu.make_async_copy(wimg, wimg_v, in_s.at[1]),
        pltpu.make_async_copy(wtxt, wtxt_v, in_s.at[2]),
    ]
    for load in loads:
        load.start()
    barrier, total = greet([("seq", me, seqs), ("dp", mine, dps)])
    total += seqs + dps - 1

    def greet_other(device):
        pl.semaphore_signal(
            barrier, inc=1, device_id=device, device_id_type=pl.DeviceIdType.MESH
        )

    each(seqs, lambda peer: greet_other({"seq": peer, "pair": other}))
    others(mine, dps, lambda peer: greet_other({"dp": peer, "pair": other}))

    mod_part = mm(jnp.broadcast_to(emb[...].astype(F32), (16, emb.shape[1])).astype(BF16), wmod[...])[0:1]
    modrow[...] = mod_part
    lev = (step[0].astype(F32) + 1.0) * (1.0 / horizon)
    lat_f = lat_t[...].astype(F32)
    noi_f = noi_t[...].astype(F32)
    own = ((1.0 - lev) * lat_f + lev * noi_f).T.astype(BF16)
    target = (noi_f - lat_f).T
    noisy[me] = jnp.concatenate([own[0 : rows // 2], own[rows // 2 :]], 1)
    t = txt[at_rows(slot * half, half), :].astype(F32)
    t = t - row_mean(t)
    text[at_rows(me * half, half), :] = (t * lax.rsqrt(row_mean(t * t) + epsilon)).astype(BF16)
    loads[0].wait()
    pl.semaphore_wait(barrier, total)

    def mod_copy(owner, peer):
        return remote(
            modrow,
            mod.at[:, at_lanes(owner * part, part)],
            mod_s.at[peer],
            mod_r.at[owner],
            {"seq": peer},
        )

    def noisy_copy(owner, peer):
        where = noisy.at[owner]
        return remote(where, where, noi_s.at[peer], noi_r.at[owner], {"seq": peer})

    def dp_copy(owner, peer):
        return remote(
            mod.at[:, pl.ds(0, 2 * width)],
            moddp.at[owner],
            dp_s.at[peer],
            dp_r.at[owner],
            {"dp": peer},
        )

    def region(first, count, p, s):
        return wall.at[pl.ds(first, count), at_rows(p * strip, strip), at_lanes(s * span, span)]

    def owner_at(h, away):
        return h * zs + lax.rem(z_at + away + zs, zs)

    right_z, left_z = owner_at(hi, 1), owner_at(hi, -1)

    def ring_copy(kind, lane, owner, to):
        if kind == 0:
            where, send, recv = region(owner, 1, mine, slot), wz_s, wz_r
        else:
            where, send, recv = text.at[at_rows(owner * half, half)], txt_s, txt_r
        return remote(where, where, send.at[lane * seqs + owner], recv.at[owner], {"seq": to})

    def ring_sends(kind, hop):
        last = hop == zs // 2
        sends = []
        for h in range(2):
            if not last or h == 0:
                sends.append(ring_copy(kind, 1, owner_at(h, 1 - hop), right_z))
            if not last or h == 1:
                sends.append(ring_copy(kind, 2, owner_at(h, hop - 1), left_z))
        return sends

    def ring_first(kind):
        ring_copy(kind, 0, me, flip).start()
        if zs > 2:
            ring_copy(kind, 1, me, right_z).start()
            ring_copy(kind, 2, me, left_z).start()

    def ring_hop(kind, hop):
        if hop == 1:
            ring_copy(kind, 0, flip, flip).wait_recv()
            if zs > 2:
                ring_copy(kind, 1, flip, right_z).start()
                ring_copy(kind, 2, flip, left_z).start()
                return
        else:
            for h in range(2):
                ring_copy(kind, 0, owner_at(h, 1 - hop), flip).wait_recv()
                ring_copy(kind, 0, owner_at(h, hop - 1), flip).wait_recv()
        for copy in ring_sends(kind, hop):
            copy.start()

    def ring_end(kind):
        ring_copy(kind, 0, owner_at(0, zs // 2), flip).wait_recv()
        ring_copy(kind, 0, owner_at(1, zs // 2), flip).wait_recv()

    def ring_sent(kind):
        ring_copy(kind, 0, me, flip).wait_send()
        for hop in range(1, zs // 2 + 1):
            for copy in ring_sends(kind, hop):
                copy.wait_send()

    hops = zs // 2

    def along(away):
        return lax.rem(mine + 2 * away + dps, dps)

    places = [mine, along(-1), along(1), along(2)]
    sibling = mine + 1 - 2 * lax.rem(mine, 2)

    def chunk(origin, which_half, s):
        return region(which_half * (seqs // 2), seqs // 2, origin, s)

    def x_near(way, turn, origin):
        where = chunk(origin, turn if way == 0 else 1 - turn, slot)
        at = way * 2 + turn
        return remote(where, where, wx_s.at[at], wx_r.at[at], {"dp": along(1 - 2 * way)})

    def x_far(way, origin):
        where = chunk(origin, way, slot)
        return remote(where, where, wx_s.at[4 + way], wx_r.at[4 + way], {"dp": along(1 - 2 * way)})

    def y_copy(which, side, s):
        where = chunk(places[which], side, s)
        to = me if side == 0 else flip
        at = which * 2 + side
        return remote(where, where, wy_s.at[at], wy_r.at[at], {"pair": other, "seq": to})

    def c_copy(foreign, which, side, at_sibling):
        origin = places[which]
        if at_sibling:
            origin = sibling - mine + origin
        where = chunk(origin, side, other if foreign else slot)
        at = (foreign * 4 + which) * 2 + side
        return remote(where, where, wc_s.at[at], wc_r.at[at], {"dp": sibling})

    def spread(which, side):
        y_copy(which, side, slot).start()
        c_copy(0, which, side, False).start()

    def relay(which):
        for side in range(2):
            y_copy(which, side, other).wait_recv()
            c_copy(1, which, side, False).start()

    def send_small(peer):
        mod_copy(me, peer).start()
        noisy_copy(me, peer).start()

    others(me, seqs, send_small)
    ring_first(0)
    mod[:, at_lanes(me * part, part)] = mod_part

    emb_c = embed[...].astype(F32)
    emb_c = emb_c - row_mean(emb_c)
    e_top, e_rest = halves(emb_c)
    gram = stacked(mm_nt(e_top, e_top) + mm_nt(e_top, e_rest) + mm_nt(e_rest, e_top))
    ring_hop(0, 1)

    others(me, seqs, lambda peer: mod_copy(peer, peer).wait_recv())
    shift_img, scale_img, shift_txt, scale_txt, shift_out, scale_out = [
        mod[:, i * width : (i + 1) * width] for i in range(6)
    ]
    moddp[mine] = mod[:, 0 : 2 * width]
    others(mine, dps, lambda peer: dp_copy(mine, peer).start())
    if hops > 1:
        ring_hop(0, 2)

    loads[1].wait()
    img_lhs = with_shift(emb_c * (1.0 + scale_img), shift_img)
    img_m = mm(img_lhs, wimg_v[...])
    img_m2 = stacked(img_m[0:ch])
    img_shift = img_m[ch : ch + 1] + img_m[ch + 1 : ch + 2]
    low_m = mm_nt(img_lhs, adown_t[...])
    low_m2 = stacked(low_m[0:ch])
    low_shift = low_m[ch : ch + 1] + low_m[ch + 1 : ch + 2]
    up = aup[:, at_lanes(me * 128, 128)]
    gain_q = qg[...]
    gain_k = kg[...]
    score_scale = math.log2(math.e) / math.sqrt(128.0)
    vext[:, 128:256] = jnp.ones((vext.shape[0], 128), BF16)
    if hops > 2:
        ring_hop(0, 3)

    others(me, seqs, lambda peer: noisy_copy(peer, peer).wait_recv())

    def project(i):
        here = at_rows(i * block, block)
        pieces = []
        for j in range(4):
            packed = noisy[i * 4 + j]
            pieces += [packed[:, 0:ch], packed[:, ch:]]
        nb = jnp.concatenate(pieces, 0)
        nf = nb.astype(F32)
        nb = jnp.concatenate([nb, nb], 1)
        var = jnp.sum(mm(nb, gram) * nf, -1, keepdims=True) * (1.0 / width)
        inv = lax.rsqrt(var + epsilon)
        qkv = mm(nb, img_m2) * inv + img_shift
        low = (mm(nb, low_m2) * inv + low_shift).astype(BF16)
        delta = mm(low, up).astype(BF16).astype(F32)
        q = qkv[:, 0:128]
        k = qkv[:, 128:256]
        q_pol = q + delta
        q2[here, :] = (q * rms_rows(q) * (gain_q * score_scale)).astype(BF16)
        q2[at_rows(images + i * block, block), :] = (
            q_pol * rms_rows(q_pol) * (gain_q * score_scale)
        ).astype(BF16)
        pol[here, :] = q_pol
        kk[here, :] = (k * rms_rows(k) * gain_k).astype(BF16)
        vext[here, 0:128] = qkv[:, 256:384].astype(BF16)
        lhs[here, :] = jnp.concatenate([low, (nf * inv).astype(BF16)], 1)

    def spans(start, stop, body):
        @pl.loop(start, stop)
        def _(i):
            body(i)

    spans(0, blocks // 2, project)
    if hops > 3:
        ring_hop(0, 4)
    ring_first(1)
    spans(blocks // 2, blocks, project)
    ring_end(0)
    if origins > 1:
        for turn in range(2):
            for way in range(2):
                x_near(way, turn, mine).start()
    spread(0, 0)
    spread(0, 1)
    ring_hop(1, 1)

    def attend(here, keys):
        s = mm_nt(q2[here, :], kk[keys, :])
        return mm(jnp.exp2(s).astype(BF16), vext[keys, :])

    def image_keys(i):
        here = at_rows(i * block, block)
        oacc[here, :] = attend(here, pl.ds(0, images))

    spans(0, blocks // 2, image_keys)
    if hops > 1:
        ring_hop(1, 2)
    spans(blocks // 2, blocks, image_keys)
    if origins > 1:
        x_near(0, 0, places[1]).wait_recv()
        x_far(0, places[1]).start()
        spread(1, 0)
        x_near(1, 0, places[2]).wait_recv()
        x_far(1, places[2]).start()
        spread(2, 1)
    if hops > 2:
        ring_hop(1, 3)
    spans(blocks, 2 * blocks, image_keys)
    relay(0)
    if hops > 3:
        ring_hop(1, 4)
    if origins > 1:
        x_near(0, 1, places[1]).wait_recv()
        spread(1, 1)
        x_near(1, 1, places[2]).wait_recv()
        spread(2, 0)

    ring_end(1)
    loads[2].wait()
    text_n = (text[...].astype(F32) * (1.0 + scale_txt) + shift_txt).astype(BF16)
    kv = mm(text_n, wtxt_v[...])
    k = kv[:, 0:128]
    my_keys = at_rows(images + slot * texts, texts)
    kk[my_keys, :] = (k * rms_rows(k) * gain_k).astype(BF16)
    vext[my_keys, 0:128] = kv[:, 128:256].astype(BF16)

    def kv_copies(owner):
        keys = at_rows(images + owner * texts, texts)
        v = vext.at[keys, pl.ds(0, 128)]
        return (
            remote(kk.at[keys], kk.at[keys], kv_s.at[0], kv_r.at[0], {"pair": other}),
            remote(v, v, kv_s.at[1], kv_r.at[1], {"pair": other}),
        )

    for copy in kv_copies(slot):
        copy.start()
    for copy in kv_copies(other):
        copy.wait_recv()

    def out_copy(kind, owner, peer):
        return remote(
            outb.at[at_rows(kind * images + peer * rows, rows)],
            x.at[at_rows(kind * rows, rows), at_lanes(owner * 128, 128)],
            x_s.at[kind, peer],
            x_r.at[kind, owner],
            {"seq": peer},
        )

    def text_keys(i):
        kind = lax.div(i, blocks)
        b = lax.rem(i + lax.div(me, 4), blocks)
        here = at_rows(kind * images + b * block, block)
        o = oacc[here, :] + attend(here, pl.ds(images, 2 * texts))
        inv = 1.0 / o[:, 128:256]
        out = o[:, 0:128] * inv
        outb[here, :] = out.astype(BF16)

        @pl.when(kind == 1)
        def _():
            outf[at_rows(b * block, block), :] = out
            rl[at_rows(b * block, block), :] = inv

        for j in range(4):
            peer = b * 4 + j

            @pl.when(peer != me)
            def _():
                out_copy(kind, me, peer).start()

            @pl.when(peer == me)
            def _():
                x[at_rows(kind * rows, rows), at_lanes(me * 128, 128)] = outb[
                    at_rows(kind * images + me * rows, rows), :
                ]

    spans(0, 2 * blocks, text_keys)

    if origins > 1:
        x_far(0, places[3]).wait_recv()
        spread(3, 0)
        x_far(1, places[3]).wait_recv()
        spread(3, 1)
        relay(1)
        relay(2)

    def finish_dp(peer):
        dp_copy(mine, peer).wait_send()
        dp_copy(peer, peer).wait_recv()

    others(mine, dps, finish_dp)
    first = lax.broadcasted_iota(jnp.int32, (16, width), 0) == 0
    deep = ch + 16

    def build(p):
        shift = moddp[p, :, 0:width]
        scale = moddp[p, :, width:]
        extra = jnp.where(first, shift, 0.0)
        left[at_rows(p * deep, deep), :] = jnp.concatenate(
            [emb_c * (1.0 + scale), extra], 0
        ).astype(BF16)

    for p in range(dps):
        build(p)
    acc[...] = jnp.zeros_like(acc)
    csum[...] = jnp.zeros_like(csum)
    if origins > 1:
        relay(3)

    def finish_out(peer):
        for kind in range(2):
            out_copy(kind, peer, peer).wait_recv()

    others(me, seqs, finish_out)
    for which in range(origins):
        for side in range(2):
            c_copy(0, which, side, True).wait_recv()
            c_copy(1, which, side, True).wait_recv()

    tile = 256
    xv = x[...]

    def mix(i):
        here = at_lanes(i * tile, tile)
        states = mm(own, embed[:, here])
        w = wall[:, :, here].reshape(128 * seqs, tile)
        mixed[:, here] = mm(xv, w) + jnp.concatenate([states, states], 0)

    each(width // tile, mix)
    full = mixed[...]
    full = full - row_mean(full)
    inv = lax.rsqrt(row_mean(full * full) + epsilon)
    unit = full * inv
    mixed[...] = unit
    pred = mm_nt((unit * (1.0 + scale_out) + shift_out).astype(BF16), lw_t[...])
    diff = jnp.concatenate([target, target], 0) - pred
    squares = diff * diff
    gap = (jnp.sum(squares[rows:]) - jnp.sum(squares[:rows])) * (1.0 / (images * ch))
    gapbuf[slot * seqs + me] = jnp.full((8, 128), gap, F32)

    def gap_copy(to_slot, from_slot, owner, peer):
        return remote(
            gapbuf.at[slot * seqs + me],
            gapbuf.at[from_slot * seqs + owner],
            e_s.at[to_slot * seqs + peer],
            e_r.at[from_slot * seqs + owner],
            {"seq": peer, "pair": to_slot},
        )

    g_ln = mm(diff[rows:].astype(BF16), lw_t[...]) * (1.0 + scale_out)
    unit_p = mixed[rows:, :]
    gmix[...] = (
        (g_ln - row_mean(g_ln) - unit_p * row_mean(g_ln * unit_p)) * inv[rows:]
    ).astype(BF16)

    def g_copy(owner, peer):
        return remote(
            ghs.at[peer],
            gh.at[at_rows(owner * rows, rows)],
            g_s.at[peer],
            g_r.at[owner],
            {"seq": peer},
        )

    def heads_back(i):
        pair = lax.rem(i + lax.div(me, 2), seqs // 2)
        w = wall[pl.ds(2 * pair, 2)].reshape(256, width)
        g = mm_nt(gmix[...], w).astype(BF16)
        for j in range(2):
            peer = 2 * pair + j
            ghs[peer] = g[:, j * 128 : (j + 1) * 128]

            @pl.when(peer != me)
            def _():
                g_copy(me, peer).start()

            @pl.when(peer == me)
            def _():
                gh[at_rows(me * rows, rows), :] = ghs[me]

    each(seqs // 2, heads_back)

    def send_gap(peer):
        gap_copy(slot, slot, me, peer).start()
        gap_copy(other, slot, me, peer).start()

    others(me, seqs, send_gap)
    gap_copy(other, slot, me, me).start()
    keys = kk[...]
    vals = vext[:, 0:128]

    def back(i):
        b = lax.rem(i + lax.div(me, 4), blocks)
        for j in range(4):
            peer = b * 4 + j

            @pl.when(peer != me)
            def _():
                g_copy(peer, peer).wait_recv()

        here = at_rows(b * block, block)
        g = gh[here, :]
        p = jnp.exp2(mm_nt(q2[at_rows(images + b * block, block), :], keys))
        gp = mm_nt(g, vals)
        dsum = jnp.sum(g.astype(F32) * outf[here, :], -1, keepdims=True)
        gs = (p * (gp - dsum)).astype(BF16)
        gq = mm(gs, keys) * (rl[here, :] * (1.0 / math.sqrt(128.0)))
        u = pol[here, :]
        r = rms_rows(u)
        w = gq * gain_q
        gd = (r * w - u * (r * r * r) * row_mean(u * w)).astype(BF16)
        acc[...] += mm_tn(lhs[here, :], gd)
        csum[...] += jnp.broadcast_to(
            jnp.sum(gd.astype(F32), 0, keepdims=True), csum.shape
        )

    each(blocks, back)

    def wait_gap(peer):
        gap_copy(slot, slot, peer, peer).wait_recv()
        gap_copy(slot, other, peer, peer).wait_recv()

    others(me, seqs, wait_gap)
    gap_copy(slot, other, me, me).wait_recv()
    own_gap = jnp.sum(gapbuf[pl.ds(slot * seqs, seqs)], 0)
    other_gap = jnp.sum(gapbuf[pl.ds(other * seqs, seqs)], 0)
    sgn = (1.0 - 2.0 * pref[0].astype(F32)) * (1.0 - 2.0 * slot.astype(F32))
    z = half_beta * sgn * (own_gap - other_gap)
    value[...] = (jnp.maximum(z, 0.0) + jnp.log1p(jnp.exp(-jnp.abs(z))))[0:1, 0:1]
    weight = half_beta / dps / (1.0 + jnp.exp(-z))
    factor = (sgn * weight * (-2.0 / (images * ch)))[0:1, :]
    rank = up.shape[0]
    tail_rows = ua.shape[0] - rank
    ua[0:rank, :] = acc[0:rank, :] * factor
    a_top, a_rest = halves(jnp.concatenate([acc[rank : rank + ch, :], csum[...]], 0))
    tail = mm_nt(a_top, up) + mm_nt(a_rest, up)
    lower = jnp.concatenate([tail[0 : ch // 2], tail[ch // 2 : ch]], 1)
    lowest = jnp.concatenate([tail[ch:], tail[ch:]], 1)
    ua[rank:, :] = jnp.concatenate([lower, lowest], 0) * factor

    def to(r):
        return {"pair": lax.div(r, dps), "dp": lax.rem(r, dps)}

    def u_copy(owner, peer):
        return remote(
            ua.at[pl.ds(0, rank)], ubuf.at[owner], u_s.at[peer], u_r.at[owner], to(peer)
        )

    def a_copy(owner, peer):
        return remote(
            ua.at[pl.ds(rank, tail_rows)],
            abuf.at[owner],
            a_s.at[peer],
            a_r.at[owner],
            {"seq": peer},
        )

    def v_copy(owner, peer):
        return remote(
            usum,
            upb.at[:, at_lanes(owner * 128, 128)],
            v_s.at[peer],
            v_r.at[owner],
            {"seq": peer},
        )

    def b_copy(owner, peer):
        return remote(asum, a2.at[owner], b_s.at[peer], b_r.at[owner], to(peer))

    others(rep, reps, lambda peer: u_copy(rep, peer).start())
    others(me, seqs, lambda peer: a_copy(me, peer).start())
    ubuf[rep] = ua[0:rank, :]
    abuf[me] = ua[rank:, :]

    others(rep, reps, lambda peer: u_copy(peer, peer).wait_recv())
    sums = jnp.sum(ubuf[...], 0).astype(BF16)
    usum[...] = sums
    upb[:, at_lanes(me * 128, 128)] = sums
    others(me, seqs, lambda peer: v_copy(me, peer).start())
    others(me, seqs, lambda peer: a_copy(peer, peer).wait_recv())
    sums = jnp.sum(abuf[...], 0)
    asum[...] = sums
    a2[rep] = sums
    others(rep, reps, lambda peer: b_copy(rep, peer).start())

    def sent(peer):
        mod_copy(me, peer).wait_send()
        noisy_copy(me, peer).wait_send()
        for kind in range(2):
            out_copy(kind, me, peer).wait_send()
        gap_copy(slot, slot, me, peer).wait_send()
        gap_copy(other, slot, me, peer).wait_send()
        g_copy(me, peer).wait_send()
        a_copy(me, peer).wait_send()

    others(me, seqs, sent)
    gap_copy(other, slot, me, me).wait_send()
    for kind in range(2):
        ring_sent(kind)
    for copy in kv_copies(slot):
        copy.wait_send()
    if origins > 1:
        for way in range(2):
            for turn in range(2):
                x_near(way, turn, mine).wait_send()
            x_far(way, mine).wait_send()
    for which in range(origins):
        for side in range(2):
            y_copy(which, side, slot).wait_send()
            c_copy(0, which, side, False).wait_send()
            c_copy(1, which, side, False).wait_send()

    others(rep, reps, lambda peer: b_copy(peer, peer).wait_recv())
    for p in range(dps):
        a = a2[p] + a2[dps + p]
        top = a[0 : ch // 2]
        low_rows = a[ch // 2 :, 0:ch]
        right[p * deep : (p + 1) * deep, :] = jnp.concatenate(
            [top[:, 0:ch], top[:, ch:], low_rows, low_rows], 0
        ).astype(BF16)
    down[...] = mm_tn(right[...], left[...]).astype(BF16)

    def last_sent(peer):
        v_copy(me, peer).wait_send()
        v_copy(peer, peer).wait_recv()

    others(me, seqs, last_sent)

    def last_reps(peer):
        u_copy(rep, peer).wait_send()
        b_copy(rep, peer).wait_send()

    others(rep, reps, last_reps)


def shape(dims, kind):
    return jax.ShapeDtypeStruct(dims, kind)


def on_device(
    latents,
    noise,
    pair_timestep_index,
    preferred_image_slot,
    prompt_token_states,
    image_embed_weight,
    timestep_modulation_weight,
    image_query_key_value,
    text_key_value,
    query_norm_gain,
    key_norm_gain,
    adapter_down_weight,
    adapter_up_weight,
    image_output_weight,
    latent_out_weight,
):
    seqs = lax.axis_size("seq")
    dps = lax.axis_size("dp")
    rows, ch = latents.shape[2:]
    images = rows * seqs
    width = image_embed_weight.shape[1]
    texts = prompt_token_states.shape[1] * seqs
    keys = images + texts
    rank = adapter_down_weight.shape[1]
    step_value = pair_timestep_index[0].astype(jnp.float32)
    emb = sinusoid(step_value, timestep_modulation_weight.shape[0]).astype(BF16)[None]
    V, S, A = pltpu.VMEM, pltpu.SMEM, pl.ANY
    DMA = pltpu.SemaphoreType.DMA
    heads = 128 * seqs
    tail = ch // 2 + 8
    deep = ch + 16
    reps = 2 * dps
    scratch = [
        V((width, 384), BF16),
        V((width, 256), BF16),
        V((1, 6 * width), F32),
        V((dps, 1, 2 * width), F32),
        V((seqs, rows // 2, 128), BF16),
        V((texts // 2, width), BF16),
        V((2 * images, 256), F32),
        V((2 * images, 128), BF16),
        V((2 * images, 128), BF16),
        V((1, timestep_modulation_weight.shape[1]), F32),
        V((2 * rows, heads), BF16),
        V((seqs, 128, width), BF16),
        V((keys, 128), BF16),
        V((keys, 256), BF16),
        V((images, 128), F32),
        V((images, 128), BF16),
        V((images, 128), F32),
        V((images, 128), F32),
        V((2 * rows, width), F32),
        V((rows, width), BF16),
        V((images, 128), BF16),
        V((seqs, rows, 128), BF16),
        V((2 * seqs, 8, 128), F32),
        V((rank + ch, 128), F32),
        V((8, 128), F32),
        V((rank + tail, 128), F32),
        V((reps, rank, 128), F32),
        V((seqs, tail, 128), F32),
        V((reps, tail, 128), F32),
        V((rank, 128), BF16),
        V((tail, 128), F32),
        V((dps * deep, width), BF16),
        V((dps * deep, ch), BF16),
    ]
    one = DMA((seqs,))
    ring = [DMA((3 * seqs,)), one]
    scratch += [DMA((3,))] + [one] * 4 + ring + [DMA((dps,))] * 2 + [DMA((2,))] * 2
    scratch += [DMA((2, seqs))] * 2 + [one] * 2 + [DMA((2 * seqs,))] * 2 + ring
    scratch += [DMA((6,))] * 2 + [DMA((8,))] * 2 + [DMA((16,))] * 2
    scratch += [DMA((reps,))] * 2 + [one] * 4 + [DMA((reps,))] * 2
    down_t, up, value = pl.pallas_call(
        functools.partial(main_kernel, seqs, dps),
        out_shape=[shape((ch, width), BF16), shape((rank, heads), BF16), shape((1, 1), F32)],
        in_specs=[
            pl.BlockSpec(memory_space=m)
            for m in [S, S, V, V, V, V, V, V, A, A, V, V, V, V, A, V]
        ],
        out_specs=[pl.BlockSpec(memory_space=V)] * 3,
        scratch_shapes=scratch,
        compiler_params=pltpu.CompilerParams(
            collective_id=0, has_side_effects=True, vmem_limit_bytes=VMEM_BYTES
        ),
    )(
        pair_timestep_index,
        preferred_image_slot,
        emb,
        latents[0, 0].T,
        noise[0].T,
        prompt_token_states[0],
        image_embed_weight,
        timestep_modulation_weight,
        image_query_key_value.reshape(width, -1),
        text_key_value.reshape(width, -1),
        query_norm_gain.reshape(1, -1),
        key_norm_gain.reshape(1, -1),
        adapter_down_weight.T,
        adapter_up_weight,
        image_output_weight,
        latent_out_weight.T,
    )
    return (down_t.T.astype(F32), up.astype(F32), value.reshape(1))


def solution(mesh):
    return jax.shard_map(
        on_device,
        mesh=mesh,
        in_specs=(
            P("dp", "pair", "seq", None),
            P("dp", "seq", None),
            P("dp"),
            P("dp"),
            P("dp", "seq", None),
            P(),
            P(None, "seq"),
            P(None, "seq", None),
            P(None, "seq", None),
            P(),
            P(),
            P(),
            P(),
            P("seq", None),
            P(),
        ),
        out_specs=(P(), P(), P("dp")),
        check_vma=False,
    )
```

```python
import functools
import math

import jax
import jax.numpy as jnp
from jax import lax
from jax.experimental import pallas as pl
from jax.experimental.pallas import tpu as pltpu
from jax.sharding import PartitionSpec as P

epsilon = 1e-06
half_beta = 20.0
horizon = 1000.0
F32 = jnp.float32
BF16 = jnp.bfloat16
VMEM_BYTES = 58 * 1024 * 1024


def sinusoid(step_value, width):
    half_width = width // 2
    freqs = jnp.exp(-math.log(10000.0) * jnp.arange(half_width, dtype=jnp.float32) / half_width)
    angle = step_value * freqs
    return jnp.concatenate([jnp.cos(angle), jnp.sin(angle)])


def mm(a, b):
    return lax.dot_general(a, b, (((1,), (0,)), ((), ())), preferred_element_type=F32)


def mm_nt(a, b):
    return lax.dot_general(a, b, (((1,), (1,)), ((), ())), preferred_element_type=F32)


def mm_tn(a, b):
    return lax.dot_general(a, b, (((0,), (0,)), ((), ())), preferred_element_type=F32)


def halves(a):
    top = a.astype(BF16)
    return top, (a - top.astype(F32)).astype(BF16)


def stacked(a):
    top, rest = halves(a)
    return jnp.concatenate([top, rest], 0)


def row_mean(a):
    return jnp.mean(a, -1, keepdims=True)


def rms_rows(rows):
    return lax.rsqrt(row_mean(rows * rows) + epsilon)


def remote(src, dst, send, recv, device):
    return pltpu.make_async_remote_copy(
        src_ref=src,
        dst_ref=dst,
        send_sem=send,
        recv_sem=recv,
        device_id=device,
        device_id_type=pl.DeviceIdType.MESH,
    )


def each(count, body):
    @pl.loop(0, count)
    def _(i):
        body(i)


def others(me, count, body):
    @pl.loop(1, count)
    def _(step):
        body(lax.rem(me + step, count))


def arrived(ref, sem, device):
    remote(ref, ref, sem, sem, device).wait_recv()


def gone(ref, sem, device):
    remote(ref, ref, sem, sem, device).wait_send()


def at_rows(start, size):
    return pl.ds(pl.multiple_of(start, 16), size)


def at_lanes(start, size):
    return pl.ds(pl.multiple_of(start, 128), size)


def with_shift(scaled, shift):
    width = shift.shape[1]
    top, rest = halves(shift)
    which = lax.broadcasted_iota(jnp.int32, (16, width), 0)
    extra = jnp.where(
        which == 0,
        top.astype(F32),
        jnp.where(which == 1, rest.astype(F32), 0.0),
    )
    return jnp.concatenate([scaled, extra], 0).astype(BF16)


def main_kernel(
    seqs, dps, step, pref, emb, lat_t, noi_t, txt, embed, wmod, wimg, wtxt, qg, kg, adown_t, aup, wo, lw_t,
    down, upb, value,
    wimg_v, wtxt_v, adown_v, up_v, lw_v, mod, moddp, noisy, text, oacc, q2, outb, modrow, x, wall, kk, vext, pol, lhs, outf, rl,
    mixed, gmix, gh, ghs, gapbuf, acc, csum, ua, ubuf, abuf, a2, usum, asum, left, right,
    in_s, mod_s, mod_r, noi_s, noi_r, txt_s, txt_r, dp_s, dp_r, kv_s, kv_r, x_s, x_r,
    g_s, g_r, e_s, e_r, wz_s, wz_r, wx_s, wx_r, wy_s, wy_r, wc_s, wc_r,
    u_s, u_r, a_s, a_r, v_s, v_r, b_s, b_r,
):
    me = lax.axis_index("seq")
    slot = lax.axis_index("pair")
    mine = lax.axis_index("dp")
    other = 1 - slot
    ch, rows = lat_t.shape
    images = rows * seqs
    width = embed.shape[1]
    span = width // 2
    strip = 128 // dps
    origins = dps // 2
    half = txt.shape[0] // 2
    texts = half * seqs
    block = 4 * rows
    blocks = images // block
    part = wmod.shape[1]
    zs = seqs // 2
    z_at, hi = lax.rem(me, zs), lax.div(me, zs)
    flip = lax.rem(me + zs, seqs)
    reps = 2 * dps
    rep = slot * dps + mine

    loads = [
        pltpu.make_async_copy(
            wo.at[at_rows(mine * strip, strip), at_lanes(slot * span, span)],
            wall.at[me, at_rows(mine * strip, strip), at_lanes(slot * span, span)],
            in_s.at[0],
        ),
        pltpu.make_async_copy(wimg, wimg_v, in_s.at[1]),
        pltpu.make_async_copy(wtxt, wtxt_v, in_s.at[2]),
        pltpu.make_async_copy(adown_t, adown_v, in_s.at[3]),
        pltpu.make_async_copy(aup.at[:, at_lanes(me * 128, 128)], up_v, in_s.at[4]),
        pltpu.make_async_copy(lw_t, lw_v, in_s.at[5]),
    ]
    for load in loads:
        load.start()
    barrier = pltpu.get_barrier_semaphore()

    def at(seq=me, pair=slot, dp=mine):
        return {"pair": pair, "seq": seq, "dp": dp}

    def greet(device):
        pl.semaphore_signal(
            barrier, inc=1, device_id=device, device_id_type=pl.DeviceIdType.MESH
        )

    others(me, seqs, lambda peer: greet(at(seq=peer)))
    others(mine, dps, lambda peer: greet(at(dp=peer)))
    each(dps, lambda peer: greet(at(pair=other, dp=peer)))
    greet(at(seq=flip, pair=other))
    total = (seqs - 1) + (dps - 1) + dps + 1

    mod_part = mm(jnp.broadcast_to(emb[...].astype(F32), (16, emb.shape[1])).astype(BF16), wmod[...])[0:1]
    modrow[...] = mod_part
    lev = (step[0].astype(F32) + 1.0) * (1.0 / horizon)
    lat_f = lat_t[...].astype(F32)
    noi_f = noi_t[...].astype(F32)
    own = ((1.0 - lev) * lat_f + lev * noi_f).T.astype(BF16)
    target = (noi_f - lat_f).T
    noisy[me] = jnp.concatenate([own[0 : rows // 2], own[rows // 2 :]], 1)
    t = txt[at_rows(slot * half, half), :].astype(F32)
    t = t - row_mean(t)
    text[at_rows(me * half, half), :] = (t * lax.rsqrt(row_mean(t * t) + epsilon)).astype(BF16)
    emb_c = embed[...].astype(F32)
    emb_c = emb_c - row_mean(emb_c)
    e_top, e_rest = halves(emb_c)
    gram = stacked(mm_nt(e_top, e_top) + mm_nt(e_top, e_rest) + mm_nt(e_rest, e_top))
    vext[:, 128:256] = jnp.ones((vext.shape[0], 128), BF16)
    acc[...] = jnp.zeros_like(acc)
    csum[...] = jnp.zeros_like(csum)
    loads[0].wait()
    pl.semaphore_wait(barrier, total)

    def mod_copy(owner, peer):
        return remote(
            modrow,
            mod.at[:, at_lanes(owner * part, part)],
            mod_s.at[0],
            mod_r.at[0],
            at(seq=peer),
        )

    def noisy_copy(owner, peer):
        where = noisy.at[owner]
        return remote(where, where, noi_s.at[0], noi_r.at[0], at(seq=peer))

    def dp_copy(owner, peer):
        return remote(
            mod.at[:, pl.ds(0, 2 * width)],
            moddp.at[owner],
            dp_s.at[0],
            dp_r.at[0],
            at(dp=peer),
        )

    def region(first, count, p, s):
        return wall.at[pl.ds(first, count), at_rows(p * strip, strip), at_lanes(s * span, span)]

    def owner_at(h, away):
        return h * zs + lax.rem(z_at + away + zs, zs)

    right_z, left_z = owner_at(hi, 1), owner_at(hi, -1)

    def ring_copy(kind, lane, owner, to):
        if kind == 0:
            where, send, recv = region(owner, 1, mine, slot), wz_s, wz_r
        else:
            where, send, recv = text.at[at_rows(owner * half, half)], txt_s, txt_r
        return remote(where, where, send.at[lane * seqs + owner], recv.at[owner], at(seq=to))

    def ring_sends(kind, hop):
        last = hop == zs // 2
        sends = []
        for h in range(2):
            if not last or h == 0:
                sends.append(ring_copy(kind, 1, owner_at(h, 1 - hop), right_z))
            if not last or h == 1:
                sends.append(ring_copy(kind, 2, owner_at(h, hop - 1), left_z))
        return sends

    def ring_first(kind):
        ring_copy(kind, 0, me, flip).start()
        if zs > 2:
            ring_copy(kind, 1, me, right_z).start()
            ring_copy(kind, 2, me, left_z).start()

    def ring_hop(kind, hop):
        if hop == 1:
            ring_copy(kind, 0, flip, flip).wait_recv()
            if zs > 2:
                ring_copy(kind, 1, flip, right_z).start()
                ring_copy(kind, 2, flip, left_z).start()
                return
        else:
            for h in range(2):
                ring_copy(kind, 0, owner_at(h, 1 - hop), flip).wait_recv()
                ring_copy(kind, 0, owner_at(h, hop - 1), flip).wait_recv()
        for copy in ring_sends(kind, hop):
            copy.start()

    def ring_end(kind):
        ring_copy(kind, 0, owner_at(0, zs // 2), flip).wait_recv()
        ring_copy(kind, 0, owner_at(1, zs // 2), flip).wait_recv()

    def ring_sent(kind):
        ring_copy(kind, 0, me, flip).wait_send()
        for hop in range(1, zs // 2 + 1):
            for copy in ring_sends(kind, hop):
                copy.wait_send()

    hops = zs // 2

    def along(away):
        return lax.rem(mine + 2 * away + dps, dps)

    places = [mine, along(-1), along(1), along(2)]
    sibling = mine + 1 - 2 * lax.rem(mine, 2)

    def chunk(origin, which_half, s):
        return region(which_half * (seqs // 2), seqs // 2, origin, s)

    def x_near(way, turn, origin):
        where = chunk(origin, turn if way == 0 else 1 - turn, slot)
        n = way * 2 + turn
        return remote(where, where, wx_s.at[n], wx_r.at[n], at(dp=along(1 - 2 * way)))

    def x_far(way, origin):
        where = chunk(origin, way, slot)
        return remote(where, where, wx_s.at[4 + way], wx_r.at[4 + way], at(dp=along(1 - 2 * way)))

    def y_copy(which, side, s):
        where = chunk(places[which], side, s)
        to = me if side == 0 else flip
        n = which * 2 + side
        return remote(where, where, wy_s.at[n], wy_r.at[n], at(pair=other, seq=to))

    def c_copy(foreign, which, side, at_sibling):
        origin = places[which]
        if at_sibling:
            origin = sibling - mine + origin
        where = chunk(origin, side, other if foreign else slot)
        n = (foreign * 4 + which) * 2 + side
        return remote(where, where, wc_s.at[n], wc_r.at[n], at(dp=sibling))

    def spread(which, side):
        y_copy(which, side, slot).start()
        c_copy(0, which, side, False).start()

    def relay(which):
        for side in range(2):
            y_copy(which, side, other).wait_recv()
            c_copy(1, which, side, False).start()

    def send_small(peer):
        mod_copy(me, peer).start()
        noisy_copy(me, peer).start()

    others(me, seqs, send_small)
    ring_first(0)
    mod[:, at_lanes(me * part, part)] = mod_part
    ring_hop(0, 1)
    ring_first(1)

    mod_others = mod.at[:, pl.ds(0, (seqs - 1) * part)]
    arrived(mod_others, mod_r.at[0], at(seq=flip))
    shift_img, scale_img, shift_txt, scale_txt, shift_out, scale_out = [
        mod[:, i * width : (i + 1) * width] for i in range(6)
    ]
    moddp[mine] = mod[:, 0 : 2 * width]
    others(mine, dps, lambda peer: dp_copy(mine, peer).start())
    if hops > 1:
        ring_hop(0, 2)

    loads[1].wait()
    loads[3].wait()
    loads[4].wait()
    img_lhs = with_shift(emb_c * (1.0 + scale_img), shift_img)
    img_m = mm(img_lhs, wimg_v[...])
    img_m2 = stacked(img_m[0:ch])
    img_shift = img_m[ch : ch + 1] + img_m[ch + 1 : ch + 2]
    low_m = mm_nt(img_lhs, adown_v[...])
    low_m2 = stacked(low_m[0:ch])
    low_shift = low_m[ch : ch + 1] + low_m[ch + 1 : ch + 2]
    up = up_v[...]
    gain_q = qg[...]
    gain_k = kg[...]
    score_scale = math.log2(math.e) / math.sqrt(128.0)
    if hops > 2:
        ring_hop(0, 3)

    noisy_others = noisy.at[pl.ds(0, seqs - 1)]
    arrived(noisy_others, noi_r.at[0], at(seq=flip))

    def project(i):
        here = at_rows(i * block, block)
        pieces = []
        for j in range(4):
            packed = noisy[i * 4 + j]
            pieces += [packed[:, 0:ch], packed[:, ch:]]
        nb = jnp.concatenate(pieces, 0)
        nf = nb.astype(F32)
        nb = jnp.concatenate([nb, nb], 1)
        var = jnp.sum(mm(nb, gram) * nf, -1, keepdims=True) * (1.0 / width)
        inv = lax.rsqrt(var + epsilon)
        qkv = mm(nb, img_m2) * inv + img_shift
        low = (mm(nb, low_m2) * inv + low_shift).astype(BF16)
        delta = mm(low, up).astype(BF16).astype(F32)
        q = qkv[:, 0:128]
        k = qkv[:, 128:256]
        q_pol = q + delta
        q2[here, :] = (q * rms_rows(q) * (gain_q * score_scale)).astype(BF16)
        q2[at_rows(images + i * block, block), :] = (
            q_pol * rms_rows(q_pol) * (gain_q * score_scale)
        ).astype(BF16)
        pol[here, :] = q_pol
        kk[here, :] = (k * rms_rows(k) * gain_k).astype(BF16)
        vext[here, 0:128] = qkv[:, 256:384].astype(BF16)
        lhs[here, :] = jnp.concatenate([low, (nf * inv).astype(BF16)], 1)

    def spans(start, stop, body):
        @pl.loop(start, stop)
        def _(i):
            body(i)

    spans(0, blocks // 2, project)
    if hops > 3:
        ring_hop(0, 4)
    ring_hop(1, 1)
    spans(blocks // 2, blocks, project)
    ring_end(0)
    if origins > 1:
        for turn in range(2):
            for way in range(2):
                x_near(way, turn, mine).start()
    spread(0, 0)
    spread(0, 1)
    if hops > 1:
        ring_hop(1, 2)

    def attend(here, keys):
        s = mm_nt(q2[here, :], kk[keys, :])
        return mm(jnp.exp2(s).astype(BF16), vext[keys, :])

    def image_keys(i):
        here = at_rows(i * block, block)
        oacc[here, :] = attend(here, pl.ds(0, images))

    spans(0, blocks, image_keys)
    if hops > 2:
        ring_hop(1, 3)
    if origins > 1:
        x_near(0, 0, places[1]).wait_recv()
        x_far(0, places[1]).start()
        spread(1, 0)
        x_near(1, 0, places[2]).wait_recv()
        x_far(1, places[2]).start()
        spread(2, 1)
    spans(blocks, 2 * blocks, image_keys)
    if hops > 3:
        ring_hop(1, 4)
    relay(0)
    if origins > 1:
        x_near(0, 1, places[1]).wait_recv()
        spread(1, 1)
        x_near(1, 1, places[2]).wait_recv()
        spread(2, 0)

    ring_end(1)
    loads[2].wait()
    text_n = (text[...].astype(F32) * (1.0 + scale_txt) + shift_txt).astype(BF16)
    kv = mm(text_n, wtxt_v[...])
    k = kv[:, 0:128]
    my_keys = at_rows(images + slot * texts, texts)
    kk[my_keys, :] = (k * rms_rows(k) * gain_k).astype(BF16)
    vext[my_keys, 0:128] = kv[:, 128:256].astype(BF16)

    def kv_copies(owner):
        keys = at_rows(images + owner * texts, texts)
        v = vext.at[keys, pl.ds(0, 128)]
        return (
            remote(kk.at[keys], kk.at[keys], kv_s.at[0], kv_r.at[0], at(pair=other)),
            remote(v, v, kv_s.at[1], kv_r.at[1], at(pair=other)),
        )

    for copy in kv_copies(slot):
        copy.start()

    def own_text(i):
        here = at_rows(i * block, block)
        oacc[here, :] += attend(here, my_keys)

    spans(0, blocks, own_text)
    for copy in kv_copies(other):
        copy.wait_recv()

    def out_copy(kind, owner, peer):
        return remote(
            outb.at[at_rows(kind * images + peer * rows, rows)],
            x.at[at_rows(kind * rows, rows), at_lanes(owner * 128, 128)],
            x_s.at[kind],
            x_r.at[kind],
            at(seq=peer),
        )

    def text_keys(kind, i):
        b = lax.rem(i + lax.div(me, 4), blocks)
        here = at_rows(kind * images + b * block, block)
        left_keys = at_rows(images + other * texts, texts) if kind == 0 else pl.ds(images, 2 * texts)
        o = oacc[here, :] + attend(here, left_keys)
        inv = 1.0 / o[:, 128:256]
        out = o[:, 0:128] * inv
        outb[here, :] = out.astype(BF16)

        if kind == 1:
            outf[at_rows(b * block, block), :] = out
            rl[at_rows(b * block, block), :] = inv

        for j in range(4):
            peer = b * 4 + j

            @pl.when(peer != me)
            def _():
                out_copy(kind, me, peer).start()

            @pl.when(peer == me)
            def _():
                x[at_rows(kind * rows, rows), at_lanes(me * 128, 128)] = outb[
                    at_rows(kind * images + me * rows, rows), :
                ]

    for kind in range(2):
        spans(0, blocks, functools.partial(text_keys, kind))

    if origins > 1:
        x_far(0, places[3]).wait_recv()
        spread(3, 0)
        x_far(1, places[3]).wait_recv()
        spread(3, 1)
        relay(1)
        relay(2)

    moddp_others = moddp.at[pl.ds(0, dps - 1)]
    arrived(moddp_others, dp_r.at[0], at(dp=sibling))
    first = lax.broadcasted_iota(jnp.int32, (16, width), 0) == 0
    deep = ch + 16

    def build(p):
        shift = moddp[p, :, 0:width]
        scale = moddp[p, :, width:]
        extra = jnp.where(first, shift, 0.0)
        left[at_rows(p * deep, deep), :] = jnp.concatenate(
            [emb_c * (1.0 + scale), extra], 0
        ).astype(BF16)

    for p in range(dps):
        build(p)
    if origins > 1:
        relay(3)

    out_others = [
        x.at[pl.ds(kind * rows, rows), pl.ds(0, 128 * (seqs - 1))] for kind in range(2)
    ]
    for kind in range(2):
        arrived(out_others[kind], x_r.at[kind], at(seq=flip))

    loads[5].wait()
    tile = 256 if span % 256 == 0 else 128
    xv = x[...]

    def mix(i, first_lane):
        here = at_lanes(first_lane + i * tile, tile)
        states = mm(own, embed[:, here])
        w = wall[:, :, here].reshape(128 * seqs, tile)
        mixed[:, here] = mm(xv, w) + jnp.concatenate([states, states], 0)

    for foreign in range(2):
        for which in range(origins):
            for side in range(2):
                c_copy(foreign, which, side, True).wait_recv()
        first_lane = (other if foreign else slot) * span
        each(span // tile, lambda i: mix(i, first_lane))
    full = mixed[...]
    full = full - row_mean(full)
    inv = lax.rsqrt(row_mean(full * full) + epsilon)
    unit = full * inv
    mixed[...] = unit
    pred = mm_nt((unit * (1.0 + scale_out) + shift_out).astype(BF16), lw_v[...])
    diff = jnp.concatenate([target, target], 0) - pred
    squares = diff * diff
    gap = (jnp.sum(squares[rows:]) - jnp.sum(squares[:rows])) * (1.0 / (images * ch))
    gapbuf[me] = jnp.full((8, 128), gap, F32)

    def gap_copy(owner, peer):
        return remote(
            gapbuf.at[owner], gapbuf.at[owner], e_s.at[0], e_r.at[0], at(seq=peer)
        )

    g_ln = mm(diff[rows:].astype(BF16), lw_v[...]) * (1.0 + scale_out)
    unit_p = mixed[rows:, :]
    gmix[...] = (
        (g_ln - row_mean(g_ln) - unit_p * row_mean(g_ln * unit_p)) * inv[rows:]
    ).astype(BF16)

    def g_copy(owner, peer):
        return remote(
            ghs.at[peer],
            gh.at[at_rows(owner * rows, rows)],
            g_s.at[0],
            g_r.at[lax.div(owner, 4)],
            at(seq=peer),
        )

    def heads_back(i):
        pair = lax.rem(i + lax.div(me, 2), seqs // 2)
        w = wall[pl.ds(2 * pair, 2)].reshape(256, width)
        g = mm_nt(gmix[...], w).astype(BF16)
        for j in range(2):
            peer = 2 * pair + j
            ghs[peer] = g[:, j * 128 : (j + 1) * 128]

            @pl.when(peer != me)
            def _():
                g_copy(me, peer).start()

            @pl.when(peer == me)
            def _():
                gh[at_rows(me * rows, rows), :] = ghs[me]

    each(seqs // 2, heads_back)

    others(me, seqs, lambda peer: gap_copy(me, peer).start())
    keys = kk[...]
    vals = vext[:, 0:128]

    def back(i):
        b = lax.rem(i + lax.div(me, 4), blocks)
        here = at_rows(b * block, block)

        @pl.when(i == 0)
        def _():
            arrived(gh.at[pl.ds(0, 3 * rows)], g_r.at[b], at(seq=flip))

        @pl.when(i != 0)
        def _():
            arrived(gh.at[pl.ds(0, 4 * rows)], g_r.at[b], at(seq=flip))

        g = gh[here, :]
        p = jnp.exp2(mm_nt(q2[at_rows(images + b * block, block), :], keys))
        gp = mm_nt(g, vals)
        dsum = jnp.sum(g.astype(F32) * outf[here, :], -1, keepdims=True)
        gs = (p * (gp - dsum)).astype(BF16)
        gq = mm(gs, keys) * (rl[here, :] * (1.0 / math.sqrt(128.0)))
        u = pol[here, :]
        r = rms_rows(u)
        w = gq * gain_q
        gd = (r * w - u * (r * r * r) * row_mean(u * w)).astype(BF16)
        acc[...] += mm_tn(lhs[here, :], gd)
        csum[...] += jnp.broadcast_to(
            jnp.sum(gd.astype(F32), 0, keepdims=True), csum.shape
        )

    gap_others = gapbuf.at[pl.ds(0, seqs - 1)]
    pair_copy = remote(
        gapbuf.at[seqs], gapbuf.at[seqs + 1], e_s.at[1], e_r.at[1], at(pair=other)
    )
    spans(0, blocks // 2, back)
    arrived(gap_others, e_r.at[0], at(seq=flip))
    own_gap = jnp.sum(gapbuf[0:seqs], 0)
    gapbuf[seqs] = own_gap
    pair_copy.start()
    spans(blocks // 2, blocks, back)
    pair_copy.wait_recv()
    other_gap = gapbuf[seqs + 1]
    sgn = (1.0 - 2.0 * pref[0].astype(F32)) * (1.0 - 2.0 * slot.astype(F32))
    z = half_beta * sgn * (own_gap - other_gap)
    value[...] = (jnp.maximum(z, 0.0) + jnp.log1p(jnp.exp(-jnp.abs(z))))[0:1, 0:1]
    weight = half_beta / dps / (1.0 + jnp.exp(-z))
    factor = (sgn * weight * (-2.0 / (images * ch)))[0:1, :]
    rank = up.shape[0]
    tail_rows = ua.shape[0] - rank
    ua[0:rank, :] = acc[0:rank, :] * factor
    a_top, a_rest = halves(jnp.concatenate([acc[rank : rank + ch, :], csum[...]], 0))
    tail = mm_nt(a_top, up) + mm_nt(a_rest, up)
    lower = jnp.concatenate([tail[0 : ch // 2], tail[ch // 2 : ch]], 1)
    lowest = jnp.concatenate([tail[ch:], tail[ch:]], 1)
    ua[rank:, :] = jnp.concatenate([lower, lowest], 0) * factor

    def to(r):
        return at(pair=lax.div(r, dps), dp=lax.rem(r, dps))

    def u_copy(owner, peer):
        return remote(
            ua.at[pl.ds(0, rank)], ubuf.at[owner], u_s.at[0], u_r.at[0], to(peer)
        )

    def a_copy(owner, peer):
        return remote(
            ua.at[pl.ds(rank, tail_rows)],
            abuf.at[owner],
            a_s.at[0],
            a_r.at[0],
            at(seq=peer),
        )

    def v_copy(owner, peer):
        return remote(
            usum,
            upb.at[:, at_lanes(owner * 128, 128)],
            v_s.at[0],
            v_r.at[0],
            at(seq=peer),
        )

    def b_copy(owner, peer):
        return remote(asum, a2.at[owner], b_s.at[0], b_r.at[0], to(peer))

    others(me, seqs, lambda peer: a_copy(me, peer).start())
    others(rep, reps, lambda peer: u_copy(rep, peer).start())
    ubuf[rep] = ua[0:rank, :]
    abuf[me] = ua[rank:, :]

    u_others, a_others = ubuf.at[pl.ds(0, reps - 1)], abuf.at[pl.ds(0, seqs - 1)]
    arrived(u_others, u_r.at[0], at(dp=sibling))
    sums = jnp.sum(ubuf[...], 0).astype(BF16)
    usum[...] = sums
    upb[:, at_lanes(me * 128, 128)] = sums
    others(me, seqs, lambda peer: v_copy(me, peer).start())
    arrived(a_others, a_r.at[0], at(seq=flip))
    sums = jnp.sum(abuf[...], 0)
    asum[...] = sums
    a2[rep] = sums
    others(rep, reps, lambda peer: b_copy(rep, peer).start())

    near = at(seq=flip)
    gone(mod_others, mod_s.at[0], near)
    gone(noisy_others, noi_s.at[0], near)
    gone(moddp_others, dp_s.at[0], near)
    for kind in range(2):
        gone(out_others[kind], x_s.at[kind], near)
    gone(gh.at[pl.ds(0, (seqs - 1) * rows)], g_s.at[0], near)
    gone(gap_others, e_s.at[0], near)
    pair_copy.wait_send()
    gone(a_others, a_s.at[0], near)
    for kind in range(2):
        ring_sent(kind)
    for copy in kv_copies(slot):
        copy.wait_send()
    if origins > 1:
        for way in range(2):
            for turn in range(2):
                x_near(way, turn, mine).wait_send()
            x_far(way, mine).wait_send()
    for which in range(origins):
        for side in range(2):
            y_copy(which, side, slot).wait_send()
            c_copy(0, which, side, False).wait_send()
            c_copy(1, which, side, False).wait_send()

    b_others = a2.at[pl.ds(0, reps - 1)]
    arrived(b_others, b_r.at[0], near)
    for p in range(dps):
        a = a2[p] + a2[dps + p]
        top = a[0 : ch // 2]
        low_rows = a[ch // 2 :, 0:ch]
        right[p * deep : (p + 1) * deep, :] = jnp.concatenate(
            [top[:, 0:ch], top[:, ch:], low_rows, low_rows], 0
        ).astype(BF16)
    down[...] = mm_tn(right[...], left[...]).astype(BF16)

    v_others = upb.at[:, pl.ds(0, 128 * (seqs - 1))]
    gone(v_others, v_s.at[0], near)
    arrived(v_others, v_r.at[0], near)
    gone(u_others, u_s.at[0], near)
    gone(b_others, b_s.at[0], near)


def shape(dims, kind):
    return jax.ShapeDtypeStruct(dims, kind)


def on_device(
    latents,
    noise,
    pair_timestep_index,
    preferred_image_slot,
    prompt_token_states,
    image_embed_weight,
    timestep_modulation_weight,
    image_query_key_value,
    text_key_value,
    query_norm_gain,
    key_norm_gain,
    adapter_down_weight,
    adapter_up_weight,
    image_output_weight,
    latent_out_weight,
):
    seqs = lax.axis_size("seq")
    dps = lax.axis_size("dp")
    rows, ch = latents.shape[2:]
    images = rows * seqs
    width = image_embed_weight.shape[1]
    texts = prompt_token_states.shape[1] * seqs
    keys = images + texts
    rank = adapter_down_weight.shape[1]
    step_value = pair_timestep_index[0].astype(jnp.float32)
    emb = sinusoid(step_value, timestep_modulation_weight.shape[0]).astype(BF16)[None]
    V, S, A = pltpu.VMEM, pltpu.SMEM, pl.ANY
    DMA = pltpu.SemaphoreType.DMA
    heads = 128 * seqs
    tail = ch // 2 + 8
    deep = ch + 16
    reps = 2 * dps
    scratch = [
        V((width, 384), BF16),
        V((width, 256), BF16),
        V((rank, width), BF16),
        V((rank, 128), BF16),
        V((ch, width), BF16),
        V((1, 6 * width), F32),
        V((dps, 1, 2 * width), F32),
        V((seqs, rows // 2, 128), BF16),
        V((texts // 2, width), BF16),
        V((2 * images, 256), F32),
        V((2 * images, 128), BF16),
        V((2 * images, 128), BF16),
        V((1, timestep_modulation_weight.shape[1]), F32),
        V((2 * rows, heads), BF16),
        V((seqs, 128, width), BF16),
        V((keys, 128), BF16),
        V((keys, 256), BF16),
        V((images, 128), F32),
        V((images, 128), BF16),
        V((images, 128), F32),
        V((images, 128), F32),
        V((2 * rows, width), F32),
        V((rows, width), BF16),
        V((images, 128), BF16),
        V((seqs, rows, 128), BF16),
        V((seqs + 2, 8, 128), F32),
        V((rank + ch, 128), F32),
        V((8, 128), F32),
        V((rank + tail, 128), F32),
        V((reps, rank, 128), F32),
        V((seqs, tail, 128), F32),
        V((reps, tail, 128), F32),
        V((rank, 128), BF16),
        V((tail, 128), F32),
        V((dps * deep, width), BF16),
        V((dps * deep, ch), BF16),
    ]
    one = DMA((1,))
    ring = [DMA((3 * seqs,)), DMA((seqs,))]
    scratch += [DMA((6,))] + [one] * 4 + ring + [one] * 2 + [DMA((2,))] * 2
    scratch += [DMA((2,))] * 2 + [one, DMA((seqs // 4,))] + [DMA((2,))] * 2 + ring
    scratch += [DMA((6,))] * 2 + [DMA((8,))] * 2 + [DMA((16,))] * 2 + [one] * 8
    down_t, up, value = pl.pallas_call(
        functools.partial(main_kernel, seqs, dps),
        out_shape=[shape((ch, width), BF16), shape((rank, heads), BF16), shape((1, 1), F32)],
        in_specs=[
            pl.BlockSpec(memory_space=m)
            for m in [S, S, V, V, V, V, V, V, A, A, V, V, A, A, A, A]
        ],
        out_specs=[pl.BlockSpec(memory_space=V)] * 3,
        scratch_shapes=scratch,
        compiler_params=pltpu.CompilerParams(
            collective_id=0, has_side_effects=True, vmem_limit_bytes=VMEM_BYTES
        ),
    )(
        pair_timestep_index,
        preferred_image_slot,
        emb,
        latents[0, 0].T,
        noise[0].T,
        prompt_token_states[0],
        image_embed_weight,
        timestep_modulation_weight,
        image_query_key_value.reshape(width, -1),
        text_key_value.reshape(width, -1),
        query_norm_gain.reshape(1, -1),
        key_norm_gain.reshape(1, -1),
        adapter_down_weight.T,
        adapter_up_weight,
        image_output_weight,
        latent_out_weight.T,
    )
    return (down_t.T.astype(F32), up.astype(F32), value.reshape(1))


def solution(mesh):
    return jax.shard_map(
        on_device,
        mesh=mesh,
        in_specs=(
            P("dp", "pair", "seq", None),
            P("dp", "seq", None),
            P("dp"),
            P("dp"),
            P("dp", "seq", None),
            P(),
            P(None, "seq"),
            P(None, "seq", None),
            P(None, "seq", None),
            P(),
            P(),
            P(),
            P(),
            P("seq", None),
            P(),
        ),
        out_specs=(P(), P(), P("dp")),
        check_vma=False,
    )
```

```python
import functools
import math

import jax
import jax.numpy as jnp
from jax import lax
from jax.experimental import pallas as pl
from jax.experimental.pallas import tpu as pltpu
from jax.sharding import PartitionSpec as P

epsilon = 1e-06
half_beta = 20.0
horizon = 1000.0
F32 = jnp.float32
BF16 = jnp.bfloat16
VMEM_BYTES = 58 * 1024 * 1024


def sinusoid(step_value, width):
    half_width = width // 2
    freqs = jnp.exp(-math.log(10000.0) * jnp.arange(half_width, dtype=jnp.float32) / half_width)
    angle = step_value * freqs
    return jnp.concatenate([jnp.cos(angle), jnp.sin(angle)])


def mm(a, b):
    return lax.dot_general(a, b, (((1,), (0,)), ((), ())), preferred_element_type=F32)


def mm_nt(a, b):
    return lax.dot_general(a, b, (((1,), (1,)), ((), ())), preferred_element_type=F32)


def mm_tn(a, b):
    return lax.dot_general(a, b, (((0,), (0,)), ((), ())), preferred_element_type=F32)


def halves(a):
    top = a.astype(BF16)
    return top, (a - top.astype(F32)).astype(BF16)


def stacked(a):
    top, rest = halves(a)
    return jnp.concatenate([top, rest], 0)


def row_mean(a):
    return jnp.mean(a, -1, keepdims=True)


def rms_rows(rows):
    return lax.rsqrt(row_mean(rows * rows) + epsilon)


def remote(src, dst, send, recv, device):
    return pltpu.make_async_remote_copy(
        src_ref=src,
        dst_ref=dst,
        send_sem=send,
        recv_sem=recv,
        device_id=device,
        device_id_type=pl.DeviceIdType.MESH,
    )


def each(count, body):
    @pl.loop(0, count)
    def _(i):
        body(i)


def others(me, count, body):
    @pl.loop(1, count)
    def _(step):
        body(lax.rem(me + step, count))


def arrived(ref, sem, device):
    remote(ref, ref, sem, sem, device).wait_recv()


def gone(ref, sem, device):
    remote(ref, ref, sem, sem, device).wait_send()


def at_rows(start, size):
    return pl.ds(pl.multiple_of(start, 16), size)


def at_lanes(start, size):
    return pl.ds(pl.multiple_of(start, 128), size)


def with_shift(scaled, shift):
    width = shift.shape[1]
    top, rest = halves(shift)
    which = lax.broadcasted_iota(jnp.int32, (16, width), 0)
    extra = jnp.where(
        which == 0,
        top.astype(F32),
        jnp.where(which == 1, rest.astype(F32), 0.0),
    )
    return jnp.concatenate([scaled, extra], 0).astype(BF16)


def main_kernel(
    seqs, dps, step, pref, emb, lat_t, noi_t, txt, embed, wmod, wimg, wtxt, qg, kg, adown_t, aup, wo, lw_t,
    down, upb, value,
    wimg_v, wtxt_v, adown_v, up_v, lw_v, mod, moddp, noisy, text, oacc, q2, outb, modrow, x, wall, kk, vext, pol, lhs, outf, rl,
    mixed, gmix, gh, ghs, gapbuf, acc, csum, ua, ubuf, abuf, a2, usum, asum, left, right,
    in_s, mod_s, mod_r, noi_s, noi_r, txt_s, txt_r, dp_s, dp_r, kv_s, kv_r, x_s, x_r,
    g_s, g_r, e_s, e_r, wz_s, wz_r, wx_s, wx_r, wy_s, wy_r, wc_s, wc_r,
    u_s, u_r, a_s, a_r, v_s, v_r, b_s, b_r,
):
    me = lax.axis_index("seq")
    slot = lax.axis_index("pair")
    mine = lax.axis_index("dp")
    other = 1 - slot
    ch, rows = lat_t.shape
    images = rows * seqs
    width = embed.shape[1]
    span = width // 2
    strip = 128 // dps
    origins = dps // 2
    half = txt.shape[0] // 2
    texts = half * seqs
    block = 4 * rows
    blocks = images // block
    part = wmod.shape[1]
    zs = seqs // 2
    z_at, hi = lax.rem(me, zs), lax.div(me, zs)
    flip = lax.rem(me + zs, seqs)
    reps = 2 * dps
    rep = slot * dps + mine

    loads = [
        pltpu.make_async_copy(
            wo.at[at_rows(mine * strip, strip), at_lanes(slot * span, span)],
            wall.at[me, at_rows(mine * strip, strip), at_lanes(slot * span, span)],
            in_s.at[0],
        ),
        pltpu.make_async_copy(wimg, wimg_v, in_s.at[1]),
        pltpu.make_async_copy(wtxt, wtxt_v, in_s.at[2]),
        pltpu.make_async_copy(adown_t, adown_v, in_s.at[3]),
        pltpu.make_async_copy(aup.at[:, at_lanes(me * 128, 128)], up_v, in_s.at[4]),
        pltpu.make_async_copy(lw_t, lw_v, in_s.at[5]),
    ]
    for load in loads:
        load.start()
    barrier = pltpu.get_barrier_semaphore()

    def at(seq=me, pair=slot, dp=mine):
        return {"pair": pair, "seq": seq, "dp": dp}

    def greet(device):
        pl.semaphore_signal(
            barrier, inc=1, device_id=device, device_id_type=pl.DeviceIdType.MESH
        )

    others(me, seqs, lambda peer: greet(at(seq=peer)))
    others(mine, dps, lambda peer: greet(at(dp=peer)))
    each(dps, lambda peer: greet(at(pair=other, dp=peer)))
    greet(at(seq=flip, pair=other))
    total = (seqs - 1) + (dps - 1) + dps + 1

    mod_part = mm(jnp.broadcast_to(emb[...].astype(F32), (16, emb.shape[1])).astype(BF16), wmod[...])[0:1]
    modrow[...] = mod_part
    lev = (step[0].astype(F32) + 1.0) * (1.0 / horizon)
    lat_f = lat_t[...].astype(F32)
    noi_f = noi_t[...].astype(F32)
    own = ((1.0 - lev) * lat_f + lev * noi_f).T.astype(BF16)
    target = (noi_f - lat_f).T
    noisy[me] = jnp.concatenate([own[0 : rows // 2], own[rows // 2 :]], 1)
    t = txt[at_rows(slot * half, half), :].astype(F32)
    t = t - row_mean(t)
    text[at_rows(me * half, half), :] = (t * lax.rsqrt(row_mean(t * t) + epsilon)).astype(BF16)
    emb_c = embed[...].astype(F32)
    emb_c = emb_c - row_mean(emb_c)
    e_top, e_rest = halves(emb_c)
    gram = stacked(mm_nt(e_top, e_top) + mm_nt(e_top, e_rest) + mm_nt(e_rest, e_top))
    vext[:, 128:256] = jnp.ones((vext.shape[0], 128), BF16)
    acc[...] = jnp.zeros_like(acc)
    csum[...] = jnp.zeros_like(csum)
    loads[0].wait()
    pl.semaphore_wait(barrier, total)

    def mod_copy(owner, peer):
        return remote(
            modrow,
            mod.at[:, at_lanes(owner * part, part)],
            mod_s.at[0],
            mod_r.at[0],
            at(seq=peer),
        )

    def noisy_copy(owner, peer):
        where = noisy.at[owner]
        return remote(where, where, noi_s.at[0], noi_r.at[0], at(seq=peer))

    def dp_copy(owner, peer):
        return remote(
            mod.at[:, pl.ds(0, 2 * width)],
            moddp.at[owner],
            dp_s.at[0],
            dp_r.at[0],
            at(dp=peer),
        )

    def region(first, count, p, s):
        return wall.at[pl.ds(first, count), at_rows(p * strip, strip), at_lanes(s * span, span)]

    def owner_at(h, away):
        return h * zs + lax.rem(z_at + away + zs, zs)

    right_z, left_z = owner_at(hi, 1), owner_at(hi, -1)

    def ring_copy(kind, lane, owner, to):
        if kind == 0:
            where, send, recv = region(owner, 1, mine, slot), wz_s, wz_r
        else:
            where, send, recv = text.at[at_rows(owner * half, half)], txt_s, txt_r
        return remote(where, where, send.at[lane * seqs + owner], recv.at[owner], at(seq=to))

    def ring_sends(kind, hop):
        last = hop == zs // 2
        sends = []
        for h in range(2):
            if not last or h == 0:
                sends.append(ring_copy(kind, 1, owner_at(h, 1 - hop), right_z))
            if not last or h == 1:
                sends.append(ring_copy(kind, 2, owner_at(h, hop - 1), left_z))
        return sends

    def ring_flip(kind):
        ring_copy(kind, 0, me, flip).start()

    def ring_first(kind):
        if zs > 2:
            ring_copy(kind, 1, me, right_z).start()
            ring_copy(kind, 2, me, left_z).start()

    def ring_hop(kind, hop):
        if hop == 1:
            ring_copy(kind, 0, flip, flip).wait_recv()
            if zs > 2:
                ring_copy(kind, 1, flip, right_z).start()
                ring_copy(kind, 2, flip, left_z).start()
                return
        else:
            for h in range(2):
                ring_copy(kind, 0, owner_at(h, 1 - hop), flip).wait_recv()
                ring_copy(kind, 0, owner_at(h, hop - 1), flip).wait_recv()
        for copy in ring_sends(kind, hop):
            copy.start()

    def ring_end(kind):
        ring_copy(kind, 0, owner_at(0, zs // 2), flip).wait_recv()
        ring_copy(kind, 0, owner_at(1, zs // 2), flip).wait_recv()

    def ring_sent(kind):
        ring_copy(kind, 0, me, flip).wait_send()
        for hop in range(1, zs // 2 + 1):
            for copy in ring_sends(kind, hop):
                copy.wait_send()

    hops = zs // 2

    def along(away):
        return lax.rem(mine + 2 * away + dps, dps)

    places = [mine, along(-1), along(1), along(2)]
    sibling = mine + 1 - 2 * lax.rem(mine, 2)

    def chunk(origin, which_half, s):
        return region(which_half * (seqs // 2), seqs // 2, origin, s)

    def x_near(way, turn, origin):
        where = chunk(origin, turn if way == 0 else 1 - turn, slot)
        n = way * 2 + turn
        return remote(where, where, wx_s.at[n], wx_r.at[n], at(dp=along(1 - 2 * way)))

    def x_far(way, origin):
        where = chunk(origin, way, slot)
        return remote(where, where, wx_s.at[4 + way], wx_r.at[4 + way], at(dp=along(1 - 2 * way)))

    def x_other(way, origin):
        where = chunk(origin, way, other)
        return remote(where, where, wx_s.at[6 + way], wx_r.at[6 + way], at(dp=along(1 - 2 * way)))

    def y_copy(which, side, s):
        where = chunk(places[which], side, s)
        to = me if side == 0 else flip
        n = which * 2 + side
        return remote(where, where, wy_s.at[n], wy_r.at[n], at(pair=other, seq=to))

    def c_copy(foreign, which, side, at_sibling):
        origin = places[which]
        if at_sibling:
            origin = sibling - mine + origin
        where = chunk(origin, side, other if foreign else slot)
        n = (foreign * 4 + which) * 2 + side
        return remote(where, where, wc_s.at[n], wc_r.at[n], at(dp=sibling))

    def spread(which, side):
        y_copy(which, side, slot).start()
        c_copy(0, which, side, False).start()

    def relay(which, side):
        y_copy(which, side, other).wait_recv()
        c_copy(1, which, side, False).start()

    others(me, seqs, lambda peer: mod_copy(me, peer).start())
    ring_flip(0)
    ring_first(0)
    others(me, seqs, lambda peer: noisy_copy(me, peer).start())
    ring_flip(1)
    mod[:, at_lanes(me * part, part)] = mod_part
    ring_hop(0, 1)

    mod_others = mod.at[:, pl.ds(0, (seqs - 1) * part)]
    arrived(mod_others, mod_r.at[0], at(seq=flip))
    shift_img, scale_img, shift_txt, scale_txt, shift_out, scale_out = [
        mod[:, i * width : (i + 1) * width] for i in range(6)
    ]
    moddp[mine] = mod[:, 0 : 2 * width]
    others(mine, dps, lambda peer: dp_copy(mine, peer).start())

    loads[1].wait()
    loads[3].wait()
    loads[4].wait()
    img_lhs = with_shift(emb_c * (1.0 + scale_img), shift_img)
    img_m = mm(img_lhs, wimg_v[...])
    img_m2 = stacked(img_m[0:ch])
    img_shift = img_m[ch : ch + 1] + img_m[ch + 1 : ch + 2]
    low_m = mm_nt(img_lhs, adown_v[...])
    low_m2 = stacked(low_m[0:ch])
    low_shift = low_m[ch : ch + 1] + low_m[ch + 1 : ch + 2]
    up = up_v[...]
    gain_q = qg[...]
    gain_k = kg[...]
    score_scale = math.log2(math.e) / math.sqrt(128.0)
    if hops > 1:
        ring_hop(0, 2)
    ring_first(1)
    ring_hop(1, 1)

    noisy_others = noisy.at[pl.ds(0, seqs - 1)]
    arrived(noisy_others, noi_r.at[0], at(seq=flip))

    def project(i):
        here = at_rows(i * block, block)
        pieces = []
        for j in range(4):
            packed = noisy[i * 4 + j]
            pieces += [packed[:, 0:ch], packed[:, ch:]]
        nb = jnp.concatenate(pieces, 0)
        nf = nb.astype(F32)
        nb = jnp.concatenate([nb, nb], 1)
        var = jnp.sum(mm(nb, gram) * nf, -1, keepdims=True) * (1.0 / width)
        inv = lax.rsqrt(var + epsilon)
        qkv = mm(nb, img_m2) * inv + img_shift
        low = (mm(nb, low_m2) * inv + low_shift).astype(BF16)
        delta = mm(low, up).astype(BF16).astype(F32)
        q = qkv[:, 0:128]
        k = qkv[:, 128:256]
        q_pol = q + delta
        q2[here, :] = (q * rms_rows(q) * (gain_q * score_scale)).astype(BF16)
        q2[at_rows(images + i * block, block), :] = (
            q_pol * rms_rows(q_pol) * (gain_q * score_scale)
        ).astype(BF16)
        pol[here, :] = q_pol
        kk[here, :] = (k * rms_rows(k) * gain_k).astype(BF16)
        vext[here, 0:128] = qkv[:, 256:384].astype(BF16)
        lhs[here, :] = jnp.concatenate([low, (nf * inv).astype(BF16)], 1)

    def spans(start, stop, body):
        @pl.loop(start, stop)
        def _(i):
            body(i)

    spans(0, blocks // 2, project)
    if hops > 2:
        ring_hop(0, 3)
    spans(blocks // 2, blocks, project)
    if hops > 3:
        ring_hop(0, 4)

    def attend(here, keys):
        s = mm_nt(q2[here, :], kk[keys, :])
        return mm(jnp.exp2(s).astype(BF16), vext[keys, :])

    def image_keys(i):
        here = at_rows(i * block, block)
        oacc[here, :] = attend(here, pl.ds(0, images))

    cuts = [min(cut, 2 * blocks) for cut in (0, 1, 4)] + [2 * blocks]
    spans(cuts[0], cuts[1], image_keys)
    if hops > 1:
        ring_hop(1, 2)
    ring_end(0)
    if origins > 1:
        for turn in range(2):
            for way in range(2):
                x_near(way, turn, mine).start()
    spread(0, 0)
    spread(0, 1)
    spans(cuts[1], cuts[2], image_keys)
    if hops > 2:
        ring_hop(1, 3)
    spans(cuts[2], cuts[3], image_keys)
    if hops > 3:
        ring_hop(1, 4)
    if origins > 1:
        x_near(0, 0, places[1]).wait_recv()
        x_far(0, places[1]).start()
        spread(1, 0)
        x_near(1, 0, places[2]).wait_recv()
        x_far(1, places[2]).start()
        spread(2, 1)
    relay(0, 0)
    relay(0, 1)

    ring_end(1)
    loads[2].wait()
    text_n = (text[...].astype(F32) * (1.0 + scale_txt) + shift_txt).astype(BF16)
    kv = mm(text_n, wtxt_v[...])
    k = kv[:, 0:128]
    my_keys = at_rows(images + slot * texts, texts)
    kk[my_keys, :] = (k * rms_rows(k) * gain_k).astype(BF16)
    vext[my_keys, 0:128] = kv[:, 128:256].astype(BF16)

    def kv_copies(owner):
        keys = at_rows(images + owner * texts, texts)
        v = vext.at[keys, pl.ds(0, 128)]
        return (
            remote(kk.at[keys], kk.at[keys], kv_s.at[0], kv_r.at[0], at(pair=other)),
            remote(v, v, kv_s.at[1], kv_r.at[1], at(pair=other)),
        )

    for copy in kv_copies(slot):
        copy.start()

    def own_text(i):
        here = at_rows(i * block, block)
        oacc[here, :] += attend(here, my_keys)

    spans(0, blocks, own_text)
    if origins > 1:
        x_near(0, 1, places[1]).wait_recv()
        spread(1, 1)
        x_near(1, 1, places[2]).wait_recv()
        spread(2, 0)
    for copy in kv_copies(other):
        copy.wait_recv()

    def out_copy(kind, owner, peer):
        return remote(
            outb.at[at_rows(kind * images + peer * rows, rows)],
            x.at[at_rows(kind * rows, rows), at_lanes(owner * 128, 128)],
            x_s.at[kind],
            x_r.at[kind],
            at(seq=peer),
        )

    def text_keys(kind, i):
        b = lax.rem(i + lax.div(me, 4), blocks)
        here = at_rows(kind * images + b * block, block)
        left_keys = at_rows(images + other * texts, texts) if kind == 0 else pl.ds(images, 2 * texts)
        o = oacc[here, :] + attend(here, left_keys)
        inv = 1.0 / o[:, 128:256]
        out = o[:, 0:128] * inv
        outb[here, :] = out.astype(BF16)

        if kind == 1:
            outf[at_rows(b * block, block), :] = out
            rl[at_rows(b * block, block), :] = inv

        for j in range(4):
            peer = b * 4 + j

            @pl.when(peer != me)
            def _():
                out_copy(kind, me, peer).start()

            @pl.when(peer == me)
            def _():
                x[at_rows(kind * rows, rows), at_lanes(me * 128, 128)] = outb[
                    at_rows(kind * images + me * rows, rows), :
                ]

    for kind in range(2):
        spans(0, blocks, functools.partial(text_keys, kind))

    if origins > 1:
        relay(1, 0)
        x_other(0, places[1]).start()
        relay(2, 1)
        x_other(1, places[2]).start()
        for way in range(2):
            x_far(way, places[3]).wait_recv()
            c_copy(0, 3, way, False).start()
        relay(1, 1)
        relay(2, 0)

    moddp_others = moddp.at[pl.ds(0, dps - 1)]
    arrived(moddp_others, dp_r.at[0], at(dp=sibling))
    first = lax.broadcasted_iota(jnp.int32, (16, width), 0) == 0
    deep = ch + 16

    def build(p):
        shift = moddp[p, :, 0:width]
        scale = moddp[p, :, width:]
        extra = jnp.where(first, shift, 0.0)
        left[at_rows(p * deep, deep), :] = jnp.concatenate(
            [emb_c * (1.0 + scale), extra], 0
        ).astype(BF16)

    for p in range(dps):
        build(p)
    if origins > 1:
        for way in range(2):
            x_other(way, places[3]).wait_recv()
            c_copy(1, 3, way, False).start()

    out_others = [
        x.at[pl.ds(kind * rows, rows), pl.ds(0, 128 * (seqs - 1))] for kind in range(2)
    ]
    for kind in range(2):
        arrived(out_others[kind], x_r.at[kind], at(seq=flip))

    loads[5].wait()
    tile = 256 if span % 256 == 0 else 128
    xv = x[...]

    def mix(i, first_lane):
        here = at_lanes(first_lane + i * tile, tile)
        states = mm(own, embed[:, here])
        w = wall[:, :, here].reshape(128 * seqs, tile)
        mixed[:, here] = mm(xv, w) + jnp.concatenate([states, states], 0)

    for foreign in range(2):
        for which in range(origins):
            for side in range(2):
                c_copy(foreign, which, side, True).wait_recv()
        first_lane = (other if foreign else slot) * span
        each(span // tile, lambda i: mix(i, first_lane))
    full = mixed[...]
    full = full - row_mean(full)
    inv = lax.rsqrt(row_mean(full * full) + epsilon)
    unit = full * inv
    mixed[...] = unit
    pred = mm_nt((unit * (1.0 + scale_out) + shift_out).astype(BF16), lw_v[...])
    diff = jnp.concatenate([target, target], 0) - pred
    squares = diff * diff
    gap = (jnp.sum(squares[rows:]) - jnp.sum(squares[:rows])) * (1.0 / (images * ch))
    gapbuf[me] = jnp.full((8, 128), gap, F32)

    def gap_copy(owner, peer):
        return remote(
            gapbuf.at[owner], gapbuf.at[owner], e_s.at[0], e_r.at[0], at(seq=peer)
        )

    g_ln = mm(diff[rows:].astype(BF16), lw_v[...]) * (1.0 + scale_out)
    unit_p = mixed[rows:, :]
    gmix[...] = (
        (g_ln - row_mean(g_ln) - unit_p * row_mean(g_ln * unit_p)) * inv[rows:]
    ).astype(BF16)

    def g_copy(owner, peer):
        return remote(
            ghs.at[peer],
            gh.at[at_rows(owner * rows, rows)],
            g_s.at[0],
            g_r.at[lax.div(owner, 4)],
            at(seq=peer),
        )

    def heads_back(i):
        pair = lax.rem(i + lax.div(me, 2), seqs // 2)
        w = wall[pl.ds(2 * pair, 2)].reshape(256, width)
        g = mm_nt(gmix[...], w).astype(BF16)
        for j in range(2):
            peer = 2 * pair + j
            ghs[peer] = g[:, j * 128 : (j + 1) * 128]

            @pl.when(peer != me)
            def _():
                g_copy(me, peer).start()

            @pl.when(peer == me)
            def _():
                gh[at_rows(me * rows, rows), :] = ghs[me]

    each(seqs // 2, heads_back)

    others(me, seqs, lambda peer: gap_copy(me, peer).start())
    keys = kk[...]
    vals = vext[:, 0:128]

    def back(i):
        b = lax.rem(i + lax.div(me, 4), blocks)
        here = at_rows(b * block, block)

        @pl.when(i == 0)
        def _():
            arrived(gh.at[pl.ds(0, 3 * rows)], g_r.at[b], at(seq=flip))

        @pl.when(i != 0)
        def _():
            arrived(gh.at[pl.ds(0, 4 * rows)], g_r.at[b], at(seq=flip))

        g = gh[here, :]
        p = jnp.exp2(mm_nt(q2[at_rows(images + b * block, block), :], keys))
        gp = mm_nt(g, vals)
        dsum = jnp.sum(g.astype(F32) * outf[here, :], -1, keepdims=True)
        gs = (p * (gp - dsum)).astype(BF16)
        gq = mm(gs, keys) * (rl[here, :] * (1.0 / math.sqrt(128.0)))
        u = pol[here, :]
        r = rms_rows(u)
        w = gq * gain_q
        gd = (r * w - u * (r * r * r) * row_mean(u * w)).astype(BF16)
        acc[...] += mm_tn(lhs[here, :], gd)
        csum[...] += jnp.broadcast_to(
            jnp.sum(gd.astype(F32), 0, keepdims=True), csum.shape
        )

    gap_others = gapbuf.at[pl.ds(0, seqs - 1)]
    pair_copy = remote(
        gapbuf.at[seqs], gapbuf.at[seqs + 1], e_s.at[1], e_r.at[1], at(pair=other)
    )
    spans(0, blocks // 2, back)
    arrived(gap_others, e_r.at[0], at(seq=flip))
    own_gap = jnp.sum(gapbuf[0:seqs], 0)
    gapbuf[seqs] = own_gap
    pair_copy.start()
    spans(blocks // 2, blocks, back)
    pair_copy.wait_recv()
    other_gap = gapbuf[seqs + 1]
    sgn = (1.0 - 2.0 * pref[0].astype(F32)) * (1.0 - 2.0 * slot.astype(F32))
    z = half_beta * sgn * (own_gap - other_gap)
    value[...] = (jnp.maximum(z, 0.0) + jnp.log1p(jnp.exp(-jnp.abs(z))))[0:1, 0:1]
    weight = half_beta / dps / (1.0 + jnp.exp(-z))
    factor = (sgn * weight * (-2.0 / (images * ch)))[0:1, :]
    rank = up.shape[0]
    tail_rows = ua.shape[0] - rank
    ua[0:rank, :] = acc[0:rank, :] * factor
    a_top, a_rest = halves(jnp.concatenate([acc[rank : rank + ch, :], csum[...]], 0))
    tail = mm_nt(a_top, up) + mm_nt(a_rest, up)
    lower = jnp.concatenate([tail[0 : ch // 2], tail[ch // 2 : ch]], 1)
    lowest = jnp.concatenate([tail[ch:], tail[ch:]], 1)
    ua[rank:, :] = jnp.concatenate([lower, lowest], 0) * factor

    def to(r):
        return at(pair=lax.div(r, dps), dp=lax.rem(r, dps))

    def u_copy(owner, peer):
        return remote(
            ua.at[pl.ds(0, rank)], ubuf.at[owner], u_s.at[0], u_r.at[0], to(peer)
        )

    def a_copy(owner, peer):
        return remote(
            ua.at[pl.ds(rank, tail_rows)],
            abuf.at[owner],
            a_s.at[0],
            a_r.at[0],
            at(seq=peer),
        )

    def v_copy(owner, peer):
        return remote(
            usum,
            upb.at[:, at_lanes(owner * 128, 128)],
            v_s.at[0],
            v_r.at[0],
            at(seq=peer),
        )

    def b_copy(owner, peer):
        return remote(asum, a2.at[owner], b_s.at[0], b_r.at[0], to(peer))

    others(me, seqs, lambda peer: a_copy(me, peer).start())
    others(rep, reps, lambda peer: u_copy(rep, peer).start())
    ubuf[rep] = ua[0:rank, :]
    abuf[me] = ua[rank:, :]

    u_others, a_others = ubuf.at[pl.ds(0, reps - 1)], abuf.at[pl.ds(0, seqs - 1)]
    arrived(u_others, u_r.at[0], at(dp=sibling))
    sums = jnp.sum(ubuf[...], 0).astype(BF16)
    usum[...] = sums
    upb[:, at_lanes(me * 128, 128)] = sums
    others(me, seqs, lambda peer: v_copy(me, peer).start())
    arrived(a_others, a_r.at[0], at(seq=flip))
    sums = jnp.sum(abuf[...], 0)
    asum[...] = sums
    a2[rep] = sums
    others(rep, reps, lambda peer: b_copy(rep, peer).start())

    near = at(seq=flip)
    gone(mod_others, mod_s.at[0], near)
    gone(noisy_others, noi_s.at[0], near)
    gone(moddp_others, dp_s.at[0], near)
    for kind in range(2):
        gone(out_others[kind], x_s.at[kind], near)
    gone(gh.at[pl.ds(0, (seqs - 1) * rows)], g_s.at[0], near)
    gone(gap_others, e_s.at[0], near)
    pair_copy.wait_send()
    gone(a_others, a_s.at[0], near)
    for kind in range(2):
        ring_sent(kind)
    for copy in kv_copies(slot):
        copy.wait_send()
    if origins > 1:
        for way in range(2):
            for turn in range(2):
                x_near(way, turn, mine).wait_send()
            x_far(way, mine).wait_send()
            x_other(way, mine).wait_send()
    for which in range(origins):
        for side in range(2):
            if which < 3:
                y_copy(which, side, slot).wait_send()
            c_copy(0, which, side, False).wait_send()
            c_copy(1, which, side, False).wait_send()

    b_others = a2.at[pl.ds(0, reps - 1)]
    arrived(b_others, b_r.at[0], near)
    for p in range(dps):
        a = a2[p] + a2[dps + p]
        top = a[0 : ch // 2]
        low_rows = a[ch // 2 :, 0:ch]
        right[p * deep : (p + 1) * deep, :] = jnp.concatenate(
            [top[:, 0:ch], top[:, ch:], low_rows, low_rows], 0
        ).astype(BF16)
    down[...] = mm_tn(right[...], left[...]).astype(BF16)

    v_others = upb.at[:, pl.ds(0, 128 * (seqs - 1))]
    gone(v_others, v_s.at[0], near)
    arrived(v_others, v_r.at[0], near)
    gone(u_others, u_s.at[0], near)
    gone(b_others, b_s.at[0], near)


def shape(dims, kind):
    return jax.ShapeDtypeStruct(dims, kind)


def on_device(
    latents,
    noise,
    pair_timestep_index,
    preferred_image_slot,
    prompt_token_states,
    image_embed_weight,
    timestep_modulation_weight,
    image_query_key_value,
    text_key_value,
    query_norm_gain,
    key_norm_gain,
    adapter_down_weight,
    adapter_up_weight,
    image_output_weight,
    latent_out_weight,
):
    seqs = lax.axis_size("seq")
    dps = lax.axis_size("dp")
    rows, ch = latents.shape[2:]
    images = rows * seqs
    width = image_embed_weight.shape[1]
    texts = prompt_token_states.shape[1] * seqs
    keys = images + texts
    rank = adapter_down_weight.shape[1]
    step_value = pair_timestep_index[0].astype(jnp.float32)
    emb = sinusoid(step_value, timestep_modulation_weight.shape[0]).astype(BF16)[None]
    V, S, A = pltpu.VMEM, pltpu.SMEM, pl.ANY
    DMA = pltpu.SemaphoreType.DMA
    heads = 128 * seqs
    tail = ch // 2 + 8
    deep = ch + 16
    reps = 2 * dps
    scratch = [
        V((width, 384), BF16),
        V((width, 256), BF16),
        V((rank, width), BF16),
        V((rank, 128), BF16),
        V((ch, width), BF16),
        V((1, 6 * width), F32),
        V((dps, 1, 2 * width), F32),
        V((seqs, rows // 2, 128), BF16),
        V((texts // 2, width), BF16),
        V((2 * images, 256), F32),
        V((2 * images, 128), BF16),
        V((2 * images, 128), BF16),
        V((1, timestep_modulation_weight.shape[1]), F32),
        V((2 * rows, heads), BF16),
        V((seqs, 128, width), BF16),
        V((keys, 128), BF16),
        V((keys, 256), BF16),
        V((images, 128), F32),
        V((images, 128), BF16),
        V((images, 128), F32),
        V((images, 128), F32),
        V((2 * rows, width), F32),
        V((rows, width), BF16),
        V((images, 128), BF16),
        V((seqs, rows, 128), BF16),
        V((seqs + 2, 8, 128), F32),
        V((rank + ch, 128), F32),
        V((8, 128), F32),
        V((rank + tail, 128), F32),
        V((reps, rank, 128), F32),
        V((seqs, tail, 128), F32),
        V((reps, tail, 128), F32),
        V((rank, 128), BF16),
        V((tail, 128), F32),
        V((dps * deep, width), BF16),
        V((dps * deep, ch), BF16),
    ]
    one = DMA((1,))
    ring = [DMA((3 * seqs,)), DMA((seqs,))]
    scratch += [DMA((6,))] + [one] * 4 + ring + [one] * 2 + [DMA((2,))] * 2
    scratch += [DMA((2,))] * 2 + [one, DMA((seqs // 4,))] + [DMA((2,))] * 2 + ring
    scratch += [DMA((8,))] * 2 + [DMA((8,))] * 2 + [DMA((16,))] * 2 + [one] * 8
    down_t, up, value = pl.pallas_call(
        functools.partial(main_kernel, seqs, dps),
        out_shape=[shape((ch, width), BF16), shape((rank, heads), BF16), shape((1, 1), F32)],
        in_specs=[
            pl.BlockSpec(memory_space=m)
            for m in [S, S, V, V, V, V, V, V, A, A, V, V, A, A, A, A]
        ],
        out_specs=[pl.BlockSpec(memory_space=V)] * 3,
        scratch_shapes=scratch,
        compiler_params=pltpu.CompilerParams(
            collective_id=0, has_side_effects=True, vmem_limit_bytes=VMEM_BYTES
        ),
    )(
        pair_timestep_index,
        preferred_image_slot,
        emb,
        latents[0, 0].T,
        noise[0].T,
        prompt_token_states[0],
        image_embed_weight,
        timestep_modulation_weight,
        image_query_key_value.reshape(width, -1),
        text_key_value.reshape(width, -1),
        query_norm_gain.reshape(1, -1),
        key_norm_gain.reshape(1, -1),
        adapter_down_weight.T,
        adapter_up_weight,
        image_output_weight,
        latent_out_weight.T,
    )
    return (down_t.T.astype(F32), up.astype(F32), value.reshape(1))


def solution(mesh):
    return jax.shard_map(
        on_device,
        mesh=mesh,
        in_specs=(
            P("dp", "pair", "seq", None),
            P("dp", "seq", None),
            P("dp"),
            P("dp"),
            P("dp", "seq", None),
            P(),
            P(None, "seq"),
            P(None, "seq", None),
            P(None, "seq", None),
            P(),
            P(),
            P(),
            P(),
            P("seq", None),
            P(),
        ),
        out_specs=(P(), P(), P("dp")),
        check_vma=False,
    )
```

```python
import functools
import math

import jax
import jax.numpy as jnp
from jax import lax
from jax.experimental import pallas as pl
from jax.experimental.pallas import tpu as pltpu
from jax.sharding import PartitionSpec as P

epsilon = 1e-06
half_beta = 20.0
horizon = 1000.0
F32 = jnp.float32
BF16 = jnp.bfloat16
VMEM_BYTES = 58 * 1024 * 1024


def sinusoid(step_value, width):
    half_width = width // 2
    freqs = jnp.exp(-math.log(10000.0) * jnp.arange(half_width, dtype=jnp.float32) / half_width)
    angle = step_value * freqs
    return jnp.concatenate([jnp.cos(angle), jnp.sin(angle)])


def mm(a, b):
    return lax.dot_general(a, b, (((1,), (0,)), ((), ())), preferred_element_type=F32)


def mm_nt(a, b):
    return lax.dot_general(a, b, (((1,), (1,)), ((), ())), preferred_element_type=F32)


def mm_tn(a, b):
    return lax.dot_general(a, b, (((0,), (0,)), ((), ())), preferred_element_type=F32)


def halves(a):
    top = a.astype(BF16)
    return top, (a - top.astype(F32)).astype(BF16)


def stacked(a):
    top, rest = halves(a)
    return jnp.concatenate([top, rest], 0)


def row_mean(a):
    return jnp.mean(a, -1, keepdims=True)


def rms_rows(rows):
    return lax.rsqrt(row_mean(rows * rows) + epsilon)


def remote(src, dst, send, recv, device):
    return pltpu.make_async_remote_copy(
        src_ref=src,
        dst_ref=dst,
        send_sem=send,
        recv_sem=recv,
        device_id=device,
        device_id_type=pl.DeviceIdType.MESH,
    )


def each(count, body):
    @pl.loop(0, count)
    def _(i):
        body(i)


def others(me, count, body):
    @pl.loop(1, count)
    def _(step):
        body(lax.rem(me + step, count))


def arrived(ref, sem, device):
    remote(ref, ref, sem, sem, device).wait_recv()


def gone(ref, sem, device):
    remote(ref, ref, sem, sem, device).wait_send()


def at_rows(start, size):
    return pl.ds(pl.multiple_of(start, 16), size)


def at_lanes(start, size):
    return pl.ds(pl.multiple_of(start, 128), size)


def with_shift(scaled, shift):
    width = shift.shape[1]
    top, rest = halves(shift)
    which = lax.broadcasted_iota(jnp.int32, (16, width), 0)
    extra = jnp.where(
        which == 0,
        top.astype(F32),
        jnp.where(which == 1, rest.astype(F32), 0.0),
    )
    return jnp.concatenate([scaled, extra], 0).astype(BF16)


def main_kernel(
    seqs, dps, step, pref, emb, lat_t, noi_t, txt, embed, wmod, wimg, wtxt, qg, kg, adown_t, aup, wo, lw_t,
    down, upb, value,
    wimg_v, wtxt_v, adown_v, up_v, lw_v, mod, moddp, noisy, text, oacc, q2, outb, modrow, x, wall, kk, vext, pol, lhs, outf, rl,
    mixed, gmix, gh, ghs, gapbuf, acc, csum, ua, ubuf, abuf, a2, usum, asum, left, right,
    in_s, mod_s, mod_r, noi_s, noi_r, txt_s, txt_r, dp_s, dp_r, kv_s, kv_r, x_s, x_r,
    g_s, g_r, e_s, e_r, wz_s, wz_r, wx_s, wx_r, wy_s, wy_r, wc_s, wc_r,
    u_s, u_r, a_s, a_r, v_s, v_r, b_s, b_r,
):
    me = lax.axis_index("seq")
    slot = lax.axis_index("pair")
    mine = lax.axis_index("dp")
    other = 1 - slot
    ch, rows = lat_t.shape
    images = rows * seqs
    width = embed.shape[1]
    span = width // 2
    strip = 128 // dps
    origins = dps // 2
    half = txt.shape[0] // 2
    texts = half * seqs
    block = 4 * rows
    blocks = images // block
    part = wmod.shape[1]
    zs = seqs // 2
    z_at, hi = lax.rem(me, zs), lax.div(me, zs)
    flip = lax.rem(me + zs, seqs)
    reps = 2 * dps
    rep = slot * dps + mine

    loads = [
        pltpu.make_async_copy(
            wo.at[at_rows(mine * strip, strip), at_lanes(slot * span, span)],
            wall.at[me, at_rows(mine * strip, strip), at_lanes(slot * span, span)],
            in_s.at[0],
        ),
        pltpu.make_async_copy(wimg, wimg_v, in_s.at[1]),
        pltpu.make_async_copy(wtxt, wtxt_v, in_s.at[2]),
        pltpu.make_async_copy(adown_t, adown_v, in_s.at[3]),
        pltpu.make_async_copy(aup.at[:, at_lanes(me * 128, 128)], up_v, in_s.at[4]),
        pltpu.make_async_copy(lw_t, lw_v, in_s.at[5]),
    ]
    for load in loads:
        load.start()
    barrier = pltpu.get_barrier_semaphore()

    def at(seq=me, pair=slot, dp=mine):
        return {"pair": pair, "seq": seq, "dp": dp}

    def greet(device):
        pl.semaphore_signal(
            barrier, inc=1, device_id=device, device_id_type=pl.DeviceIdType.MESH
        )

    others(me, seqs, lambda peer: greet(at(seq=peer)))
    others(mine, dps, lambda peer: greet(at(dp=peer)))
    each(dps, lambda peer: greet(at(pair=other, dp=peer)))
    greet(at(seq=flip, pair=other))
    total = (seqs - 1) + (dps - 1) + dps + 1

    mod_part = mm(jnp.broadcast_to(emb[...].astype(F32), (16, emb.shape[1])).astype(BF16), wmod[...])[0:1]
    modrow[...] = mod_part
    lev = (step[0].astype(F32) + 1.0) * (1.0 / horizon)
    lat_f = lat_t[...].astype(F32)
    noi_f = noi_t[...].astype(F32)
    own = ((1.0 - lev) * lat_f + lev * noi_f).T.astype(BF16)
    target = (noi_f - lat_f).T
    noisy[me] = jnp.concatenate([own[0 : rows // 2], own[rows // 2 :]], 1)
    t = txt[at_rows(slot * half, half), :].astype(F32)
    t = t - row_mean(t)
    text[at_rows(me * half, half), :] = (t * lax.rsqrt(row_mean(t * t) + epsilon)).astype(BF16)
    emb_c = embed[...].astype(F32)
    emb_c = emb_c - row_mean(emb_c)
    e_top, e_rest = halves(emb_c)
    gram = stacked(mm_nt(e_top, e_top) + mm_nt(e_top, e_rest) + mm_nt(e_rest, e_top))
    vext[:, 128:256] = jnp.ones((vext.shape[0], 128), BF16)
    acc[...] = jnp.zeros_like(acc)
    csum[...] = jnp.zeros_like(csum)
    loads[0].wait()
    pl.semaphore_wait(barrier, total)

    def mod_copy(owner, peer):
        return remote(
            modrow,
            mod.at[:, at_lanes(owner * part, part)],
            mod_s.at[0],
            mod_r.at[0],
            at(seq=peer),
        )

    def noisy_copy(owner, peer):
        where = noisy.at[owner]
        return remote(where, where, noi_s.at[0], noi_r.at[0], at(seq=peer))

    def dp_copy(owner, peer):
        return remote(
            mod.at[:, pl.ds(0, 2 * width)],
            moddp.at[owner],
            dp_s.at[0],
            dp_r.at[0],
            at(dp=peer),
        )

    def region(first, count, p, s):
        return wall.at[pl.ds(first, count), at_rows(p * strip, strip), at_lanes(s * span, span)]

    def owner_at(h, away):
        return h * zs + lax.rem(z_at + away + zs, zs)

    right_z, left_z = owner_at(hi, 1), owner_at(hi, -1)

    def ring_copy(kind, lane, owner, to):
        if kind == 0:
            where, send, recv = region(owner, 1, mine, slot), wz_s, wz_r
        else:
            where, send, recv = text.at[at_rows(owner * half, half)], txt_s, txt_r
        return remote(where, where, send.at[lane * seqs + owner], recv.at[owner], at(seq=to))

    def ring_sends(kind, hop):
        last = hop == zs // 2
        sends = []
        for h in range(2):
            if not last or h == 0:
                sends.append(ring_copy(kind, 1, owner_at(h, 1 - hop), right_z))
            if not last or h == 1:
                sends.append(ring_copy(kind, 2, owner_at(h, hop - 1), left_z))
        return sends

    def ring_flip(kind):
        ring_copy(kind, 0, me, flip).start()

    def ring_first(kind):
        if zs > 2:
            ring_copy(kind, 1, me, right_z).start()
            ring_copy(kind, 2, me, left_z).start()

    def ring_hop(kind, hop):
        if hop == 1:
            ring_copy(kind, 0, flip, flip).wait_recv()
            if zs > 2:
                ring_copy(kind, 1, flip, right_z).start()
                ring_copy(kind, 2, flip, left_z).start()
                return
        else:
            for h in range(2):
                ring_copy(kind, 0, owner_at(h, 1 - hop), flip).wait_recv()
                ring_copy(kind, 0, owner_at(h, hop - 1), flip).wait_recv()
        for copy in ring_sends(kind, hop):
            copy.start()

    def ring_end(kind):
        ring_copy(kind, 0, owner_at(0, zs // 2), flip).wait_recv()
        ring_copy(kind, 0, owner_at(1, zs // 2), flip).wait_recv()

    def ring_sent(kind):
        ring_copy(kind, 0, me, flip).wait_send()
        for hop in range(1, zs // 2 + 1):
            for copy in ring_sends(kind, hop):
                copy.wait_send()

    hops = zs // 2

    def along(away):
        return lax.rem(mine + 2 * away + dps, dps)

    places = [mine, along(-1), along(1), along(2)]
    sibling = mine + 1 - 2 * lax.rem(mine, 2)

    def chunk(origin, which_half, s):
        return region(which_half * (seqs // 2), seqs // 2, origin, s)

    def x_near(way, turn, origin):
        where = chunk(origin, turn if way == 0 else 1 - turn, slot)
        n = way * 2 + turn
        return remote(where, where, wx_s.at[n], wx_r.at[n], at(dp=along(1 - 2 * way)))

    def x_far(way, origin):
        where = chunk(origin, way, slot)
        return remote(where, where, wx_s.at[4 + way], wx_r.at[4 + way], at(dp=along(1 - 2 * way)))

    def x_other(way, origin):
        where = chunk(origin, way, other)
        return remote(where, where, wx_s.at[6 + way], wx_r.at[6 + way], at(dp=along(1 - 2 * way)))

    def y_copy(which, side, s):
        where = chunk(places[which], side, s)
        to = me if side == 0 else flip
        n = which * 2 + side
        return remote(where, where, wy_s.at[n], wy_r.at[n], at(pair=other, seq=to))

    def c_copy(foreign, which, side, at_sibling):
        origin = places[which]
        if at_sibling:
            origin = sibling - mine + origin
        where = chunk(origin, side, other if foreign else slot)
        n = (foreign * 4 + which) * 2 + side
        return remote(where, where, wc_s.at[n], wc_r.at[n], at(dp=sibling))

    def spread(which, side):
        y_copy(which, side, slot).start()
        c_copy(0, which, side, False).start()

    def relay(which, side):
        y_copy(which, side, other).wait_recv()
        c_copy(1, which, side, False).start()

    others(me, seqs, lambda peer: mod_copy(me, peer).start())
    ring_flip(0)
    ring_first(0)
    others(me, seqs, lambda peer: noisy_copy(me, peer).start())
    ring_flip(1)
    ring_first(1)
    mod[:, at_lanes(me * part, part)] = mod_part
    ring_hop(0, 1)
    ring_hop(1, 1)

    mod_others = mod.at[:, pl.ds(0, (seqs - 1) * part)]
    arrived(mod_others, mod_r.at[0], at(seq=flip))
    shift_img, scale_img, shift_txt, scale_txt, shift_out, scale_out = [
        mod[:, i * width : (i + 1) * width] for i in range(6)
    ]
    moddp[mine] = mod[:, 0 : 2 * width]
    others(mine, dps, lambda peer: dp_copy(mine, peer).start())

    loads[1].wait()
    loads[3].wait()
    loads[4].wait()
    img_lhs = with_shift(emb_c * (1.0 + scale_img), shift_img)
    img_m = mm(img_lhs, wimg_v[...])
    img_m2 = stacked(img_m[0:ch])
    img_shift = img_m[ch : ch + 1] + img_m[ch + 1 : ch + 2]
    low_m = mm_nt(img_lhs, adown_v[...])
    low_m2 = stacked(low_m[0:ch])
    low_shift = low_m[ch : ch + 1] + low_m[ch + 1 : ch + 2]
    up = up_v[...]
    gain_q = qg[...]
    gain_k = kg[...]
    score_scale = math.log2(math.e) / math.sqrt(128.0)
    if hops > 1:
        ring_hop(0, 2)

    noisy_others = noisy.at[pl.ds(0, seqs - 1)]
    arrived(noisy_others, noi_r.at[0], at(seq=flip))

    def project(i):
        here = at_rows(i * block, block)
        pieces = []
        for j in range(4):
            packed = noisy[i * 4 + j]
            pieces += [packed[:, 0:ch], packed[:, ch:]]
        nb = jnp.concatenate(pieces, 0)
        nf = nb.astype(F32)
        nb = jnp.concatenate([nb, nb], 1)
        var = jnp.sum(mm(nb, gram) * nf, -1, keepdims=True) * (1.0 / width)
        inv = lax.rsqrt(var + epsilon)
        qkv = mm(nb, img_m2) * inv + img_shift
        low = (mm(nb, low_m2) * inv + low_shift).astype(BF16)
        delta = mm(low, up).astype(BF16).astype(F32)
        q = qkv[:, 0:128]
        k = qkv[:, 128:256]
        q_pol = q + delta
        q2[here, :] = (q * rms_rows(q) * (gain_q * score_scale)).astype(BF16)
        q2[at_rows(images + i * block, block), :] = (
            q_pol * rms_rows(q_pol) * (gain_q * score_scale)
        ).astype(BF16)
        pol[here, :] = q_pol
        kk[here, :] = (k * rms_rows(k) * gain_k).astype(BF16)
        vext[here, 0:128] = qkv[:, 256:384].astype(BF16)
        lhs[here, :] = jnp.concatenate([low, (nf * inv).astype(BF16)], 1)

    def spans(start, stop, body):
        @pl.loop(start, stop)
        def _(i):
            body(i)

    spans(0, blocks // 2, project)
    if hops > 2:
        ring_hop(0, 3)
    spans(blocks // 2, blocks, project)
    if hops > 3:
        ring_hop(0, 4)

    def attend(here, keys):
        s = mm_nt(q2[here, :], kk[keys, :])
        return mm(jnp.exp2(s).astype(BF16), vext[keys, :])

    def image_keys(i):
        here = at_rows(i * block, block)
        oacc[here, :] = attend(here, pl.ds(0, images))

    cuts = [min(cut, 2 * blocks) for cut in (0, 1, 4)] + [2 * blocks]
    spans(cuts[0], cuts[1], image_keys)
    if hops > 1:
        ring_hop(1, 2)
    ring_end(0)
    if origins > 1:
        for turn in range(2):
            for way in range(2):
                x_near(way, turn, mine).start()
    spread(0, 0)
    spread(0, 1)
    spans(cuts[1], cuts[2], image_keys)
    if hops > 2:
        ring_hop(1, 3)
    spans(cuts[2], cuts[3], image_keys)
    if hops > 3:
        ring_hop(1, 4)
    if origins > 1:
        x_near(0, 0, places[1]).wait_recv()
        x_far(0, places[1]).start()
        spread(1, 0)
        x_near(1, 0, places[2]).wait_recv()
        x_far(1, places[2]).start()
        spread(2, 1)
    relay(0, 0)
    relay(0, 1)

    ring_end(1)
    loads[2].wait()
    text_n = (text[...].astype(F32) * (1.0 + scale_txt) + shift_txt).astype(BF16)
    kv = mm(text_n, wtxt_v[...])
    k = kv[:, 0:128]
    my_keys = at_rows(images + slot * texts, texts)
    kk[my_keys, :] = (k * rms_rows(k) * gain_k).astype(BF16)
    vext[my_keys, 0:128] = kv[:, 128:256].astype(BF16)

    def kv_copies(owner):
        keys = at_rows(images + owner * texts, texts)
        v = vext.at[keys, pl.ds(0, 128)]
        return (
            remote(kk.at[keys], kk.at[keys], kv_s.at[0], kv_r.at[0], at(pair=other)),
            remote(v, v, kv_s.at[1], kv_r.at[1], at(pair=other)),
        )

    for copy in kv_copies(slot):
        copy.start()

    def own_text(i):
        here = at_rows(i * block, block)
        oacc[here, :] += attend(here, my_keys)

    spans(0, blocks, own_text)
    if origins > 1:
        x_near(0, 1, places[1]).wait_recv()
        spread(1, 1)
        x_near(1, 1, places[2]).wait_recv()
        spread(2, 0)
    for copy in kv_copies(other):
        copy.wait_recv()

    def out_copy(kind, owner, peer):
        return remote(
            outb.at[at_rows(kind * images + peer * rows, rows)],
            x.at[at_rows(kind * rows, rows), at_lanes(owner * 128, 128)],
            x_s.at[kind],
            x_r.at[kind],
            at(seq=peer),
        )

    def text_keys(kind, i):
        b = lax.rem(i + lax.div(me, 4), blocks)
        here = at_rows(kind * images + b * block, block)
        left_keys = at_rows(images + other * texts, texts) if kind == 0 else pl.ds(images, 2 * texts)
        o = oacc[here, :] + attend(here, left_keys)
        inv = 1.0 / o[:, 128:256]
        out = o[:, 0:128] * inv
        outb[here, :] = out.astype(BF16)

        if kind == 1:
            outf[at_rows(b * block, block), :] = out
            rl[at_rows(b * block, block), :] = inv

        for j in range(4):
            peer = b * 4 + j

            @pl.when(peer != me)
            def _():
                out_copy(kind, me, peer).start()

            @pl.when(peer == me)
            def _():
                x[at_rows(kind * rows, rows), at_lanes(me * 128, 128)] = outb[
                    at_rows(kind * images + me * rows, rows), :
                ]

    for kind in range(2):
        spans(0, blocks, functools.partial(text_keys, kind))

    if origins > 1:
        relay(1, 0)
        x_other(0, places[1]).start()
        relay(2, 1)
        x_other(1, places[2]).start()
        for way in range(2):
            x_far(way, places[3]).wait_recv()
            c_copy(0, 3, way, False).start()
        relay(1, 1)
        relay(2, 0)

    moddp_others = moddp.at[pl.ds(0, dps - 1)]
    arrived(moddp_others, dp_r.at[0], at(dp=sibling))
    first = lax.broadcasted_iota(jnp.int32, (16, width), 0) == 0
    deep = ch + 16

    def build(p):
        shift = moddp[p, :, 0:width]
        scale = moddp[p, :, width:]
        extra = jnp.where(first, shift, 0.0)
        left[at_rows(p * deep, deep), :] = jnp.concatenate(
            [emb_c * (1.0 + scale), extra], 0
        ).astype(BF16)

    for p in range(dps):
        build(p)
    if origins > 1:
        for way in range(2):
            x_other(way, places[3]).wait_recv()
            c_copy(1, 3, way, False).start()

    out_others = [
        x.at[pl.ds(kind * rows, rows), pl.ds(0, 128 * (seqs - 1))] for kind in range(2)
    ]
    for kind in range(2):
        arrived(out_others[kind], x_r.at[kind], at(seq=flip))

    loads[5].wait()
    tile = 256 if span % 256 == 0 else 128
    xv = x[...]

    def mix(i, first_lane):
        here = at_lanes(first_lane + i * tile, tile)
        states = mm(own, embed[:, here])
        w = wall[:, :, here].reshape(128 * seqs, tile)
        mixed[:, here] = mm(xv, w) + jnp.concatenate([states, states], 0)

    for foreign in range(2):
        for which in range(origins):
            for side in range(2):
                c_copy(foreign, which, side, True).wait_recv()
        first_lane = (other if foreign else slot) * span
        each(span // tile, lambda i: mix(i, first_lane))
    full = mixed[...]
    full = full - row_mean(full)
    inv = lax.rsqrt(row_mean(full * full) + epsilon)
    unit = full * inv
    mixed[...] = unit
    pred = mm_nt((unit * (1.0 + scale_out) + shift_out).astype(BF16), lw_v[...])
    diff = jnp.concatenate([target, target], 0) - pred
    squares = diff * diff
    gap = (jnp.sum(squares[rows:]) - jnp.sum(squares[:rows])) * (1.0 / (images * ch))
    gapbuf[me] = jnp.full((8, 128), gap, F32)

    def gap_copy(owner, peer):
        return remote(
            gapbuf.at[owner], gapbuf.at[owner], e_s.at[0], e_r.at[0], at(seq=peer)
        )

    g_ln = mm(diff[rows:].astype(BF16), lw_v[...]) * (1.0 + scale_out)
    unit_p = mixed[rows:, :]
    gmix[...] = (
        (g_ln - row_mean(g_ln) - unit_p * row_mean(g_ln * unit_p)) * inv[rows:]
    ).astype(BF16)

    def g_copy(owner, peer):
        return remote(
            ghs.at[peer],
            gh.at[at_rows(owner * rows, rows)],
            g_s.at[0],
            g_r.at[lax.div(owner, 4)],
            at(seq=peer),
        )

    def heads_back(i):
        pair = lax.rem(i + lax.div(me, 2), seqs // 2)
        w = wall[pl.ds(2 * pair, 2)].reshape(256, width)
        g = mm_nt(gmix[...], w).astype(BF16)
        for j in range(2):
            peer = 2 * pair + j
            ghs[peer] = g[:, j * 128 : (j + 1) * 128]

            @pl.when(peer != me)
            def _():
                g_copy(me, peer).start()

            @pl.when(peer == me)
            def _():
                gh[at_rows(me * rows, rows), :] = ghs[me]

    each(seqs // 2, heads_back)

    others(me, seqs, lambda peer: gap_copy(me, peer).start())
    keys = kk[...]
    vals = vext[:, 0:128]

    def back(i):
        b = lax.rem(i + lax.div(me, 4), blocks)
        here = at_rows(b * block, block)

        @pl.when(i == 0)
        def _():
            arrived(gh.at[pl.ds(0, 3 * rows)], g_r.at[b], at(seq=flip))

        @pl.when(i != 0)
        def _():
            arrived(gh.at[pl.ds(0, 4 * rows)], g_r.at[b], at(seq=flip))

        g = gh[here, :]
        p = jnp.exp2(mm_nt(q2[at_rows(images + b * block, block), :], keys))
        gp = mm_nt(g, vals)
        dsum = jnp.sum(g.astype(F32) * outf[here, :], -1, keepdims=True)
        gs = (p * (gp - dsum)).astype(BF16)
        gq = mm(gs, keys) * (rl[here, :] * (1.0 / math.sqrt(128.0)))
        u = pol[here, :]
        r = rms_rows(u)
        w = gq * gain_q
        gd = (r * w - u * (r * r * r) * row_mean(u * w)).astype(BF16)
        acc[...] += mm_tn(lhs[here, :], gd)
        csum[...] += jnp.broadcast_to(
            jnp.sum(gd.astype(F32), 0, keepdims=True), csum.shape
        )

    gap_others = gapbuf.at[pl.ds(0, seqs - 1)]
    pair_copy = remote(
        gapbuf.at[seqs], gapbuf.at[seqs + 1], e_s.at[1], e_r.at[1], at(pair=other)
    )
    spans(0, blocks // 2, back)
    arrived(gap_others, e_r.at[0], at(seq=flip))
    own_gap = jnp.sum(gapbuf[0:seqs], 0)
    gapbuf[seqs] = own_gap
    pair_copy.start()
    spans(blocks // 2, blocks, back)
    pair_copy.wait_recv()
    other_gap = gapbuf[seqs + 1]
    sgn = (1.0 - 2.0 * pref[0].astype(F32)) * (1.0 - 2.0 * slot.astype(F32))
    z = half_beta * sgn * (own_gap - other_gap)
    value[...] = (jnp.maximum(z, 0.0) + jnp.log1p(jnp.exp(-jnp.abs(z))))[0:1, 0:1]
    weight = half_beta / dps / (1.0 + jnp.exp(-z))
    factor = (sgn * weight * (-2.0 / (images * ch)))[0:1, :]
    rank = up.shape[0]
    tail_rows = ua.shape[0] - rank
    ua[0:rank, :] = acc[0:rank, :] * factor
    a_top, a_rest = halves(jnp.concatenate([acc[rank : rank + ch, :], csum[...]], 0))
    tail = mm_nt(a_top, up) + mm_nt(a_rest, up)
    lower = jnp.concatenate([tail[0 : ch // 2], tail[ch // 2 : ch]], 1)
    lowest = jnp.concatenate([tail[ch:], tail[ch:]], 1)
    ua[rank:, :] = jnp.concatenate([lower, lowest], 0) * factor

    def to(r):
        return at(pair=lax.div(r, dps), dp=lax.rem(r, dps))

    def u_copy(owner, peer):
        return remote(
            ua.at[pl.ds(0, rank)], ubuf.at[owner], u_s.at[0], u_r.at[0], to(peer)
        )

    def a_copy(owner, peer):
        return remote(
            ua.at[pl.ds(rank, tail_rows)],
            abuf.at[owner],
            a_s.at[0],
            a_r.at[0],
            at(seq=peer),
        )

    def v_copy(owner, peer):
        return remote(
            usum,
            upb.at[:, at_lanes(owner * 128, 128)],
            v_s.at[0],
            v_r.at[0],
            at(seq=peer),
        )

    def b_copy(owner, peer):
        return remote(asum, a2.at[owner], b_s.at[0], b_r.at[0], to(peer))

    others(me, seqs, lambda peer: a_copy(me, peer).start())
    others(rep, reps, lambda peer: u_copy(rep, peer).start())
    ubuf[rep] = ua[0:rank, :]
    abuf[me] = ua[rank:, :]

    u_others, a_others = ubuf.at[pl.ds(0, reps - 1)], abuf.at[pl.ds(0, seqs - 1)]
    arrived(u_others, u_r.at[0], at(dp=sibling))
    sums = jnp.sum(ubuf[...], 0).astype(BF16)
    usum[...] = sums
    upb[:, at_lanes(me * 128, 128)] = sums
    others(me, seqs, lambda peer: v_copy(me, peer).start())
    arrived(a_others, a_r.at[0], at(seq=flip))
    sums = jnp.sum(abuf[...], 0)
    asum[...] = sums
    a2[rep] = sums
    others(rep, reps, lambda peer: b_copy(rep, peer).start())

    near = at(seq=flip)
    gone(mod_others, mod_s.at[0], near)
    gone(noisy_others, noi_s.at[0], near)
    gone(moddp_others, dp_s.at[0], near)
    for kind in range(2):
        gone(out_others[kind], x_s.at[kind], near)
    gone(gh.at[pl.ds(0, (seqs - 1) * rows)], g_s.at[0], near)
    gone(gap_others, e_s.at[0], near)
    pair_copy.wait_send()
    gone(a_others, a_s.at[0], near)
    for kind in range(2):
        ring_sent(kind)
    for copy in kv_copies(slot):
        copy.wait_send()
    if origins > 1:
        for way in range(2):
            for turn in range(2):
                x_near(way, turn, mine).wait_send()
            x_far(way, mine).wait_send()
            x_other(way, mine).wait_send()
    for which in range(origins):
        for side in range(2):
            if which < 3:
                y_copy(which, side, slot).wait_send()
            c_copy(0, which, side, False).wait_send()
            c_copy(1, which, side, False).wait_send()

    b_others = a2.at[pl.ds(0, reps - 1)]
    arrived(b_others, b_r.at[0], near)
    for p in range(dps):
        a = a2[p] + a2[dps + p]
        top = a[0 : ch // 2]
        low_rows = a[ch // 2 :, 0:ch]
        right[p * deep : (p + 1) * deep, :] = jnp.concatenate(
            [top[:, 0:ch], top[:, ch:], low_rows, low_rows], 0
        ).astype(BF16)
    down[...] = mm_tn(right[...], left[...]).astype(BF16)

    v_others = upb.at[:, pl.ds(0, 128 * (seqs - 1))]
    gone(v_others, v_s.at[0], near)
    arrived(v_others, v_r.at[0], near)
    gone(u_others, u_s.at[0], near)
    gone(b_others, b_s.at[0], near)


def shape(dims, kind):
    return jax.ShapeDtypeStruct(dims, kind)


def on_device(
    latents,
    noise,
    pair_timestep_index,
    preferred_image_slot,
    prompt_token_states,
    image_embed_weight,
    timestep_modulation_weight,
    image_query_key_value,
    text_key_value,
    query_norm_gain,
    key_norm_gain,
    adapter_down_weight,
    adapter_up_weight,
    image_output_weight,
    latent_out_weight,
):
    seqs = lax.axis_size("seq")
    dps = lax.axis_size("dp")
    rows, ch = latents.shape[2:]
    images = rows * seqs
    width = image_embed_weight.shape[1]
    texts = prompt_token_states.shape[1] * seqs
    keys = images + texts
    rank = adapter_down_weight.shape[1]
    step_value = pair_timestep_index[0].astype(jnp.float32)
    emb = sinusoid(step_value, timestep_modulation_weight.shape[0]).astype(BF16)[None]
    V, S, A = pltpu.VMEM, pltpu.SMEM, pl.ANY
    DMA = pltpu.SemaphoreType.DMA
    heads = 128 * seqs
    tail = ch // 2 + 8
    deep = ch + 16
    reps = 2 * dps
    scratch = [
        V((width, 384), BF16),
        V((width, 256), BF16),
        V((rank, width), BF16),
        V((rank, 128), BF16),
        V((ch, width), BF16),
        V((1, 6 * width), F32),
        V((dps, 1, 2 * width), F32),
        V((seqs, rows // 2, 128), BF16),
        V((texts // 2, width), BF16),
        V((2 * images, 256), F32),
        V((2 * images, 128), BF16),
        V((2 * images, 128), BF16),
        V((1, timestep_modulation_weight.shape[1]), F32),
        V((2 * rows, heads), BF16),
        V((seqs, 128, width), BF16),
        V((keys, 128), BF16),
        V((keys, 256), BF16),
        V((images, 128), F32),
        V((images, 128), BF16),
        V((images, 128), F32),
        V((images, 128), F32),
        V((2 * rows, width), F32),
        V((rows, width), BF16),
        V((images, 128), BF16),
        V((seqs, rows, 128), BF16),
        V((seqs + 2, 8, 128), F32),
        V((rank + ch, 128), F32),
        V((8, 128), F32),
        V((rank + tail, 128), F32),
        V((reps, rank, 128), F32),
        V((seqs, tail, 128), F32),
        V((reps, tail, 128), F32),
        V((rank, 128), BF16),
        V((tail, 128), F32),
        V((dps * deep, width), BF16),
        V((dps * deep, ch), BF16),
    ]
    one = DMA((1,))
    ring = [DMA((3 * seqs,)), DMA((seqs,))]
    scratch += [DMA((6,))] + [one] * 4 + ring + [one] * 2 + [DMA((2,))] * 2
    scratch += [DMA((2,))] * 2 + [one, DMA((seqs // 4,))] + [DMA((2,))] * 2 + ring
    scratch += [DMA((8,))] * 2 + [DMA((8,))] * 2 + [DMA((16,))] * 2 + [one] * 8
    down_t, up, value = pl.pallas_call(
        functools.partial(main_kernel, seqs, dps),
        out_shape=[shape((ch, width), BF16), shape((rank, heads), BF16), shape((1, 1), F32)],
        in_specs=[
            pl.BlockSpec(memory_space=m)
            for m in [S, S, V, V, V, V, V, V, A, A, V, V, A, A, A, A]
        ],
        out_specs=[pl.BlockSpec(memory_space=V)] * 3,
        scratch_shapes=scratch,
        compiler_params=pltpu.CompilerParams(
            collective_id=0, has_side_effects=True, vmem_limit_bytes=VMEM_BYTES
        ),
    )(
        pair_timestep_index,
        preferred_image_slot,
        emb,
        latents[0, 0].T,
        noise[0].T,
        prompt_token_states[0],
        image_embed_weight,
        timestep_modulation_weight,
        image_query_key_value.reshape(width, -1),
        text_key_value.reshape(width, -1),
        query_norm_gain.reshape(1, -1),
        key_norm_gain.reshape(1, -1),
        adapter_down_weight.T,
        adapter_up_weight,
        image_output_weight,
        latent_out_weight.T,
    )
    return (down_t.T.astype(F32), up.astype(F32), value.reshape(1))


def solution(mesh):
    return jax.shard_map(
        on_device,
        mesh=mesh,
        in_specs=(
            P("dp", "pair", "seq", None),
            P("dp", "seq", None),
            P("dp"),
            P("dp"),
            P("dp", "seq", None),
            P(),
            P(None, "seq"),
            P(None, "seq", None),
            P(None, "seq", None),
            P(),
            P(),
            P(),
            P(),
            P("seq", None),
            P(),
        ),
        out_specs=(P(), P(), P("dp")),
        check_vma=False,
    )
```
